32 devices in a mesh: gx: 4 (over y, x), gy: 4 (over z), gz: 2 (over core).
Axes of the slice: x: 2, y: 2, z: 4, core: 2. Of those that a mesh axis runs over, the one named last changes fastest.
Arguments:
- positions: float32 [3, 1024], P(None, ('gx', 'gy', 'gz')), may hold values from 0 to 35.2, as said below
- species: int32 [1024], P(('gx', 'gy', 'gz')), may hold values from 0 to 63
- neighbours: int32 [32, 1024], P(None, ('gx', 'gy', 'gz')), may hold values from 0 to 863, as said below
- embed_center: float32 [64, 1024], replicated, may hold values from -3.5 to 3.5
- embed_neigh: float32 [64, 1024], replicated, may hold values from -3.5 to 3.5
- embed_radial: float32 [8, 1024], replicated, may hold values from -3.5 to 3.5
- value_proj: float32 [1024, 64], replicated, may hold values from -0.1875 to 0.1875
- env_weight: float32 [2, 1024, 64], replicated, may hold values from -0.1875 to 0.1875
- latent_weight: float32 [2, 1216, 1024], replicated, may hold values from -0.15625 to 0.15625
- path_weight: float32 [9, 64], replicated, may hold values from -4 to 4
- out_weight: float32 [1024], replicated, may hold values from -0.1875 to 0.1875
- scale_table: float32 [64], replicated, may hold values from 0.2 to 1
- shift_table: float32 [64], replicated, may hold values from -4 to 4
- cotangent: float32 [1024], P(('gx', 'gy', 'gz')), may hold values from -6 to 6
Outputs:
- atom_energy: float32 [1024], P(('gx', 'gy', 'gz'))
- position_grad: float32 [3, 1024], P(None, ('gx', 'gy', 'gz'))
- grad_embed_center: float32 [64, 1024], replicated
- grad_embed_neigh: float32 [64, 1024], replicated
- grad_embed_radial: float32 [8, 1024], replicated
- grad_value_proj: float32 [1024, 64], replicated
- grad_env_weight: float32 [2, 1024, 64], replicated
- grad_latent_weight: float32 [2, 1216, 1024], replicated
- grad_path_weight: float32 [9, 64], replicated
- grad_out_weight: float32 [1024], replicated
- grad_scale_table: float32 [64], replicated
- grad_shift_table: float32 [64], replicated
The draws below stay inside these ranges and needn't reach their ends.
Inputs may be any that keep to these rules, and one draw needn't show every extreme that they name: Column i = d * 32 + a lists atom i's neighbours as slots (bx * 9 + by * 3 + bz) * 32 + a' of a table of the atoms of the 27 devices at grid offsets (bx - 1, by - 1, bz - 1) around d; the real neighbours come first, lie on devices that exist, are distinct and are closer than 5 to atom i; the other slots hold 416 + a; at most 32 real neighbours per atom. `positions`: atoms of device d lie in its own box of the grid of devices, at distances 1.5 or more from each other.
All inputs are finite; a program needn't handle non-finite values.
Results may differ from the reference program's by a relative error of at most 0.0003.
Values sent between devices are 32-bit elements; how exact they have to be, the bound alone decides.
No kernel may reach another device: no remote copies, remote signals or barrier semaphores. Data moves between devices by JAX's collectives and lax.ppermute only.
A program may use at most 256 MiB of HBM per device.

```python
import math
import jax
import jax.numpy as jnp
import numpy as np
from jax import lax

LATENT = 1024
CHANNELS = 64
NSPEC = 64
NBESSEL = 8
PATHS = 9
NB = 32
LZ = 2
ATOM_DEV = 32
ATOMS = 1024
N_GX = 4
N_GY = 4
N_GZ = 2


SPACING = 2.2


OFFSETS = np.array([[i, j, k] for i in range(-2, 3) for j in range(-2, 3) for k in range(-2, 3) if 0 < i * i + j * j + k * k <= 4], dtype=np.int32)


def lattice():
    index = jnp.arange(ATOMS, dtype=jnp.int32)
    device = index // ATOM_DEV
    local_index = index % ATOM_DEV
    dev_x = device // (N_GY * N_GZ)
    dev_y = device // N_GZ % N_GY
    dev_z = device % N_GZ
    cell_x = local_index // (4 * LZ)
    cell_y = local_index // LZ % 4
    cell_z = local_index % LZ
    return (device, local_index, dev_x, dev_y, dev_z, cell_x, cell_y, cell_z)


def draw_positions(key, part):
    key = jax.random.fold_in(key, 11)
    device, local_index, dev_x, dev_y, dev_z, cell_x, cell_y, cell_z = lattice()
    coords = jnp.stack([dev_x * 4 + cell_x, dev_y * 4 + cell_y, dev_z * LZ + cell_z]).astype(jnp.float32)
    jitter = jnp.clip(jax.random.normal(key, (3, ATOMS), jnp.float32) * 0.08, -0.2, 0.2)
    return SPACING * (coords + 0.5) + jitter


def draw_neighbours(key, part):
    key = jax.random.fold_in(key, 23)
    subkeys = jax.random.split(key, 3)
    device, local_index, dev_x, dev_y, dev_z, cell_x, cell_y, cell_z = lattice()
    offsets = jnp.asarray(OFFSETS, jnp.int32)
    target_x = (dev_x * 4 + cell_x)[:, None] + offsets[None, :, 0]
    target_y = (dev_y * 4 + cell_y)[:, None] + offsets[None, :, 1]
    target_z = (dev_z * LZ + cell_z)[:, None] + offsets[None, :, 2]
    inside = (target_x >= 0) & (target_x < 4 * N_GX) & (target_y >= 0) & (target_y < 4 * N_GY) & (target_z >= 0) & (target_z < LZ * N_GZ)
    floor_dev = jax.random.randint(subkeys[0], (N_GX * N_GY * N_GZ,), NB // 4, NB + 1)
    wanted = jax.random.randint(subkeys[1], (ATOMS,), floor_dev[device], NB + 1)
    scores = jax.random.randint(subkeys[2], (ATOMS, NB), 0, 1 << 20) * 64 + jnp.arange(NB, dtype=jnp.int32)[None]
    scores = scores + jnp.where(inside, 0, 1 << 27)
    ranking = jnp.argsort(scores, axis=1)
    sorted_x = jnp.take_along_axis(target_x, ranking, 1)
    sorted_y = jnp.take_along_axis(target_y, ranking, 1)
    sorted_z = jnp.take_along_axis(target_z, ranking, 1)
    block_x = sorted_x // 4 - dev_x[:, None]
    block_y = sorted_y // 4 - dev_y[:, None]
    block_z = sorted_z // LZ - dev_z[:, None]
    inner = (sorted_x % 4 * 4 + sorted_y % 4) * LZ + sorted_z % LZ
    slot_value = (((block_x + 1) * 3 + block_y + 1) * 3 + block_z + 1) * ATOM_DEV + inner
    kept_count = jnp.minimum(wanted, jnp.sum(inside.astype(jnp.int32), 1))
    real_slot = jnp.arange(NB, dtype=jnp.int32)[None] < kept_count[:, None]
    own_slot = 13 * ATOM_DEV + local_index
    return jnp.where(real_slot, slot_value, own_slot[:, None]).T.astype(jnp.int32)


def with_ends(result, rng, least, largest):
    dims = result.shape
    place = [jax.random.randint(jax.random.fold_in(rng, axis), (), 0, dims[axis]) for axis in range(len(dims))]
    result = result.at[tuple(place)].set(least)
    longest = dims.index(max(dims))
    place[longest] = (place[longest] + 1) % dims[longest]
    return result.at[tuple(place)].set(largest)


def level_of(key, shape, shards, smallest, largest):
    gain, own = 1.0, jax.random.fold_in(key, 6)
    for axis_at, shards_of in shards:
        draws = jnp.exp(jax.random.uniform(jax.random.fold_in(own, axis_at), (shards_of,), jnp.float32, smallest / len(shards), largest / len(shards)))
        gain = gain * jnp.repeat(draws, shape[axis_at] // shards_of).reshape([-1 if axis == axis_at else 1 for axis in range(len(shape))])
    return gain


def rank_table(number_of, lean):
    loads = [(1 << 20) // math.isqrt(grade ** lean) + 1 for grade in range(1, number_of + 1)]
    deviation = 1 + sum(loads) // (1 << 30)
    return np.cumsum(np.array([max(1, weight // deviation) for weight in loads]))


def ranked_ids(stream_key, shape, number_of, slope):
    listing = rank_table(number_of, slope)
    pick = jax.random.randint(jax.random.fold_in(stream_key, 1), shape, 0, int(listing[number_of - 1]))
    standing = jnp.searchsorted(jnp.asarray(listing, jnp.int32), pick, side="right")
    return jax.random.permutation(jax.random.fold_in(stream_key, 2), number_of)[standing].astype(jnp.int32)


def noise(stream_key, dims, scale, bound, shards=(), kind=jnp.bfloat16):
    entries = jax.random.normal(stream_key, dims, jnp.float32) * scale
    if len(shards) > 0:
        entries = level_of(stream_key, dims, shards, -0.22, 0.18) * entries
    return jnp.clip(entries, min=-bound, max=bound).astype(kind)


def setup_inputs(seed: int = 0) -> dict:
    seeds = jax.random.split(jax.random.key(seed), 15)
    return {
        "positions": draw_positions(jax.random.fold_in(seeds[14], 71), 0),
        "species": with_ends(ranked_ids(seeds[1], (ATOMS,), NSPEC, 2), jax.random.fold_in(seeds[1], 3), 0, NSPEC - 1).astype(jnp.int32),
        "neighbours": draw_neighbours(jax.random.fold_in(seeds[14], 71), 0),
        "embed_center": noise(seeds[3], (NSPEC, LATENT), 3 ** -0.5, 3.5, (), jnp.float32),
        "embed_neigh": noise(seeds[4], (NSPEC, LATENT), 3 ** -0.5, 3.5, (), jnp.float32),
        "embed_radial": noise(seeds[5], (NBESSEL, LATENT), 3 ** -0.5, 3.5, (), jnp.float32),
        "value_proj": noise(seeds[6], (LATENT, CHANNELS), LATENT ** -0.5, 0.1875, (), jnp.float32),
        "env_weight": noise(seeds[7], (2, LATENT, CHANNELS), LATENT ** -0.5, 0.1875, (), jnp.float32),
        "latent_weight": noise(seeds[8], (2, LATENT + 3 * CHANNELS, LATENT), (LATENT + 3 * CHANNELS) ** -0.5, 0.15625, (), jnp.float32),
        "path_weight": noise(seeds[9], (PATHS, CHANNELS), 1.0, 4.0, (), jnp.float32),
        "out_weight": noise(seeds[10], (LATENT,), LATENT ** -0.5, 0.1875, (), jnp.float32),
        "scale_table": jnp.clip(jnp.exp(jax.random.uniform(seeds[11], (NSPEC,), jnp.float32, math.log(0.2), math.log(1.0))), 0.2, 1.0),
        "shift_table": noise(seeds[12], (NSPEC,), 1.0, 4.0, (), jnp.float32),
        "cotangent": noise(seeds[13], (ATOMS,), 1.0, 6.0, ((0, 32),), jnp.float32),
    }


CUTOFF = 5.0
ROOT_HALF = 0.7071067811865476
HALF_ROOT = 0.7071067811865476
SIXTH_ROOT = 0.4082482904638631
PRECISE = lax.Precision.HIGHEST
BASIS = np.array([[[HALF_ROOT, 0.0, 0.0], [0.0, -HALF_ROOT, 0.0], [0.0, 0.0, 0.0]], [[SIXTH_ROOT, 0.0, 0.0], [0.0, SIXTH_ROOT, 0.0], [0.0, 0.0, -2.0 * SIXTH_ROOT]], [[0.0, HALF_ROOT, 0.0], [HALF_ROOT, 0.0, 0.0], [0.0, 0.0, 0.0]], [[0.0, 0.0, HALF_ROOT], [0.0, 0.0, 0.0], [HALF_ROOT, 0.0, 0.0]], [[0.0, 0.0, 0.0], [0.0, 0.0, HALF_ROOT], [0.0, HALF_ROOT, 0.0]]])

def product(left_side, right_side):
    return jnp.dot(left_side, right_side, precision=PRECISE, preferred_element_type=jnp.float32)

def geometry(centre, neighbour, live_mask):
    padding = jnp.array([2.5, 0.0, 0.0], jnp.float32)[:, None]
    displacement = (neighbour - centre) * live_mask[None] + (1.0 - live_mask)[None] * padding
    distance = jnp.sqrt(lax.optimization_barrier(jnp.sum(displacement * displacement, axis=0)))
    scaled = distance / CUTOFF
    sixth_power = scaled ** 6
    smooth = live_mask * (1.0 - 28.0 * sixth_power + 48.0 * sixth_power * scaled - 21.0 * sixth_power * scaled * scaled)
    orders = (jnp.arange(NBESSEL) + 1).astype(jnp.float32)[:, None]
    radial = smooth[None] * math.sqrt(2.0 / CUTOFF) * jnp.sin(orders * (math.pi / CUTOFF) * distance[None]) / distance[None]
    direction = displacement / distance[None]
    harmonic_basis = jnp.asarray(BASIS, jnp.float32)
    second = math.sqrt(7.5) * jnp.einsum('mik,in,kn->mn', harmonic_basis, direction, direction, precision=PRECISE)
    harmonics = jnp.concatenate([jnp.ones_like(distance)[None], math.sqrt(3.0) * direction, second], 0)
    return (smooth, radial, harmonics)

def embedding(radial, smooth, centre_species, neighbour_species, embed_center, embed_neigh, embed_radial):
    species_ids = jnp.arange(NSPEC, dtype=jnp.int32)[None]
    centre_hot = (centre_species[:, None] == species_ids).astype(jnp.float32)
    neighbour_hot = (neighbour_species[:, None] == species_ids).astype(jnp.float32)
    before = product(centre_hot, embed_center) + product(neighbour_hot, embed_neigh) + product(radial.T, embed_radial)
    return jax.nn.silu(before) * smooth[:, None]

def environment(latent, harmonics, env_weight):
    weights = product(latent, env_weight).T
    edge_count = weights.shape[1]
    atom_count = edge_count // NB
    summed = lax.optimization_barrier(jnp.sum((harmonics[:, None, :] * weights[None]).reshape(9, CHANNELS, NB, atom_count), axis=2)) * NB ** (-0.5)
    return jnp.broadcast_to(summed[:, :, None, :], (9, CHANNELS, NB, atom_count)).reshape(9, CHANNELS, edge_count)

def invariants(features, surround):
    parts = jnp.concatenate([features[0:1] * surround[0:1], lax.optimization_barrier(jnp.sum(features[1:4] * surround[1:4], 0, keepdims=True)), lax.optimization_barrier(jnp.sum(features[4:9] * surround[4:9], 0, keepdims=True))], 0)
    return parts.reshape(3 * CHANNELS, -1).T

def update(latent, features, surround, smooth, latent_weight):
    joined = jnp.concatenate([latent, invariants(features, surround)], 1)
    return (latent + smooth[:, None] * jax.nn.silu(product(joined, latent_weight))) * ROOT_HALF

def couple(features, surround, path_weight):
    harmonic_basis = jnp.asarray(BASIS, jnp.float32)
    scalar_part, vector_part, tensor_part = (features[0], features[1:4], features[4:9])
    env_scalar, env_vector, env_tensor = (surround[0], surround[1:4], surround[4:9])
    path_gain = path_weight[:, :, None]
    crossed = jnp.stack([vector_part[1] * env_vector[2] - vector_part[2] * env_vector[1], vector_part[2] * env_vector[0] - vector_part[0] * env_vector[2], vector_part[0] * env_vector[1] - vector_part[1] * env_vector[0]])
    turned = jnp.einsum('mik,mcn,kcn->icn', harmonic_basis, tensor_part, env_vector, precision=PRECISE)
    paired = jnp.einsum('mik,icn,kcn->mcn', harmonic_basis, vector_part, env_vector, precision=PRECISE)
    new_scalar = path_gain[0] * scalar_part * env_scalar + path_gain[1] * lax.optimization_barrier(jnp.sum(vector_part * env_vector, 0))
    new_vector = path_gain[2] * scalar_part[None] * env_vector + path_gain[3] * vector_part * env_scalar[None] + path_gain[4] * crossed + path_gain[5] * turned
    new_tensor = path_gain[6] * paired + path_gain[7] * scalar_part[None] * env_tensor + path_gain[8] * tensor_part * env_scalar[None]
    return jnp.concatenate([new_scalar[None], new_vector, new_tensor], 0)

def readout(latent, smooth, species, out_weight, scale_table, shift_table):
    edge_energy = product(latent, out_weight[:, None])[:, 0] * smooth
    atom_count = species.shape[0]
    summed = lax.optimization_barrier(jnp.sum(edge_energy.reshape(NB, atom_count), 0))
    species_hot = (jnp.arange(NSPEC, dtype=jnp.int32)[:, None] == species[None]).astype(jnp.float32)
    return product(scale_table[None], species_hot)[0] * summed + product(shift_table[None], species_hot)[0]

def atom_energy(centre, neighbour, live_mask, species, neighbour_species, embed_center, embed_neigh, embed_radial, value_proj, env_weight, latent_weight, path_weight, out_weight, scale_table, shift_table):
    smooth, radial, harmonics = geometry(centre, neighbour, live_mask)
    latent = embedding(radial, smooth, jnp.tile(species, NB), neighbour_species, embed_center, embed_neigh, embed_radial)
    features = harmonics[:, None, :] * product(latent, value_proj).T[None]
    surround = environment(latent, harmonics, env_weight[0])
    next_features = couple(features, surround, path_weight)
    latent = update(latent, features, surround, smooth, latent_weight[0])
    surround = environment(latent, harmonics, env_weight[1])
    latent = update(latent, next_features, surround, smooth, latent_weight[1])
    return readout(latent, smooth, species, out_weight, scale_table, shift_table)

def reference(positions, species, neighbours, embed_center, embed_neigh, embed_radial, value_proj, env_weight, latent_weight, path_weight, out_weight, scale_table, shift_table, cotangent):
    devices = N_GX * N_GY * N_GZ

    def energies(positions, embed_center, embed_neigh, embed_radial, value_proj, env_weight, latent_weight, path_weight, out_weight, scale_table, shift_table):

        def device_energy(device):
            first_atom = (device * ATOM_DEV).astype(jnp.int32)
            centre = lax.dynamic_slice_in_dim(positions, first_atom, ATOM_DEV, 1)
            own_species = lax.dynamic_slice_in_dim(species, first_atom, ATOM_DEV, 0)
            slot_table = lax.dynamic_slice_in_dim(neighbours, first_atom, ATOM_DEV, 1)
            block_index = slot_table // ATOM_DEV
            along_x = jnp.clip(device // (N_GY * N_GZ) + block_index // 9 - 1, 0, N_GX - 1)
            along_y = jnp.clip(device // N_GZ % N_GY + block_index // 3 % 3 - 1, 0, N_GY - 1)
            along_z = jnp.clip(device % N_GZ + block_index % 3 - 1, 0, N_GZ - 1)
            owner_device = (along_x * N_GY + along_y) * N_GZ + along_z
            global_index = (owner_device * ATOM_DEV + slot_table % ATOM_DEV).reshape(-1).astype(jnp.int32)
            own_slot = 13 * ATOM_DEV + jnp.arange(ATOM_DEV, dtype=jnp.int32)
            live_mask = (slot_table != own_slot[None]).astype(jnp.float32).reshape(-1)
            return atom_energy(jnp.tile(centre, (1, NB)), positions[:, global_index], live_mask, own_species, species[global_index], embed_center, embed_neigh, embed_radial, value_proj, env_weight, latent_weight, path_weight, out_weight, scale_table, shift_table)
        return lax.map(jax.checkpoint(device_energy), jnp.arange(devices, dtype=jnp.int32)).reshape(-1)
    values, pullback = jax.vjp(energies, positions, embed_center, embed_neigh, embed_radial, value_proj, env_weight, latent_weight, path_weight, out_weight, scale_table, shift_table)
    gradients = pullback(cotangent)
    return (values, gradients[0], gradients[1], gradients[2], gradients[3], gradients[4], gradients[5], gradients[6], gradients[7], gradients[8], gradients[9], gradients[10])
```

```python
import functools
import math

import jax
import jax.numpy as jnp
import numpy as np
from jax import lax
from jax.experimental import pallas as pl
from jax.experimental.pallas import tpu as pltpu
from jax.sharding import PartitionSpec as P

LATENT = 1024
CHANNELS = 64
NSPEC = 64
NBESSEL = 8
NB = 32
ATOMS = 32
EDGES = NB * ATOMS
WIDE = LATENT + 3 * CHANNELS
HALF = LATENT // 2
QUARTER = LATENT // 4
NTAB = 27 * ATOMS
OWN = 13 * ATOMS

CUTOFF = 5.0
RH = 0.7071067811865476
HR = 0.7071067811865476
SR = 0.4082482904638631
R3 = math.sqrt(3.0)
Q75 = math.sqrt(7.5)
NORM = NB**-0.5
BESSEL = math.sqrt(2.0 / CUTOFF)

F32 = jnp.float32
BF16 = jnp.bfloat16

G_SMOOTH, G_LIVE, G_R, G_DISP, G_GRAD, G_RAD, G_GS, G_SPEC = 9, 10, 11, 12, 15, 16, 24, 25
G_ROWS = 32


def dot(a, b, ca, cb):
    return lax.dot_general(a, b, (((ca,), (cb,)), ((), ())), preferred_element_type=F32)


def dot3(ah, al, bh, bl, ca, cb):
    return dot(ah, bh, ca, cb) + dot(ah, bl, ca, cb) + dot(al, bh, ca, cb)


def split(x):
    hi = x.astype(BF16)
    return hi, (x - hi.astype(F32)).astype(BF16)


def pieces(x):
    hi = x.astype(BF16).astype(F32)
    rest = x - hi
    mid = rest.astype(BF16).astype(F32)
    return hi, mid, rest - mid


def sigmoid(x):
    return 0.5 * jnp.tanh(0.5 * x) + 0.5


def silu_both(x):
    sig = sigmoid(x)
    return x * sig, sig * (1.0 + x * (1.0 - sig))


def lanes(i, width):
    return pl.ds(pl.multiple_of(i * width, width), width)


def over(count, body):
    def step(i, carry):
        body(i)
        return carry

    lax.fori_loop(0, count, step, 0)


def iota(shape, dim):
    return lax.broadcasted_iota(jnp.int32, shape, dim)


def slot_total(x):
    x = x + pltpu.roll(x, 64, 1)
    return x + pltpu.roll(x, 32, 1)


def make_env(geo, w, env):
    for c in range(9):
        acc = None
        for k in range(8):
            cols = pl.ds(k * 128, 128)
            term = w[:, cols] if c == 0 else geo[c : c + 1, cols] * w[:, cols]
            acc = term if acc is None else acc + term
        env[c * 64 : (c + 1) * 64, :] = slot_total(acc) * NORM


def rows_of(ref, c, cols=slice(None)):
    return ref[c * 64 : (c + 1) * 64, cols]


def fwd_kernel(
    tab, slots, cent, w0h, w0l, ec, en, rad_w, ve, ev, path, scale,
    x0h, x0l, x1h, x1l, z0, pre, vw, w1, geo, g0, g1, f1,
    gat, table, veh, vel, evh, evl,
):
    hi, mid, lo = pieces(tab[...])
    tab24 = jnp.concatenate([hi, mid, lo], 0).astype(BF16)

    def gather(i):
        cols = lanes(i, 256)
        hot = jnp.where(iota((NTAB, 256), 0) == slots[:, cols], 1.0, 0.0).astype(BF16)
        got = dot(tab24, hot, 1, 0)
        gat[:, cols] = got[0:8] + got[8:16] + got[16:24]

    over(4, gather)

    live = jnp.where(slots[...] != OWN + iota((1, EDGES), 1) % ATOMS, 1.0, 0.0)
    dead = 1.0 - live
    dx = (gat[0:1, :] - cent[0:1, :]) * live + dead * 2.5
    dy = (gat[1:2, :] - cent[1:2, :]) * live
    dz = (gat[2:3, :] - cent[2:3, :]) * live
    r = jnp.sqrt(dx * dx + dy * dy + dz * dz)
    inv = 1.0 / r
    t = r / CUTOFF
    t2 = t * t
    t6 = t2 * t2 * t2
    smooth = live * (1.0 - 28.0 * t6 + 48.0 * t6 * t - 21.0 * t6 * t * t)
    ux, uy, uz = dx * inv, dy * inv, dz * inv
    geo[0:1, :] = jnp.ones_like(r)
    geo[1:2, :] = R3 * ux
    geo[2:3, :] = R3 * uy
    geo[3:4, :] = R3 * uz
    geo[4:5, :] = Q75 * HR * (ux * ux - uy * uy)
    geo[5:6, :] = Q75 * SR * (ux * ux + uy * uy - 2.0 * uz * uz)
    geo[6:7, :] = Q75 * 2.0 * HR * (ux * uy)
    geo[7:8, :] = Q75 * 2.0 * HR * (ux * uz)
    geo[8:9, :] = Q75 * 2.0 * HR * (uy * uz)
    geo[9:10, :] = smooth
    geo[10:11, :] = live
    geo[11:12, :] = r
    geo[12:13, :] = dx
    geo[13:14, :] = dy
    geo[14:15, :] = dz
    order = (iota((8, EDGES), 0) + 1).astype(F32) * (math.pi / CUTOFF)
    geo[16:24, :] = smooth * BESSEL * jnp.sin(order * r) * inv
    hot_c = jnp.where(iota((NSPEC, EDGES), 0).astype(F32) == cent[3:4, :], 1.0, 0.0)
    grad = cent[4:5, :] * jnp.sum(hot_c * scale[...], 0, keepdims=True)
    geo[15:16, :] = grad
    geo[24:25, :] = grad * smooth
    geo[25:26, :] = gat[3:4, :]
    geo[26:32, :] = jnp.zeros((6, EDGES), F32)

    ech, ecl = split(ec[...])
    enh, enl = split(en[...])
    rh = rad_w[...].astype(BF16).astype(F32)
    rl = rad_w[...] - rh
    table[0:64, :] = ech
    table[64:128, :] = enh
    table[128:192, :] = ecl
    table[192:256, :] = enl
    table[256:288, :] = jnp.concatenate([rh, rl, rh, jnp.zeros_like(rh)], 0).astype(BF16)
    veh[...], vel[...] = split(ve[...])
    evh[...], evl[...] = split(ev[...])

    def embed(i):
        cols = lanes(i, 256)
        kinds = iota((NSPEC, 256), 0).astype(F32)
        hot_c = jnp.where(kinds == cent[3:4, cols], 1.0, 0.0)
        hot_n = jnp.where(kinds == gat[3:4, cols], 1.0, 0.0)
        hots = jnp.concatenate([hot_c, hot_n], 0).astype(BF16)
        rad = geo[16:24, cols]
        rad_h = rad.astype(BF16).astype(F32)
        rads = jnp.concatenate([rad_h, rad_h, rad - rad_h, jnp.zeros_like(rad)], 0).astype(BF16)
        pre[:, cols] = dot(table[...], jnp.concatenate([hots, hots, rads], 0), 0, 0)
        sm = geo[9:10, cols]
        for b in range(8):
            rows = pl.ds(b * 128, 128)
            p = pre[rows, cols]
            x0h[rows, cols], x0l[rows, cols] = split(p * sigmoid(p) * sm)
        vw[:, cols] = dot3(
            veh[...], vel[...], x0h[0:LATENT, cols], x0l[0:LATENT, cols], 0, 0
        )

    over(4, embed)
    make_env(geo, vw.at[64:128, :], g0)

    def tensor(k):
        cols = lanes(k, 128)
        v = vw[0:64, cols]
        y = [geo[c : c + 1, cols] for c in range(9)]
        e0 = rows_of(g0, 0)
        e1, e2, e3 = rows_of(g0, 1), rows_of(g0, 2), rows_of(g0, 3)
        a, b, c = y[1] * e1, y[2] * e2, y[3] * e3
        vec = a + b + c
        quad = y[4] * rows_of(g0, 4)
        for m in range(5, 9):
            quad = quad + y[m] * rows_of(g0, m)
        x0h[1024:1088, cols], x0l[1024:1088, cols] = split(v * e0)
        x0h[1088:1152, cols], x0l[1088:1152, cols] = split(v * vec)
        x0h[1152:1216, cols], x0l[1152:1216, cols] = split(v * quad)
        p = [rows_of(path, n) for n in range(9)]
        e12, e13 = y[1] * e2, y[1] * e3
        e21, e23 = y[2] * e1, y[2] * e3
        e31, e32 = y[3] * e1, y[3] * e2
        q00 = HR * y[4] + SR * y[5]
        q11 = SR * y[5] - HR * y[4]
        q22 = -2.0 * SR * y[5]
        q01, q02, q12 = HR * y[6], HR * y[7], HR * y[8]
        f1[0:64, cols] = v * (p[0] * e0 + p[1] * vec)
        p3g = p[3] * e0
        f1[64:128, cols] = v * (
            p[2] * e1 + p3g * y[1] + p[4] * (e23 - e32) + p[5] * (q00 * e1 + q01 * e2 + q02 * e3)
        )
        f1[128:192, cols] = v * (
            p[2] * e2 + p3g * y[2] + p[4] * (e31 - e13) + p[5] * (q01 * e1 + q11 * e2 + q12 * e3)
        )
        f1[192:256, cols] = v * (
            p[2] * e3 + p3g * y[3] + p[4] * (e12 - e21) + p[5] * (q02 * e1 + q12 * e2 + q22 * e3)
        )
        p8g = p[8] * e0
        pair = (
            HR * (a - b),
            SR * (a + b - 2.0 * c),
            HR * (e12 + e21),
            HR * (e13 + e31),
            HR * (e23 + e32),
        )
        for m in range(5):
            f1[(4 + m) * 64 : (5 + m) * 64, cols] = v * (
                p[6] * pair[m] + p[7] * rows_of(g0, 4 + m) + p8g * y[4 + m]
            )

    over(8, tensor)

    def layer(i):
        cols = lanes(i, 256)
        z0[:, cols] = dot3(w0h[...], w0l[...], x0h[:, cols], x0l[:, cols], 0, 0)
        sm = geo[9:10, cols]
        for b in range(8):
            rows = pl.ds(b * 128, 128)
            z = z0[rows, cols]
            old = x0h[rows, cols].astype(F32) + x0l[rows, cols].astype(F32)
            x1h[rows, cols], x1l[rows, cols] = split((old + sm * (z * sigmoid(z))) * RH)
        w1[:, cols] = dot3(
            evh[...], evl[...], x1h[0:LATENT, cols], x1l[0:LATENT, cols], 0, 0
        )

    over(4, layer)
    make_env(geo, w1, g1)

    def scalars(k):
        cols = lanes(k, 128)
        s0 = rows_of(f1, 0, cols) * rows_of(g1, 0)
        s1 = rows_of(f1, 1, cols) * rows_of(g1, 1)
        for c in range(2, 4):
            s1 = s1 + rows_of(f1, c, cols) * rows_of(g1, c)
        s2 = rows_of(f1, 4, cols) * rows_of(g1, 4)
        for c in range(5, 9):
            s2 = s2 + rows_of(f1, c, cols) * rows_of(g1, c)
        x1h[1024:1088, cols], x1l[1024:1088, cols] = split(s0)
        x1h[1088:1152, cols], x1l[1088:1152, cols] = split(s1)
        x1h[1152:1216, cols], x1l[1152:1216, cols] = split(s2)

    over(8, scalars)


def weight_grad(core, xh, xl, qh, ql, keep, send):
    for out, block in ((send, 1 - core), (keep, core)):
        rows = pl.ds(pl.multiple_of(block * QUARTER, QUARTER), QUARTER)
        out[...] = dot3(xh[...], xl[...], qh[rows, :], ql[rows, :], 1, 1)


def late_kernel(half, core, x1h, x1l, wh, wl, outw, geo, qh, ql, keep, send, side, dout, acc):
    wcols = slice(half * HALF, (half + 1) * HALF)
    acc[...] = jnp.zeros_like(acc)
    side[...] = jnp.zeros_like(side)

    def step(i):
        cols = lanes(i, 256)
        z = dot3(wh[:, wcols], wl[:, wcols], x1h[:, cols], x1l[:, cols], 0, 0)
        sm = geo[9:10, cols]
        gs = geo[24:25, cols]
        scale = gs * sm * RH
        reach = jnp.zeros((8, 256), F32)
        total = jnp.zeros((8, 256), F32)
        for b in range(4):
            rows = pl.ds(b * 128, 128)
            frows = pl.ds(half * HALF + b * 128, 128)
            si, dsi = silu_both(z[b * 128 : (b + 1) * 128])
            ow = outw[frows, :]
            qh[rows, cols], ql[rows, cols] = split((ow * scale) * dsi)
            lat = (
                x1h[frows, cols].astype(F32) + x1l[frows, cols].astype(F32) + sm * si
            ) * RH
            part = gs * lat
            acc[rows, :] += part[:, 0:128] + part[:, 128:256]
            reach = reach + jnp.sum((ow * si).reshape(16, 8, 256), 0)
            total = total + jnp.sum((ow * lat).reshape(16, 8, 256), 0)
        side[0:1, cols] = jnp.sum(reach, 0, keepdims=True)
        side[1:2, cols] = jnp.sum(total, 0, keepdims=True)

    over(4, step)
    dout[...] = jnp.broadcast_to(jnp.sum(acc[...].T, 0, keepdims=True), dout.shape)
    weight_grad(core[0], x1h, x1l, qh, ql, keep, send)


def mid_kernel(qah, qal, qbh, qbl, wh, wl, f1, g1, w1, geo, ds1, dwh, dwl, dy, denv):
    def scal(i):
        cols = lanes(i, 256)
        ds1[:, cols] = dot3(
            wh[1024:1216, 0:512], wl[1024:1216, 0:512], qah[:, cols], qal[:, cols], 1, 0
        ) + dot3(
            wh[1024:1216, 512:1024], wl[1024:1216, 512:1024], qbh[:, cols], qbl[:, cols], 1, 0
        )

    over(4, scal)
    for c in range(9):
        kind = 0 if c == 0 else (1 if c < 4 else 2)
        acc = None
        for k in range(8):
            cols = pl.ds(k * 128, 128)
            term = rows_of(ds1, kind, cols) * rows_of(f1, c, cols)
            acc = term if acc is None else acc + term
        denv[c * 64 : (c + 1) * 64, :] = slot_total(acc) * NORM
    env_back(geo, w1, denv, dwh, dwl, dy, None)


def env_back(geo, w, denv, dwh, dwl, dy, more):
    def step(k):
        cols = lanes(k, 128)
        acc = rows_of(denv, 0)
        wk = w[:, cols]
        rows = [jnp.zeros((1, 128), F32)]
        for c in range(1, 9):
            d = rows_of(denv, c)
            acc = acc + geo[c : c + 1, cols] * d
            rows.append(jnp.sum(wk * d, 0, keepdims=True))
        dwh[:, cols], dwl[:, cols] = split(acc)
        for c in range(1, 9):
            if more is None:
                dy[c : c + 1, cols] = rows[c]
            else:
                dy[c : c + 1, cols] = rows[c] + more[c : c + 1, cols]

    over(8, step)


def early_kernel(
    half, core, qah, qal, qbh, qbl, wh, wl, ev, dwh, dwl, outw, geo, z0, x0h, x0l,
    dlat, qh, ql, keep, send, side,
    evh, evl,
):
    base = half * HALF
    evh[...], evl[...] = split(ev[base : base + HALF, :])
    side[...] = jnp.zeros_like(side)

    def step(i):
        cols = lanes(i, 256)
        wr = slice(base, base + HALF)
        d = (
            dot3(wh[wr, 0:512], wl[wr, 0:512], qah[:, cols], qal[:, cols], 1, 0)
            + dot3(wh[wr, 512:1024], wl[wr, 512:1024], qbh[:, cols], qbl[:, cols], 1, 0)
            + dot3(evh[...], evl[...], dwh[:, cols], dwl[:, cols], 1, 0)
        )
        sm = geo[9:10, cols] * RH
        gs = geo[24:25, cols] * RH
        total = jnp.zeros((8, 256), F32)
        for b in range(4):
            rows = pl.ds(b * 128, 128)
            frows = pl.ds(base + b * 128, 128)
            dl = d[b * 128 : (b + 1) * 128] + outw[frows, :] * gs
            dlat[rows, cols] = dl * RH
            si, dsi = silu_both(z0[frows, cols])
            qh[rows, cols], ql[rows, cols] = split(dl * dsi * sm)
            total = total + jnp.sum((dl * si).reshape(16, 8, 256), 0)
        side[0:1, cols] = jnp.sum(total, 0, keepdims=True) * RH

    over(4, step)
    weight_grad(core[0], x0h, x0l, qh, ql, keep, send)


def couple_kernel(
    qah, qal, qbh, qbl, wh, wl, vw, geo, g0, g1, ds1, path, x0h, x0l, x1h, x1l, dw1h, dw1l, dy1,
    dvwh, dvwl, dy, dpath, dve, dev,
    ds0, denv, dyv,
):
    def scal(i):
        cols = lanes(i, 256)
        ds0[:, cols] = dot3(
            wh[1024:1216, 0:512], wl[1024:1216, 0:512], qah[:, cols], qal[:, cols], 1, 0
        ) + dot3(
            wh[1024:1216, 512:1024], wl[1024:1216, 512:1024], qbh[:, cols], qbl[:, cols], 1, 0
        )

    over(4, scal)
    denv[...] = jnp.zeros_like(denv)
    dpath[...] = jnp.zeros_like(dpath)

    def step(k):
        cols = lanes(k, 128)
        v = vw[0:64, cols]
        y = [geo[c : c + 1, cols] for c in range(9)]
        e = [rows_of(g0, c) for c in range(9)]
        p = [rows_of(path, n) for n in range(9)]
        s = [rows_of(ds0, n, cols) for n in range(3)]
        u = [rows_of(ds1, n, cols) for n in range(3)]
        f0 = u[0] * rows_of(g1, 0)
        fv = [u[1] * rows_of(g1, c) for c in range(1, 4)]
        fq = [u[2] * rows_of(g1, c) for c in range(4, 9)]
        yv, yq, ev_, eq = y[1:4], y[4:9], e[1:4], e[4:9]

        def dot_of(a, b):
            out = a[0] * b[0]
            for i in range(1, len(a)):
                out = out + a[i] * b[i]
            return out

        m00 = HR * yq[0] + SR * yq[1]
        m11 = SR * yq[1] - HR * yq[0]
        m22 = -2.0 * SR * yq[1]
        m01, m02, m12 = HR * yq[2], HR * yq[3], HR * yq[4]
        t00 = HR * fq[0] + SR * fq[1]
        t11 = SR * fq[1] - HR * fq[0]
        t22 = (-2.0 * SR) * fq[1]
        t01, t02, t12 = HR * fq[2], HR * fq[3], HR * fq[4]

        te = [
            t00 * ev_[0] + t01 * ev_[1] + t02 * ev_[2],
            t01 * ev_[0] + t11 * ev_[1] + t12 * ev_[2],
            t02 * ev_[0] + t12 * ev_[1] + t22 * ev_[2],
        ]
        ty = [
            t00 * yv[0] + t01 * yv[1] + t02 * yv[2],
            t01 * yv[0] + t11 * yv[1] + t12 * yv[2],
            t02 * yv[0] + t12 * yv[1] + t22 * yv[2],
        ]
        mf = [
            m00 * fv[0] + m01 * fv[1] + m02 * fv[2],
            m01 * fv[0] + m11 * fv[1] + m12 * fv[2],
            m02 * fv[0] + m12 * fv[1] + m22 * fv[2],
        ]
        ef = [
            ev_[1] * fv[2] - ev_[2] * fv[1],
            ev_[2] * fv[0] - ev_[0] * fv[2],
            ev_[0] * fv[1] - ev_[1] * fv[0],
        ]
        fy = [
            fv[1] * yv[2] - fv[2] * yv[1],
            fv[2] * yv[0] - fv[0] * yv[2],
            fv[0] * yv[1] - fv[1] * yv[0],
        ]
        e_fv = dot_of(ev_, fv)
        y_fv = dot_of(yv, fv)
        e_fq = dot_of(eq, fq)
        y_fq = dot_of(yq, fq)
        vec = dot_of(yv, ev_)
        y_te = dot_of(yv, te)
        e_mf = dot_of(ev_, mf)
        y_ef = dot_of(yv, ef)

        grads = (
            e[0] * f0,
            vec * f0,
            e_fv,
            e[0] * y_fv,
            y_ef,
            e_mf,
            y_te,
            e_fq,
            e[0] * y_fq,
        )
        for n in range(9):
            dpath[n * 64 : (n + 1) * 64, :] += v * grads[n]

        p1f = p[1] * f0
        d0 = s[0] * e[0] + p[0] * e[0] * f0 + p[2] * e_fv + p[7] * e_fq
        p3e = p[3] * e[0]
        p8e = p[8] * e[0]
        s1f = s[1] + p1f
        dv = d0
        for i in range(3):
            di = s1f * ev_[i] + p3e * fv[i] + p[4] * ef[i] + p[6] * te[i]
            dv = dv + yv[i] * di
            dyv[1 + i : 2 + i, cols] = jnp.sum(v * di, 0, keepdims=True)
        a, b, c = fv[0] * ev_[0], fv[1] * ev_[1], fv[2] * ev_[2]
        bil = (
            HR * (a - b),
            SR * (a + b - 2.0 * c),
            HR * (fv[0] * ev_[1] + fv[1] * ev_[0]),
            HR * (fv[0] * ev_[2] + fv[2] * ev_[0]),
            HR * (fv[1] * ev_[2] + fv[2] * ev_[1]),
        )
        for m in range(5):
            dm = s[2] * eq[m] + p[5] * bil[m] + p8e * fq[m]
            dv = dv + yq[m] * dm
            dyv[4 + m : 5 + m, cols] = jnp.sum(v * dm, 0, keepdims=True)
        dvwh[0:64, cols], dvwl[0:64, cols] = split(dv)

        denv[0:64, :] += v * (s[0] + p[0] * f0 + p[3] * y_fv + p[8] * y_fq)
        for i in range(3):
            denv[(1 + i) * 64 : (2 + i) * 64, :] += v * (
                s1f * yv[i] + p[2] * fv[i] + p[4] * fy[i] + p[5] * mf[i] + p[6] * ty[i]
            )
        for m in range(5):
            denv[(4 + m) * 64 : (5 + m) * 64, :] += v * (s[2] * yq[m] + p[7] * fq[m])

    over(8, step)
    for c in range(9):
        denv[c * 64 : (c + 1) * 64, :] = slot_total(rows_of(denv, c)) * NORM
    dyv[0:1, :] = jnp.zeros((1, EDGES), F32)
    dyv[...] += dy1[...]
    env_back(geo, vw.at[64:128, :], denv, dvwh.at[64:128, :], dvwl.at[64:128, :], dy, dyv)
    dve[...] = dot3(dvwh[...], dvwl[...], x0h[0:LATENT, :], x0l[0:LATENT, :], 1, 1)
    dev[...] = dot3(dw1h[...], dw1l[...], x1h[0:LATENT, :], x1l[0:LATENT, :], 1, 1)


def last_kernel(
    qah, qal, qbh, qbl, wh, wl, ve, dvwh, dvwl, dla, dlb, pre, geo, slots, cent, rad_w,
    sla, slb, sea, seb, dy, dpath, scale, shift,
    hots_grad, rad_grad, ghost, own, energy, misc,
    veh, vel, qph, qpl, dsm, drad,
):
    veh[...], vel[...] = split(ve[...])
    rwh, rwl = split(jnp.concatenate([rad_w[...], jnp.zeros_like(rad_w)], 0))

    def step(i):
        cols = lanes(i, 256)
        sm = geo[9:10, cols]
        total = jnp.zeros((8, 256), F32)
        for h, dl in ((0, dla), (1, dlb)):
            wr = slice(h * HALF, (h + 1) * HALF)
            d = (
                dot3(wh[wr, 0:512], wl[wr, 0:512], qah[:, cols], qal[:, cols], 1, 0)
                + dot3(wh[wr, 512:1024], wl[wr, 512:1024], qbh[:, cols], qbl[:, cols], 1, 0)
                + dot3(veh[wr, :], vel[wr, :], dvwh[:, cols], dvwl[:, cols], 1, 0)
            )
            for b in range(4):
                rows = pl.ds(b * 128, 128)
                frows = pl.ds(h * HALF + b * 128, 128)
                dd = d[b * 128 : (b + 1) * 128] + dl[rows, cols]
                si, dsi = silu_both(pre[frows, cols])
                qph[frows, cols], qpl[frows, cols] = split(dd * dsi * sm)
                total = total + jnp.sum((dd * si).reshape(16, 8, 256), 0)
        dsm[:, cols] = jnp.sum(total, 0, keepdims=True)
        drad[:, cols] = dot3(rwh, rwl, qph[:, cols], qpl[:, cols], 1, 0)[0:8]

    over(4, step)

    kinds = iota((NSPEC, EDGES), 0).astype(F32)
    hot_c = jnp.where(kinds == cent[3:4, :], 1.0, 0.0)
    hot_n = jnp.where(kinds == geo[25:26, :], 1.0, 0.0)
    hots = jnp.concatenate([hot_c, hot_n], 0).astype(BF16)
    rad = geo[16:24, :]
    rad_h = rad.astype(BF16).astype(F32)
    rads = jnp.concatenate([rad_h, rad - rad_h], 0).astype(BF16)
    left = jnp.concatenate([hots, rads], 0)
    full = dot(left, qph[...], 1, 1)
    rest = dot(left, qpl[...], 1, 1)
    hots_grad[...] = full[0:128] + rest[0:128]
    rad_grad[...] = full[128:136] + full[136:144] + rest[128:136]

    live, r, smooth = geo[10:11, :], geo[11:12, :], geo[9:10, :]
    inv = 1.0 / r
    grad = geo[15:16, :]
    reach = sla[0:1, :] + slb[0:1, :]
    lat_out = sla[1:2, :] + slb[1:2, :]
    order = (iota((8, EDGES), 0) + 1).astype(F32) * (math.pi / CUTOFF)
    angle = order * r
    sine = jnp.sin(angle) * inv
    cosine = jnp.cos(angle) * inv
    dr8 = drad[...]
    d_s = (
        grad * lat_out
        + grad * smooth * RH * reach
        + sea[0:1, :]
        + seb[0:1, :]
        + dsm[...]
        + BESSEL * jnp.sum(dr8 * sine, 0, keepdims=True)
    )
    t = r / CUTOFF
    t2 = t * t
    gap = 1.0 - t
    d_r = d_s * (live * (-168.0 / CUTOFF) * (t2 * t2 * t) * (gap * gap)) + (
        smooth * BESSEL
    ) * jnp.sum(dr8 * (order * cosine - sine * inv), 0, keepdims=True)
    ux, uy, uz = geo[12:13, :] * inv, geo[13:14, :] * inv, geo[14:15, :] * inv
    yy = [dy[c : c + 1, :] for c in range(9)]
    h2, s2 = 2.0 * HR * Q75, 2.0 * SR * Q75
    gx = R3 * yy[1] + ux * (h2 * yy[4] + s2 * yy[5]) + h2 * (uy * yy[6] + uz * yy[7])
    gy = R3 * yy[2] + uy * (s2 * yy[5] - h2 * yy[4]) + h2 * (ux * yy[6] + uz * yy[8])
    gz = R3 * yy[3] - 2.0 * s2 * uz * yy[5] + h2 * (ux * yy[7] + uy * yy[8])
    along = ux * gx + uy * gy + uz * gz
    zero = jnp.zeros((5, EDGES), F32)
    disp = jnp.concatenate(
        [
            live * ((gx - ux * along) * inv + ux * d_r),
            live * ((gy - uy * along) * inv + uy * d_r),
            live * ((gz - uz * along) * inv + uz * d_r),
            zero,
        ],
        0,
    )
    hi, mid, lo = pieces(disp)
    disp24 = jnp.concatenate([hi, mid, lo], 0).astype(BF16)
    acc = None
    mine = None
    for k in range(8):
        term = disp[:, k * 128 : (k + 1) * 128]
        mine = term if mine is None else mine + term
    own[...] = slot_total(mine)
    for i in range(4):
        cols = pl.ds(i * 256, 256)
        hot = jnp.where(iota((NTAB, 256), 0) == slots[:, cols], 1.0, 0.0).astype(BF16)
        term = dot(disp24[:, i * 256 : (i + 1) * 256], hot, 1, 1)
        acc = term if acc is None else acc + term
    ghost[...] = acc[0:8] + acc[8:16] + acc[16:24]

    edge_energy = smooth * lat_out
    total = None
    for k in range(8):
        term = edge_energy[:, k * 128 : (k + 1) * 128]
        total = term if total is None else total + term
    total = slot_total(jnp.broadcast_to(total, (8, 128)))[0:1]
    hot = jnp.where(iota((NSPEC, 128), 0).astype(F32) == cent[3:4, 0:128], 1.0, 0.0)
    energy[...] = jnp.broadcast_to(
        jnp.sum(hot * scale[...], 0, keepdims=True) * total
        + jnp.sum(hot * shift[...], 0, keepdims=True),
        energy.shape,
    )
    cot = cent[4:5, 0:128] * jnp.where(iota((1, 128), 1) < ATOMS, 1.0, 0.0)
    stack = jnp.concatenate(
        [dpath[...], hot * (cot * total), hot * cot, jnp.zeros((64, 128), F32)], 0
    )
    row = jnp.sum(stack.T, 0, keepdims=True)
    misc[...] = jnp.broadcast_to(
        jnp.concatenate([row, jnp.zeros((1, 256), F32)], 1), misc.shape
    )


VSPEC = pl.BlockSpec(memory_space=pltpu.VMEM)
SSPEC = pl.BlockSpec(memory_space=pltpu.SMEM)


def call(body, outs, args, scratch=(), scalar=False, flops=0, limit=24):
    specs = [VSPEC] * len(args)
    if scalar:
        specs[0] = SSPEC
    return pl.pallas_call(
        body,
        out_shape=[pltpu.VMEM(shape, dtype) for shape, dtype in outs],
        in_specs=specs,
        out_specs=[VSPEC] * len(outs),
        scratch_shapes=[pltpu.VMEM(shape, dtype) for shape, dtype in scratch],
        compiler_params=pltpu.CompilerParams(vmem_limit_bytes=limit << 20),
        cost_estimate=pl.CostEstimate(flops=flops, bytes_accessed=1 << 20, transcendentals=0),
    )(*args)


def split_outside(x):
    hi = lax.reduce_precision(x, 8, 7)
    return hi.astype(BF16), (x - hi).astype(BF16)


def swap(x, axis, bit):
    count = lax.axis_size(axis)
    return lax.ppermute(x, axis, [(i, i ^ bit) for i in range(count)])


def is_up(axis, bit):
    return (lax.axis_index(axis) // bit) % 2


def halve(x, axis, bit, dim):
    size = x.shape[dim] // 2
    up = is_up(axis, bit)
    send = lax.dynamic_slice_in_dim(x, (1 - up) * size, size, dim)
    keep = lax.dynamic_slice_in_dim(x, up * size, size, dim)
    return keep + swap(send, axis, bit)


def unhalve(x, axis, bit, dim):
    other = swap(x, axis, bit)
    first = is_up(axis, bit) == 0
    return jnp.concatenate(
        [jnp.where(first, x, other), jnp.where(first, other, x)], axis=dim
    )


def bits_of(axis):
    bit = 1
    while bit < lax.axis_size(axis):
        yield bit
        bit *= 2


def plan(order, dims):
    steps = []
    rest = [("gx", b) for b in bits_of("gx")]
    if order:
        rest = rest[::-1]
    rest += [("gy", b) for b in bits_of("gy")] + [("gz", b) for b in bits_of("gz") if b > 1]
    for n, (axis, bit) in enumerate(rest):
        steps.append((axis, bit, dims[n] if n < len(dims) else None))
    return steps


def all_sum(piece, steps):
    for axis, bit, dim in steps:
        if dim is None:
            piece = piece + swap(piece, axis, bit)
        else:
            piece = halve(piece, axis, bit, dim)
    for axis, bit, dim in steps[::-1]:
        if dim is not None:
            piece = unhalve(piece, axis, bit, dim)
    return piece


def shifted(value, axis, by):
    length = lax.axis_size(axis)
    pairs = [(i, i + by) for i in range(length) if 0 <= i + by < length]
    return lax.ppermute(value, axis, pairs)


def with_halo(cells, sides):
    for axis, dim in sides:
        cells = jnp.concatenate(
            [shifted(cells, axis, 1), cells, shifted(cells, axis, -1)], axis=dim
        )
    return cells


def fold(ghost_grad, axis, dim):
    def part(i):
        return lax.slice_in_dim(ghost_grad, i, i + 1, axis=dim)

    return part(1) + shifted(part(2), axis, 1) + shifted(part(0), axis, -1)


def per_device(
    positions,
    species,
    neighbours,
    embed_center,
    embed_neigh,
    embed_radial,
    value_proj,
    env_weight,
    latent_weight,
    path_weight,
    out_weight,
    scale_table,
    shift_table,
    cotangent,
):
    core = is_up("gz", 1).astype(jnp.int32).reshape(1)
    carried = jnp.concatenate(
        [positions, species.astype(F32)[None], jnp.zeros((4, ATOMS), F32)], 0
    )
    table = with_halo(
        carried.reshape(8, 1, 1, 1, ATOMS), (("gz", 3), ("gy", 2), ("gx", 1))
    ).reshape(8, NTAB)
    own_rows = jnp.concatenate(
        [positions, species.astype(F32)[None], cotangent[None], jnp.zeros((3, ATOMS), F32)], 0
    )
    cent = jnp.tile(own_rows, (1, NB))
    slots = neighbours.reshape(1, EDGES)
    w0h, w0l = split_outside(latent_weight[0])
    w1h, w1l = split_outside(latent_weight[1])
    ve = jnp.concatenate([value_proj, env_weight[0]], 1)
    ev = env_weight[1]
    path = jnp.broadcast_to(path_weight.reshape(9 * CHANNELS, 1), (9 * CHANNELS, 128))
    outw = out_weight[:, None]
    scale = scale_table[:, None]
    shift = shift_table[:, None]

    big = 2 * EDGES * LATENT * WIDE * 3
    wide = ((WIDE, EDGES), BF16)
    half = ((HALF, EDGES), BF16)
    quarter = ((WIDE, QUARTER), F32)
    x0h, x0l, x1h, x1l, z0, pre, vw, w1, geo, g0, g1, f1 = call(
        fwd_kernel,
        [
            wide, wide, wide, wide,
            ((LATENT, EDGES), F32), ((LATENT, EDGES), F32), ((128, EDGES), F32),
            ((64, EDGES), F32), ((G_ROWS, EDGES), F32), ((576, 128), F32), ((576, 128), F32),
            ((576, EDGES), F32),
        ],
        (table, slots, cent, w0h, w0l, embed_center, embed_neigh, embed_radial, ve, ev, path,
         scale),
        [
            ((8, EDGES), F32), ((288, LATENT), BF16), ((LATENT, 128), BF16), ((LATENT, 128), BF16),
            ((LATENT, 64), BF16), ((LATENT, 64), BF16),
        ],
        flops=3 * big,
    )

    late = []
    for h in range(2):
        late.append(
            call(
                functools.partial(late_kernel, h),
                [half, half, quarter, quarter, ((8, EDGES), F32), ((8, HALF), F32)],
                (core, x1h, x1l, w1h, w1l, outw, geo),
                [((HALF, 128), F32)],
                scalar=True,
                flops=big,
            )
        )
    (qah, qal, keep_a, send_a, sla, outa), (qbh, qbl, keep_b, send_b, slb, outb) = late
    lat_a = all_sum(keep_a + swap(send_a, "gz", 1), plan(0, (0, 0, 0, 1)))
    lat_b = all_sum(keep_b + swap(send_b, "gz", 1), plan(1, (0, 0, 0, 1)))

    ds1, dw1h, dw1l, dy1 = call(
        mid_kernel,
        [((192, EDGES), F32), ((64, EDGES), BF16), ((64, EDGES), BF16), ((16, EDGES), F32)],
        (qah, qal, qbh, qbl, w1h, w1l, f1, g1, w1, geo),
        [((576, 128), F32)],
        flops=big // 4,
    )
    early = []
    for h in range(2):
        early.append(
            call(
                functools.partial(early_kernel, h),
                [((HALF, EDGES), F32), half, half, quarter, quarter, ((8, EDGES), F32)],
                (core, qah, qal, qbh, qbl, w1h, w1l, ev, dw1h, dw1l, outw, geo, z0, x0h, x0l),
                [((HALF, 64), BF16), ((HALF, 64), BF16)],
                scalar=True,
                flops=big,
            )
        )
    (dla, rah, ral, keep_c, send_c, sea), (dlb, rbh, rbl, keep_d, send_d, seb) = early
    lat_c = all_sum(keep_c + swap(send_c, "gz", 1), plan(0, (0, 0, 0, 1)))
    lat_d = all_sum(keep_d + swap(send_d, "gz", 1), plan(1, (0, 0, 0, 1)))

    dvwh, dvwl, dy, dpath, dve, dev = call(
        couple_kernel,
        [
            ((128, EDGES), BF16), ((128, EDGES), BF16), ((16, EDGES), F32), ((576, 128), F32),
            ((128, LATENT), F32), ((64, LATENT), F32),
        ],
        (rah, ral, rbh, rbl, w0h, w0l, vw, geo, g0, g1, ds1, path, x0h, x0l, x1h, x1l, dw1h, dw1l,
         dy1),
        [((192, EDGES), F32), ((576, 128), F32), ((16, EDGES), F32)],
        flops=big // 3,
    )
    hots_grad, rad_grad, ghost, own, energy, misc = call(
        last_kernel,
        [
            ((128, LATENT), F32), ((8, LATENT), F32), ((8, NTAB), F32), ((8, 128), F32),
            ((8, 128), F32), ((8, LATENT), F32),
        ],
        (rah, ral, rbh, rbl, w0h, w0l, ve, dvwh, dvwl, dla, dlb, pre, geo, slots, cent,
         embed_radial, sla, slb, sea, seb, dy, dpath, scale, shift),
        [
            ((LATENT, 128), BF16), ((LATENT, 128), BF16), ((LATENT, EDGES), BF16),
            ((LATENT, EDGES), BF16), ((1, EDGES), F32), ((8, EDGES), F32),
        ],
        flops=2 * big,
    )
    dout = jnp.concatenate([outa, outb], 1)
    small = jnp.concatenate([hots_grad, dve, dev, rad_grad, misc[0:1], dout[0:1], misc[2:8]], 0)
    small = halve(small, "gz", 1, 1)
    small = all_sum(small, plan(0, (0, 1, 1)))
    small = unhalve(small, "gz", 1, 1)
    misc_row = small[328]

    ghost_grad = ghost[0:3].reshape(3, 3, 3, 3, ATOMS)
    ghost_grad = fold(fold(fold(ghost_grad, "gx", 1), "gy", 2), "gz", 3)
    position_grad = ghost_grad.reshape(3, ATOMS) - own[0:3, 0:ATOMS]

    first = is_up("gz", 1) == 0

    def joined(mine):
        other = swap(mine, "gz", 1)
        return [jnp.where(first, mine, other), jnp.where(first, other, mine)]

    d_latent = jnp.stack(
        [
            jnp.concatenate(joined(lat_c) + joined(lat_d), 1),
            jnp.concatenate(joined(lat_a) + joined(lat_b), 1),
        ]
    )
    return (
        energy[0, 0:ATOMS],
        position_grad,
        small[0:64],
        small[64:128],
        small[320:328],
        small[128:192].T,
        jnp.stack([small[192:256].T, small[256:320].T]),
        d_latent,
        misc_row[0:576].reshape(9, CHANNELS),
        small[329],
        misc_row[576:640],
        misc_row[640:704],
    )


def solution(mesh):
    everything = ("gx", "gy", "gz")
    return jax.shard_map(
        per_device,
        mesh=mesh,
        in_specs=(
            P(None, everything),
            P(everything),
            P(None, everything),
            P(),
            P(),
            P(),
            P(),
            P(),
            P(),
            P(),
            P(),
            P(),
            P(),
            P(everything),
        ),
        out_specs=(
            P(everything),
            P(None, everything),
            P(),
            P(),
            P(),
            P(),
            P(),
            P(),
            P(),
            P(),
            P(),
            P(),
        ),
        check_vma=False,
    )
```

```python
import functools
import math

import jax
import jax.numpy as jnp
import numpy as np
from jax import lax
from jax.experimental import pallas as pl
from jax.experimental.pallas import tpu as pltpu
from jax.sharding import PartitionSpec as P

LATENT = 1024
CHANNELS = 64
NSPEC = 64
NBESSEL = 8
NB = 32
ATOMS = 32
EDGES = NB * ATOMS
WIDE = LATENT + 3 * CHANNELS
HALF = LATENT // 2
QUARTER = LATENT // 4
NTAB = 9 * 128
OWN = 4 * 128 + ATOMS

CUTOFF = 5.0
RH = 0.7071067811865476
HR = 0.7071067811865476
SR = 0.4082482904638631
R3 = math.sqrt(3.0)
Q75 = math.sqrt(7.5)
NORM = NB**-0.5
BESSEL = math.sqrt(2.0 / CUTOFF)

F32 = jnp.float32
BF16 = jnp.bfloat16

G_SMOOTH, G_LIVE, G_R, G_DISP, G_GRAD, G_RAD, G_GS, G_SPEC = 9, 10, 11, 12, 15, 16, 24, 25
G_ROWS = 32


def dot(a, b, ca, cb):
    return lax.dot_general(a, b, (((ca,), (cb,)), ((), ())), preferred_element_type=F32)


def dot3(ah, al, bh, bl, ca, cb):
    return dot(ah, bh, ca, cb) + dot(ah, bl, ca, cb) + dot(al, bh, ca, cb)


def split(x):
    hi = x.astype(BF16)
    return hi, (x - hi.astype(F32)).astype(BF16)


def pieces(x):
    hi = x.astype(BF16).astype(F32)
    rest = x - hi
    mid = rest.astype(BF16).astype(F32)
    return hi, mid, rest - mid


def sigmoid(x):
    return 0.5 * jnp.tanh(0.5 * x) + 0.5


def silu_both(x):
    sig = sigmoid(x)
    return x * sig, sig * (1.0 + x * (1.0 - sig))


def lanes(i, width):
    return pl.ds(pl.multiple_of(i * width, width), width)


def over(count, body):
    def step(i, carry):
        body(i)
        return carry

    lax.fori_loop(0, count, step, 0)


def iota(shape, dim):
    return lax.broadcasted_iota(jnp.int32, shape, dim)


def slot_total(x):
    x = x + pltpu.roll(x, 64, 1)
    return x + pltpu.roll(x, 32, 1)


def make_env(geo, w, env):
    for c in range(9):
        acc = None
        for k in range(8):
            cols = pl.ds(k * 128, 128)
            term = w[:, cols] if c == 0 else geo[c : c + 1, cols] * w[:, cols]
            acc = term if acc is None else acc + term
        env[c * 64 : (c + 1) * 64, :] = slot_total(acc) * NORM


def rows_of(ref, c, cols=slice(None)):
    return ref[c * 64 : (c + 1) * 64, cols]


def pack_kernel(pos, spec, out):
    out[...] = jnp.zeros_like(out)
    out[0:3, 0:ATOMS] = pos[...]
    out[3:4, 0:ATOMS] = spec[...].astype(F32)


def join_z_kernel(place, own, even_in, odd_in, out):
    is_odd = place[0] == 1
    left = jnp.where(is_odd, even_in[...], odd_in[...])
    right = jnp.where(is_odd, odd_in[...], even_in[...])
    out[...] = left + pltpu.roll(own[...], ATOMS, 1) + pltpu.roll(right, 2 * ATOMS, 1)


def join_y_kernel(place, own, even_in, odd_in, out):
    is_odd = place[1] == 1
    out[:, 0:128] = jnp.where(is_odd, even_in[...], odd_in[...])
    out[:, 128:256] = own[...]
    out[:, 256:384] = jnp.where(is_odd, odd_in[...], even_in[...])


def prep_kernel(
    w, ec_in, en_in, rad_in, vp_in, env_in, neigh_in, pos_in, spec_in, cot_in, path_in, outw_in,
    scale_in, shift_in,
    w0h, w0l, w1h, w1l, table, veh, vel, evh, evl, path_b, cols, slots, cent, rad_w,
    ec, en, vp, env, neigh, pos, spec, cot, path, outw, scale, shift, square, sem,
):
    pairs = (
        (ec_in, ec), (en_in, en), (rad_in, rad_w), (vp_in, vp), (env_in, env), (neigh_in, neigh),
        (pos_in, pos), (spec_in, spec), (cot_in, cot), (path_in, path), (outw_in, outw),
        (scale_in, scale), (shift_in, shift),
    )
    copies = [
        pltpu.make_async_copy(src, dst, sem.at[n]) for n, (src, dst) in enumerate(pairs)
    ]
    for copy in copies:
        copy.start()

    for layer, (hi, lo) in enumerate(((w0h, w0l), (w1h, w1l))):

        def part(i, layer=layer, hi=hi, lo=lo):
            rows = pl.ds(pl.multiple_of(i * 64, 64), 64)
            hi[rows, :], lo[rows, :] = split(w[layer, rows, :])

        over(WIDE // 64, part)
    for copy in copies:
        copy.wait()

    ech, ecl = split(ec[...])
    enh, enl = split(en[...])
    rh = rad_w[...].astype(BF16).astype(F32)
    rl = rad_w[...] - rh
    table[0:64, :] = ech
    table[64:128, :] = enh
    table[128:192, :] = ecl
    table[192:256, :] = enl
    table[256:288, :] = jnp.concatenate([rh, rl, rh, jnp.zeros_like(rh)], 0).astype(BF16)
    veh[0:64, :], vel[0:64, :] = split(vp[...])
    veh[64:128, :], vel[64:128, :] = split(env[0])
    evh[...], evl[...] = split(env[1])

    square[...] = jnp.zeros_like(square)
    square[0:8, :] = outw[...]
    square[8:9, 0:64] = scale[...]
    square[9:10, 0:64] = shift[...]
    square[16:25, 0:64] = path[...]
    turned = square[...].T
    cols[...] = turned
    for n in range(9):
        path_b[n * 64 : (n + 1) * 64, :] = jnp.broadcast_to(
            turned[0:64, 16 + n : 17 + n], (64, 128)
        )

    square[0:32, :] = jnp.zeros((32, 128), F32)
    square[0:32, 0:ATOMS] = neigh[...].astype(F32)
    row = square[pl.ds(0, 8, 4), :]
    for i in range(1, 4):
        row = row + pltpu.roll(square[pl.ds(i, 8, 4), :], i * ATOMS, 1)
    padded = row
    for m in range(1, 9):
        padded = padded + jnp.where(row >= 96.0 * m, 32.0, 0.0)
    padded = padded.astype(jnp.int32)
    square[0:8, :] = jnp.zeros((8, 128), F32)
    square[0:3, 0:ATOMS] = pos[...]
    square[3:4, 0:ATOMS] = spec[...].astype(F32)
    square[4:5, 0:ATOMS] = cot[...]
    own = square[0:8, :]
    own = own + pltpu.roll(own, 32, 1)
    own = own + pltpu.roll(own, 64, 1)
    for k in range(8):
        slots[:, k * 128 : (k + 1) * 128] = padded[k : k + 1]
        cent[:, k * 128 : (k + 1) * 128] = own


def fwd_kernel(
    place, tab, even_in, odd_in, slots, cent, w0h, w0l, table, veh, vel, evh, evl, path, columns,
    x0h, x0l, x1h, x1l, z0, pre, vw, w1, geo, g0, g1, f1,
    gat,
):
    is_odd = place[2] == 1
    whole = jnp.concatenate(
        [
            jnp.where(is_odd, even_in[...], odd_in[...]),
            tab[...],
            jnp.where(is_odd, odd_in[...], even_in[...]),
        ],
        1,
    )
    hi, mid, lo = pieces(whole)
    tab24 = jnp.concatenate([hi, mid, lo], 0).astype(BF16)

    def gather(i):
        cols = lanes(i, 256)
        hot = jnp.where(iota((NTAB, 256), 0) == slots[:, cols], 1.0, 0.0).astype(BF16)
        got = dot(tab24, hot, 1, 0)
        gat[:, cols] = got[0:8] + got[8:16] + got[16:24]

    over(4, gather)

    live = jnp.where(slots[...] != OWN + iota((1, EDGES), 1) % ATOMS, 1.0, 0.0)
    dead = 1.0 - live
    dx = (gat[0:1, :] - cent[0:1, :]) * live + dead * 2.5
    dy = (gat[1:2, :] - cent[1:2, :]) * live
    dz = (gat[2:3, :] - cent[2:3, :]) * live
    r = jnp.sqrt(dx * dx + dy * dy + dz * dz)
    inv = 1.0 / r
    t = r / CUTOFF
    t2 = t * t
    t6 = t2 * t2 * t2
    smooth = live * (1.0 - 28.0 * t6 + 48.0 * t6 * t - 21.0 * t6 * t * t)
    ux, uy, uz = dx * inv, dy * inv, dz * inv
    geo[0:1, :] = jnp.ones_like(r)
    geo[1:2, :] = R3 * ux
    geo[2:3, :] = R3 * uy
    geo[3:4, :] = R3 * uz
    geo[4:5, :] = Q75 * HR * (ux * ux - uy * uy)
    geo[5:6, :] = Q75 * SR * (ux * ux + uy * uy - 2.0 * uz * uz)
    geo[6:7, :] = Q75 * 2.0 * HR * (ux * uy)
    geo[7:8, :] = Q75 * 2.0 * HR * (ux * uz)
    geo[8:9, :] = Q75 * 2.0 * HR * (uy * uz)
    geo[9:10, :] = smooth
    geo[10:11, :] = live
    geo[11:12, :] = r
    geo[12:13, :] = dx
    geo[13:14, :] = dy
    geo[14:15, :] = dz
    order = (iota((8, EDGES), 0) + 1).astype(F32) * (math.pi / CUTOFF)
    geo[16:24, :] = smooth * BESSEL * jnp.sin(order * r) * inv
    hot_c = jnp.where(iota((NSPEC, EDGES), 0).astype(F32) == cent[3:4, :], 1.0, 0.0)
    grad = cent[4:5, :] * jnp.sum(hot_c * columns[0:64, 8:9], 0, keepdims=True)
    geo[15:16, :] = grad
    geo[24:25, :] = grad * smooth
    geo[25:26, :] = gat[3:4, :]
    geo[26:32, :] = jnp.zeros((6, EDGES), F32)

    def embed(i):
        cols = lanes(i, 256)
        kinds = iota((NSPEC, 256), 0).astype(F32)
        hot_c = jnp.where(kinds == cent[3:4, cols], 1.0, 0.0)
        hot_n = jnp.where(kinds == gat[3:4, cols], 1.0, 0.0)
        hots = jnp.concatenate([hot_c, hot_n], 0).astype(BF16)
        rad = geo[16:24, cols]
        rad_h = rad.astype(BF16).astype(F32)
        rads = jnp.concatenate([rad_h, rad_h, rad - rad_h, jnp.zeros_like(rad)], 0).astype(BF16)
        pre[:, cols] = dot(table[...], jnp.concatenate([hots, hots, rads], 0), 0, 0)
        sm = geo[9:10, cols]
        for b in range(8):
            rows = pl.ds(b * 128, 128)
            p = pre[rows, cols]
            x0h[rows, cols], x0l[rows, cols] = split(p * sigmoid(p) * sm)
        vw[:, cols] = dot3(
            veh[...], vel[...], x0h[0:LATENT, cols], x0l[0:LATENT, cols], 1, 0
        )

    over(4, embed)
    make_env(geo, vw.at[64:128, :], g0)

    def tensor(k):
        cols = lanes(k, 128)
        v = vw[0:64, cols]
        y = [geo[c : c + 1, cols] for c in range(9)]
        e0 = rows_of(g0, 0)
        e1, e2, e3 = rows_of(g0, 1), rows_of(g0, 2), rows_of(g0, 3)
        a, b, c = y[1] * e1, y[2] * e2, y[3] * e3
        vec = a + b + c
        quad = y[4] * rows_of(g0, 4)
        for m in range(5, 9):
            quad = quad + y[m] * rows_of(g0, m)
        x0h[1024:1088, cols], x0l[1024:1088, cols] = split(v * e0)
        x0h[1088:1152, cols], x0l[1088:1152, cols] = split(v * vec)
        x0h[1152:1216, cols], x0l[1152:1216, cols] = split(v * quad)
        p = [rows_of(path, n) for n in range(9)]
        e12, e13 = y[1] * e2, y[1] * e3
        e21, e23 = y[2] * e1, y[2] * e3
        e31, e32 = y[3] * e1, y[3] * e2
        q00 = HR * y[4] + SR * y[5]
        q11 = SR * y[5] - HR * y[4]
        q22 = -2.0 * SR * y[5]
        q01, q02, q12 = HR * y[6], HR * y[7], HR * y[8]
        f1[0:64, cols] = v * (p[0] * e0 + p[1] * vec)
        p3g = p[3] * e0
        f1[64:128, cols] = v * (
            p[2] * e1 + p3g * y[1] + p[4] * (e23 - e32) + p[5] * (q00 * e1 + q01 * e2 + q02 * e3)
        )
        f1[128:192, cols] = v * (
            p[2] * e2 + p3g * y[2] + p[4] * (e31 - e13) + p[5] * (q01 * e1 + q11 * e2 + q12 * e3)
        )
        f1[192:256, cols] = v * (
            p[2] * e3 + p3g * y[3] + p[4] * (e12 - e21) + p[5] * (q02 * e1 + q12 * e2 + q22 * e3)
        )
        p8g = p[8] * e0
        pair = (
            HR * (a - b),
            SR * (a + b - 2.0 * c),
            HR * (e12 + e21),
            HR * (e13 + e31),
            HR * (e23 + e32),
        )
        for m in range(5):
            f1[(4 + m) * 64 : (5 + m) * 64, cols] = v * (
                p[6] * pair[m] + p[7] * rows_of(g0, 4 + m) + p8g * y[4 + m]
            )

    over(8, tensor)

    def layer(i):
        cols = lanes(i, 256)
        z0[:, cols] = dot3(w0h[...], w0l[...], x0h[:, cols], x0l[:, cols], 0, 0)
        sm = geo[9:10, cols]
        for b in range(8):
            rows = pl.ds(b * 128, 128)
            z = z0[rows, cols]
            old = x0h[rows, cols].astype(F32) + x0l[rows, cols].astype(F32)
            x1h[rows, cols], x1l[rows, cols] = split((old + sm * (z * sigmoid(z))) * RH)
        w1[:, cols] = dot3(
            evh[...], evl[...], x1h[0:LATENT, cols], x1l[0:LATENT, cols], 1, 0
        )

    over(4, layer)
    make_env(geo, w1, g1)

    def scalars(k):
        cols = lanes(k, 128)
        s0 = rows_of(f1, 0, cols) * rows_of(g1, 0)
        s1 = rows_of(f1, 1, cols) * rows_of(g1, 1)
        for c in range(2, 4):
            s1 = s1 + rows_of(f1, c, cols) * rows_of(g1, c)
        s2 = rows_of(f1, 4, cols) * rows_of(g1, 4)
        for c in range(5, 9):
            s2 = s2 + rows_of(f1, c, cols) * rows_of(g1, c)
        x1h[1024:1088, cols], x1l[1024:1088, cols] = split(s0)
        x1h[1088:1152, cols], x1l[1088:1152, cols] = split(s1)
        x1h[1152:1216, cols], x1l[1152:1216, cols] = split(s2)

    over(8, scalars)


def grad_kernel(place, xh, xl, qh, ql, keep, send):
    width = keep.shape[1]
    for out, block in ((send, 1 - place[3]), (keep, place[3])):
        for n in range(0, width, QUARTER):
            rows = pl.ds(pl.multiple_of(block * width, width) + n, QUARTER)
            out[0:WIDE, n : n + QUARTER] = dot3(xh[...], xl[...], qh[rows, :], ql[rows, :], 1, 1)


def late_kernel(x1h, x1l, wh, wl, columns, geo, qh, ql, side, dout, acc):
    acc[...] = jnp.zeros_like(acc)
    side[...] = jnp.zeros_like(side)

    def step(i):
        cols = lanes(i, 256)
        z = dot3(wh[...], wl[...], x1h[:, cols], x1l[:, cols], 0, 0)
        sm = geo[9:10, cols]
        gs = geo[24:25, cols]
        scale = gs * sm * RH
        reach = jnp.zeros((8, 256), F32)
        total = jnp.zeros((8, 256), F32)
        for b in range(8):
            rows = pl.ds(b * 128, 128)
            si, dsi = silu_both(z[b * 128 : (b + 1) * 128])
            ow = columns[:, b : b + 1]
            qh[rows, cols], ql[rows, cols] = split((ow * scale) * dsi)
            lat = (x1h[rows, cols].astype(F32) + x1l[rows, cols].astype(F32) + sm * si) * RH
            part = gs * lat
            acc[rows, :] += part[:, 0:128] + part[:, 128:256]
            reach = reach + jnp.sum((ow * si).reshape(16, 8, 256), 0)
            total = total + jnp.sum((ow * lat).reshape(16, 8, 256), 0)
        side[0:1, cols] = jnp.sum(reach, 0, keepdims=True)
        side[1:2, cols] = jnp.sum(total, 0, keepdims=True)

    over(4, step)
    dout[...] = jnp.broadcast_to(jnp.sum(acc[...].T, 0, keepdims=True), dout.shape)


def mid_kernel(qh, ql, wh, wl, f1, g1, w1, geo, ds1, dwh, dwl, dy, denv):
    def scal(i):
        cols = lanes(i, 256)
        ds1[:, cols] = dot3(wh[1024:1216, :], wl[1024:1216, :], qh[:, cols], ql[:, cols], 1, 0)

    over(4, scal)
    for c in range(9):
        kind = 0 if c == 0 else (1 if c < 4 else 2)
        acc = None
        for k in range(8):
            cols = pl.ds(k * 128, 128)
            term = rows_of(ds1, kind, cols) * rows_of(f1, c, cols)
            acc = term if acc is None else acc + term
        denv[c * 64 : (c + 1) * 64, :] = slot_total(acc) * NORM
    env_back(geo, w1, denv, dwh, dwl, dy, None)


def env_back(geo, w, denv, dwh, dwl, dy, more):
    def step(k):
        cols = lanes(k, 128)
        acc = rows_of(denv, 0)
        wk = w[:, cols]
        rows = [jnp.zeros((1, 128), F32)]
        for c in range(1, 9):
            d = rows_of(denv, c)
            acc = acc + geo[c : c + 1, cols] * d
            rows.append(jnp.sum(wk * d, 0, keepdims=True))
        dwh[:, cols], dwl[:, cols] = split(acc)
        for c in range(1, 9):
            if more is None:
                dy[c : c + 1, cols] = rows[c]
            else:
                dy[c : c + 1, cols] = rows[c] + more[c : c + 1, cols]

    over(8, step)


def early_kernel(
    half, q1h, q1l, wh, wl, evh, evl, dwh, dwl, columns, geo, z0, dlat, qh, ql, side
):
    base = half * HALF
    side[...] = jnp.zeros_like(side)

    def step(i):
        cols = lanes(i, 256)
        wr = slice(base, base + HALF)
        d = dot3(wh[wr, :], wl[wr, :], q1h[:, cols], q1l[:, cols], 1, 0) + dot3(
            evh[:, wr], evl[:, wr], dwh[:, cols], dwl[:, cols], 0, 0
        )
        sm = geo[9:10, cols] * RH
        gs = geo[24:25, cols] * RH
        total = jnp.zeros((8, 256), F32)
        for b in range(4):
            rows = pl.ds(b * 128, 128)
            frows = pl.ds(base + b * 128, 128)
            ow = columns[:, half * 4 + b : half * 4 + b + 1]
            dl = d[b * 128 : (b + 1) * 128] + ow * gs
            dlat[rows, cols] = dl * RH
            si, dsi = silu_both(z0[frows, cols])
            qh[rows, cols], ql[rows, cols] = split(dl * dsi * sm)
            total = total + jnp.sum((dl * si).reshape(16, 8, 256), 0)
        side[0:1, cols] = jnp.sum(total, 0, keepdims=True) * RH

    over(4, step)


def couple_kernel(
    qah, qal, qbh, qbl, wh, wl, vw, geo, g0, g1, ds1, path, dy1,
    dvwh, dvwl, dy, dpath,
    ds0, denv, dyv,
):
    def scal(i):
        cols = lanes(i, 256)
        ds0[:, cols] = dot3(
            wh[1024:1216, 0:512], wl[1024:1216, 0:512], qah[:, cols], qal[:, cols], 1, 0
        ) + dot3(
            wh[1024:1216, 512:1024], wl[1024:1216, 512:1024], qbh[:, cols], qbl[:, cols], 1, 0
        )

    over(4, scal)
    denv[...] = jnp.zeros_like(denv)
    dpath[...] = jnp.zeros_like(dpath)

    def step(k):
        cols = lanes(k, 128)
        v = vw[0:64, cols]
        y = [geo[c : c + 1, cols] for c in range(9)]
        e = [rows_of(g0, c) for c in range(9)]
        p = [rows_of(path, n) for n in range(9)]
        s = [rows_of(ds0, n, cols) for n in range(3)]
        u = [rows_of(ds1, n, cols) for n in range(3)]
        f0 = u[0] * rows_of(g1, 0)
        fv = [u[1] * rows_of(g1, c) for c in range(1, 4)]
        fq = [u[2] * rows_of(g1, c) for c in range(4, 9)]
        yv, yq, ev_, eq = y[1:4], y[4:9], e[1:4], e[4:9]

        def dot_of(a, b):
            out = a[0] * b[0]
            for i in range(1, len(a)):
                out = out + a[i] * b[i]
            return out

        m00 = HR * yq[0] + SR * yq[1]
        m11 = SR * yq[1] - HR * yq[0]
        m22 = -2.0 * SR * yq[1]
        m01, m02, m12 = HR * yq[2], HR * yq[3], HR * yq[4]
        t00 = HR * fq[0] + SR * fq[1]
        t11 = SR * fq[1] - HR * fq[0]
        t22 = (-2.0 * SR) * fq[1]
        t01, t02, t12 = HR * fq[2], HR * fq[3], HR * fq[4]

        te = [
            t00 * ev_[0] + t01 * ev_[1] + t02 * ev_[2],
            t01 * ev_[0] + t11 * ev_[1] + t12 * ev_[2],
            t02 * ev_[0] + t12 * ev_[1] + t22 * ev_[2],
        ]
        ty = [
            t00 * yv[0] + t01 * yv[1] + t02 * yv[2],
            t01 * yv[0] + t11 * yv[1] + t12 * yv[2],
            t02 * yv[0] + t12 * yv[1] + t22 * yv[2],
        ]
        mf = [
            m00 * fv[0] + m01 * fv[1] + m02 * fv[2],
            m01 * fv[0] + m11 * fv[1] + m12 * fv[2],
            m02 * fv[0] + m12 * fv[1] + m22 * fv[2],
        ]
        ef = [
            ev_[1] * fv[2] - ev_[2] * fv[1],
            ev_[2] * fv[0] - ev_[0] * fv[2],
            ev_[0] * fv[1] - ev_[1] * fv[0],
        ]
        fy = [
            fv[1] * yv[2] - fv[2] * yv[1],
            fv[2] * yv[0] - fv[0] * yv[2],
            fv[0] * yv[1] - fv[1] * yv[0],
        ]
        e_fv = dot_of(ev_, fv)
        y_fv = dot_of(yv, fv)
        e_fq = dot_of(eq, fq)
        y_fq = dot_of(yq, fq)
        vec = dot_of(yv, ev_)
        y_te = dot_of(yv, te)
        e_mf = dot_of(ev_, mf)
        y_ef = dot_of(yv, ef)

        grads = (
            e[0] * f0,
            vec * f0,
            e_fv,
            e[0] * y_fv,
            y_ef,
            e_mf,
            y_te,
            e_fq,
            e[0] * y_fq,
        )
        for n in range(9):
            dpath[n * 64 : (n + 1) * 64, :] += v * grads[n]

        p1f = p[1] * f0
        d0 = s[0] * e[0] + p[0] * e[0] * f0 + p[2] * e_fv + p[7] * e_fq
        p3e = p[3] * e[0]
        p8e = p[8] * e[0]
        s1f = s[1] + p1f
        dv = d0
        for i in range(3):
            di = s1f * ev_[i] + p3e * fv[i] + p[4] * ef[i] + p[6] * te[i]
            dv = dv + yv[i] * di
            dyv[1 + i : 2 + i, cols] = jnp.sum(v * di, 0, keepdims=True)
        a, b, c = fv[0] * ev_[0], fv[1] * ev_[1], fv[2] * ev_[2]
        bil = (
            HR * (a - b),
            SR * (a + b - 2.0 * c),
            HR * (fv[0] * ev_[1] + fv[1] * ev_[0]),
            HR * (fv[0] * ev_[2] + fv[2] * ev_[0]),
            HR * (fv[1] * ev_[2] + fv[2] * ev_[1]),
        )
        for m in range(5):
            dm = s[2] * eq[m] + p[5] * bil[m] + p8e * fq[m]
            dv = dv + yq[m] * dm
            dyv[4 + m : 5 + m, cols] = jnp.sum(v * dm, 0, keepdims=True)
        dvwh[0:64, cols], dvwl[0:64, cols] = split(dv)

        denv[0:64, :] += v * (s[0] + p[0] * f0 + p[3] * y_fv + p[8] * y_fq)
        for i in range(3):
            denv[(1 + i) * 64 : (2 + i) * 64, :] += v * (
                s1f * yv[i] + p[2] * fv[i] + p[4] * fy[i] + p[5] * mf[i] + p[6] * ty[i]
            )
        for m in range(5):
            denv[(4 + m) * 64 : (5 + m) * 64, :] += v * (s[2] * yq[m] + p[7] * fq[m])

    over(8, step)
    for c in range(9):
        denv[c * 64 : (c + 1) * 64, :] = slot_total(rows_of(denv, c)) * NORM
    dyv[0:1, :] = jnp.zeros((1, EDGES), F32)
    dyv[...] += dy1[...]
    env_back(geo, vw.at[64:128, :], denv, dvwh.at[64:128, :], dvwl.at[64:128, :], dy, dyv)


def pre_kernel(
    half, qah, qal, qbh, qbl, wh, wl, veh, vel, dvwh, dvwl, dl, pre, geo, rad_w,
    qph, qpl, side, drad,
):
    base = half * HALF
    wr = slice(base, base + HALF)
    rwh, rwl = split(jnp.concatenate([rad_w[:, wr], jnp.zeros((8, HALF), F32)], 0))
    side[...] = jnp.zeros_like(side)

    def step(i):
        cols = lanes(i, 256)
        sm = geo[9:10, cols]
        total = jnp.zeros((8, 256), F32)
        d = (
            dot3(wh[wr, 0:512], wl[wr, 0:512], qah[:, cols], qal[:, cols], 1, 0)
            + dot3(wh[wr, 512:1024], wl[wr, 512:1024], qbh[:, cols], qbl[:, cols], 1, 0)
            + dot3(veh[:, wr], vel[:, wr], dvwh[:, cols], dvwl[:, cols], 0, 0)
        )
        for b in range(4):
            rows = pl.ds(b * 128, 128)
            frows = pl.ds(base + b * 128, 128)
            dd = d[b * 128 : (b + 1) * 128] + dl[rows, cols]
            si, dsi = silu_both(pre[frows, cols])
            qph[rows, cols], qpl[rows, cols] = split(dd * dsi * sm)
            total = total + jnp.sum((dd * si).reshape(16, 8, 256), 0)
        side[0:1, cols] = jnp.sum(total, 0, keepdims=True)
        drad[:, cols] = dot3(rwh, rwl, qph[:, cols], qpl[:, cols], 1, 0)[0:8]

    over(4, step)


def last_kernel(
    place, qpah, qpal, qpbh, qpbl, spa, spb, drad_a, drad_b, geo, slots, cent, sl, sea, seb, dy,
    dpath, columns, dout,
    small_keep, small_send, ghost_own, ghost_even, ghost_odd, own, energy,
    ghost, small,
):
    kinds = iota((NSPEC, EDGES), 0).astype(F32)
    hot_c = jnp.where(kinds == cent[3:4, :], 1.0, 0.0)
    hot_n = jnp.where(kinds == geo[25:26, :], 1.0, 0.0)
    hots = jnp.concatenate([hot_c, hot_n], 0).astype(BF16)
    rad = geo[16:24, :]
    rad_h = rad.astype(BF16).astype(F32)
    rads = jnp.concatenate([rad_h, rad - rad_h], 0).astype(BF16)
    left = jnp.concatenate([hots, rads], 0)
    for n, (qh, ql) in enumerate(((qpah, qpal), (qpbh, qpbl))):
        full = dot(left, qh[...], 1, 1)
        rest = dot(left, ql[...], 1, 1)
        part = slice(n * HALF, (n + 1) * HALF)
        small[0:128, part] = full[0:128] + rest[0:128]
        small[128:136, part] = full[128:136] + full[136:144] + rest[128:136]

    live, r, smooth = geo[10:11, :], geo[11:12, :], geo[9:10, :]
    inv = 1.0 / r
    grad = geo[15:16, :]
    reach = sl[0:1, :]
    lat_out = sl[1:2, :]
    order = (iota((8, EDGES), 0) + 1).astype(F32) * (math.pi / CUTOFF)
    angle = order * r
    sine = jnp.sin(angle) * inv
    cosine = jnp.cos(angle) * inv
    dr8 = drad_a[...] + drad_b[...]
    d_s = (
        grad * lat_out
        + grad * smooth * RH * reach
        + sea[0:1, :]
        + seb[0:1, :]
        + spa[0:1, :]
        + spb[0:1, :]
        + BESSEL * jnp.sum(dr8 * sine, 0, keepdims=True)
    )
    t = r / CUTOFF
    t2 = t * t
    gap = 1.0 - t
    d_r = d_s * (live * (-168.0 / CUTOFF) * (t2 * t2 * t) * (gap * gap)) + (
        smooth * BESSEL
    ) * jnp.sum(dr8 * (order * cosine - sine * inv), 0, keepdims=True)
    ux, uy, uz = geo[12:13, :] * inv, geo[13:14, :] * inv, geo[14:15, :] * inv
    yy = [dy[c : c + 1, :] for c in range(9)]
    h2, s2 = 2.0 * HR * Q75, 2.0 * SR * Q75
    gx = R3 * yy[1] + ux * (h2 * yy[4] + s2 * yy[5]) + h2 * (uy * yy[6] + uz * yy[7])
    gy = R3 * yy[2] + uy * (s2 * yy[5] - h2 * yy[4]) + h2 * (ux * yy[6] + uz * yy[8])
    gz = R3 * yy[3] - 2.0 * s2 * uz * yy[5] + h2 * (ux * yy[7] + uy * yy[8])
    along = ux * gx + uy * gy + uz * gz
    zero = jnp.zeros((5, EDGES), F32)
    disp = jnp.concatenate(
        [
            live * ((gx - ux * along) * inv + ux * d_r),
            live * ((gy - uy * along) * inv + uy * d_r),
            live * ((gz - uz * along) * inv + uz * d_r),
            zero,
        ],
        0,
    )
    hi, mid, lo = pieces(disp)
    disp24 = jnp.concatenate([hi, mid, lo], 0).astype(BF16)
    acc = None
    mine = None
    for k in range(8):
        term = disp[:, k * 128 : (k + 1) * 128]
        mine = term if mine is None else mine + term
    own[...] = slot_total(mine)
    for i in range(4):
        cols = pl.ds(i * 256, 256)
        hot = jnp.where(iota((NTAB, 256), 0) == slots[:, cols], 1.0, 0.0).astype(BF16)
        term = dot(disp24[:, i * 256 : (i + 1) * 256], hot, 1, 1)
        acc = term if acc is None else acc + term
    ghost[...] = acc[0:8] + acc[8:16] + acc[16:24]
    fold_out(place[2] == 1, ghost, 384, ghost_own, ghost_even, ghost_odd)

    edge_energy = smooth * lat_out
    total = None
    for k in range(8):
        term = edge_energy[:, k * 128 : (k + 1) * 128]
        total = term if total is None else total + term
    total = slot_total(jnp.broadcast_to(total, (8, 128)))[0:1]
    hot = jnp.where(iota((NSPEC, 128), 0).astype(F32) == cent[3:4, 0:128], 1.0, 0.0)
    energy[...] = jnp.broadcast_to(
        jnp.sum(hot * columns[0:64, 8:9], 0, keepdims=True) * total
        + jnp.sum(hot * columns[0:64, 9:10], 0, keepdims=True),
        energy.shape,
    )
    cot = cent[4:5, 0:128] * jnp.where(iota((1, 128), 1) < ATOMS, 1.0, 0.0)
    stack = jnp.concatenate(
        [dpath[...], hot * (cot * total), hot * cot, jnp.zeros((64, 128), F32)], 0
    )
    row = jnp.sum(stack.T, 0, keepdims=True)
    small[136:144, :] = jnp.zeros((8, LATENT), F32)
    small[136:137, 0:768] = row
    small[137:138, :] = dout[0:1, :]
    mine = pl.ds(pl.multiple_of(place[3] * HALF, HALF), HALF)
    other = pl.ds(pl.multiple_of((1 - place[3]) * HALF, HALF), HALF)
    small_keep[...] = small[:, mine]
    small_send[...] = small[:, other]


def fold_out(is_odd, blocks, width, own, even, odd):
    before, later = blocks[:, 0:width], blocks[:, 2 * width : 3 * width]
    own[...] = blocks[:, width : 2 * width]
    even[...] = jnp.where(is_odd, before, later)
    odd[...] = jnp.where(is_odd, later, before)


def fold_y_kernel(place, own, even_in, odd_in, out, even, odd, buf):
    buf[...] = own[...] + even_in[...] + odd_in[...]
    fold_out(place[1] == 1, buf, 128, out, even, odd)


def fold_z_kernel(place, own, even_in, odd_in, out, even, odd):
    total = own[...] + even_in[...] + odd_in[...]
    later = pltpu.roll(total, 128 - 2 * ATOMS, 1)
    is_odd = place[0] == 1
    out[...] = pltpu.roll(total, 128 - ATOMS, 1)
    even[...] = jnp.where(is_odd, total, later)
    odd[...] = jnp.where(is_odd, later, total)


def fold_end_kernel(own, even_in, odd_in, centre, energy, out, energy_out):
    total = own[...] + even_in[...] + odd_in[...] - centre[...]
    out[...] = total[0:3, 0:ATOMS]
    energy_out[...] = energy[0:1, 0:ATOMS]


def weights_kernel(dvwh, dvwl, x0h, x0l, dw1h, dw1l, x1h, x1l, out):
    out[0:128, :] = dot3(dvwh[...], dvwl[...], x0h[0:LATENT, :], x0l[0:LATENT, :], 1, 1)
    out[128:192, :] = dot3(dw1h[...], dw1l[...], x1h[0:LATENT, :], x1l[0:LATENT, :], 1, 1)


def grad_more_kernel(place, xh, xl, qh, ql, more, keep, send):
    grad_kernel(place, xh, xl, qh, ql, keep, send)
    for out, block in ((send, 1 - place[3]), (keep, place[3])):
        for n in range(2):
            cols = pl.ds(pl.multiple_of(block * HALF, HALF) + n * QUARTER, QUARTER)
            out[WIDE + n * 192 : WIDE + (n + 1) * 192, :] = more[:, cols]


def halves(shape, dim):
    rows, cols = shape
    return (rows // 2, cols) if dim == 0 else (rows, cols // 2) if dim == 1 else shape


def half_of(shape, dim, bit):
    rows, cols = shape
    if dim == 0:
        rows //= 2
        return pl.ds(pl.multiple_of(bit * rows, 8), rows), slice(None)
    cols //= 2
    return slice(None), pl.ds(pl.multiple_of(bit * cols, 128), cols)


def down_kernel(dim, flag, place, keep, got, *outs):
    if dim is None:
        outs[0][...] = keep[...] + got[...]
        return
    for out, bit in zip(outs, (1 - place[flag], place[flag])):
        index = half_of(keep.shape, dim, bit)
        out[...] = keep[index] + got[index]


def up_kernel(dim, flag, place, mine, got, out):
    out[half_of(out.shape, dim, place[flag])] = mine[...]
    out[half_of(out.shape, dim, 1 - place[flag])] = got[...]


def end_kernel(layer, count, core_at, place, *refs):
    srcs, out, sem = refs[:count], refs[-2], refs[-1]
    core = place[core_at]
    copies = []
    width = LATENT // count
    for n, src in enumerate(srcs):
        block = core if n % 2 == 0 else 1 - core
        cols = pl.ds(pl.multiple_of((n // 2 * 2 + block) * width, width), width)
        copies.append(pltpu.make_async_copy(src.at[0:WIDE, :], out.at[layer, :, cols], sem.at[n]))
    for copy in copies:
        copy.start()
    for copy in copies:
        copy.wait()


def small_end_kernel(
    core_at, place, mine, got, more, more_got,
    center, neigh, radial, value, env, path, out, scale, shift,
):
    for src, b in ((mine, place[core_at]), (got, 1 - place[core_at])):
        cols = pl.ds(pl.multiple_of(b * HALF, HALF), HALF)
        center[:, cols] = src[0:64, :]
        neigh[:, cols] = src[64:128, :]
        radial[:, cols] = src[128:136, :]
    for src, b in ((more, place[core_at]), (more_got, 1 - place[core_at])):
        for n in range(2):
            base = WIDE + n * 192
            cols = pl.ds(pl.multiple_of(b * HALF, HALF) + n * QUARTER, QUARTER)
            value[:, cols] = src[base : base + 64, :]
            env[0, :, cols] = src[base + 64 : base + 128, :]
            env[1, :, cols] = src[base + 128 : base + 192, :]
    first = jnp.where(place[core_at] == 0, mine[136:144, :], got[136:144, :])
    second = jnp.where(place[core_at] == 0, got[136:144, :], mine[136:144, :])
    row = jnp.concatenate([first, second], 1)
    for n in range(9):
        path[n : n + 1, :] = row[0:1, n * 64 : (n + 1) * 64]
    scale[...] = row[0:1, 576:640]
    shift[...] = row[0:1, 640:704]
    for n in range(8):
        out[n : n + 1, :] = row[1:2, n * 128 : (n + 1) * 128]


VSPEC = pl.BlockSpec(memory_space=pltpu.VMEM)
SSPEC = pl.BlockSpec(memory_space=pltpu.SMEM)
ASPEC = pl.BlockSpec(memory_space=pl.ANY)
HSPEC = pl.BlockSpec(memory_space=pltpu.HBM)


class Order:
    def __init__(self):
        self.token = None

    def __call__(
        self, body, outs, args, scratch=(), scalar=False, hbm=(), plain=False, alias=None, us=1,
        limit=8, name=None,
    ):
        specs = [HSPEC if n in hbm else VSPEC for n in range(len(args))]
        if scalar:
            specs[0] = SSPEC
        count, given = len(args), len(outs)
        tokens = () if self.token is None else (self.token,)

        def kernel(*refs):
            after = refs[count + len(tokens) :]
            after[given][...] = jnp.zeros((8, 128), F32)
            body(*refs[:count], *after[:given], *after[given + 1 :])

        if plain:
            shapes = [jax.ShapeDtypeStruct(shape, dtype) for shape, dtype in outs]
        else:
            shapes = [pltpu.VMEM(shape, dtype) for shape, dtype in outs]
        out_spec = HSPEC if plain == "hbm" else VSPEC
        got = pl.pallas_call(
            kernel,
            name=name or getattr(body, "func", body).__name__,
            out_shape=shapes + [pltpu.VMEM((8, 128), F32)],
            in_specs=specs + [ASPEC] * len(tokens),
            out_specs=[out_spec] * given + [VSPEC],
            scratch_shapes=list(scratch),
            input_output_aliases=alias or {},
            compiler_params=pltpu.CompilerParams(vmem_limit_bytes=limit << 20),
            cost_estimate=pl.CostEstimate(
                flops=int(us * 3e9), bytes_accessed=1 << 20, transcendentals=0
            ),
        )(*args, *tokens)
        self.token = got[-1]
        return got[:-1]


def is_up(axis, bit):
    return (lax.axis_index(axis) // bit) & 1


def even_pairs(axis):
    return [(i, i ^ 1) for i in range(lax.axis_size(axis))]


def odd_pairs(axis):
    count = lax.axis_size(axis)
    return [p for i in range(1, count - 1, 2) for p in ((i, i + 1), (i + 1, i))]


def neighbours_of(axis, even, odd):
    pairs = odd_pairs(axis)
    return (
        lax.ppermute(even, axis, even_pairs(axis)),
        lax.ppermute(odd, axis, pairs) if pairs else jnp.zeros_like(odd),
    )


class Route:
    def __init__(self, mesh_sizes, base):
        sizes = dict(mesh_sizes)
        names = list(sizes)

        def bits(axis, least=1):
            return [(axis, 1 << n) for n in range(20) if least <= 1 << n < sizes[axis]]

        flat, tall = bits("gx"), bits("gy") + bits("gz", 2)
        first = [("gz", 1)]
        self.steps = list(zip(first + flat + tall, first + flat[::-1] + tall[::-1]))
        self.count = len(self.steps)
        self.base = base
        self.names = tuple(names)
        coords = [()]
        for name in names:
            coords = [c + (i,) for c in coords for i in range(sizes[name])]
        index = {c: n for n, c in enumerate(coords)}
        self.pairs = []
        for step in self.steps:
            pairs = []
            for c in coords:
                axis, bit = step[c[names.index("gz")] & 1]
                at = names.index(axis)
                pairs.append((index[c], index[c[:at] + (c[at] ^ bit,) + c[at + 1 :]]))
            self.pairs.append(pairs)

    def flags(self):
        core = is_up("gz", 1)
        return [jnp.where(core == 1, is_up(*two), is_up(*one)) for one, two in self.steps]

    def swap(self, x, at):
        return lax.ppermute(x, self.names, self.pairs[at])


class Sum:
    def __init__(self, name, order, place, route, keep, send, dims):
        self.name = name
        self.order, self.place, self.route = order, place, route
        self.dims = (1,) + dims + (None,) * (route.count - 1 - len(dims))
        self.keep, self.send = keep, send
        self.at, self.rising = 0, False
        self.shapes = []
        self.launch()

    def launch(self):
        with jax.named_scope(f"sum_{self.name}_{'up' if self.rising else 'down'}_{self.at}"):
            self.got = self.route.swap(self.send, self.at)

    @property
    def over(self):
        return self.rising and self.at == 0

    def land(self):
        (self.climb if self.rising else self.descend)()
        self.launch()

    def call(self, body, dim, flag, shapes, args):
        return self.order(
            functools.partial(body, dim, flag),
            [(shape, F32) for shape in shapes],
            (self.place, *args),
            scalar=True,
            us=2,
            name=f"land_{self.name}_{'up' if self.rising else 'down'}_{self.at}",
        )

    def descend(self):
        self.shapes.append(self.keep.shape)
        self.at += 1
        last = self.at == self.route.count
        dim = None if last else self.dims[self.at]
        shapes = [halves(self.keep.shape, dim)] * (1 if dim is None else 2)
        outs = self.call(
            down_kernel, dim, self.route.base + self.at, shapes, (self.keep, self.got)
        )
        self.send, self.keep = outs[0], outs[-1]
        if last:
            self.rising = True
            self.rise()

    def rise(self):
        self.at -= 1
        while self.at > 0 and self.dims[self.at] is None:
            self.at -= 1

    def climb(self):
        (self.send,) = self.call(
            up_kernel,
            self.dims[self.at],
            self.route.base + self.at,
            [self.shapes[self.at - 1]],
            (self.send, self.got),
        )
        self.rise()


def per_device(
    positions,
    species,
    neighbours,
    embed_center,
    embed_neigh,
    embed_radial,
    value_proj,
    env_weight,
    latent_weight,
    path_weight,
    out_weight,
    scale_table,
    shift_table,
    cotangent,
):
    vm, sem = pltpu.VMEM, pltpu.SemaphoreType
    order = Order()
    sizes = [(axis, lax.axis_size(axis)) for axis in ("gx", "gy", "gz")]
    route = Route(sizes, 4)
    place = [is_up("gz", 1), is_up("gy", 1), is_up("gx", 1), is_up("gz", 1)]
    place = jnp.stack(place + route.flags()).astype(jnp.int32)
    spec_row = species.reshape(1, ATOMS)

    (table,) = order(pack_kernel, [((8, 128), F32)], (positions, spec_row), us=0.3)
    even, odd = neighbours_of("gz", table, table)
    (table,) = order(
        join_z_kernel, [((8, 128), F32)], (place, table, even, odd), scalar=True, us=0.3
    )
    even, odd = neighbours_of("gy", table, table)
    (table,) = order(
        join_y_kernel, [((8, 384), F32)], (place, table, even, odd), scalar=True, us=0.3
    )
    even, odd = neighbours_of("gx", table, table)

    wide = ((WIDE, EDGES), BF16)
    half = ((HALF, EDGES), BF16)
    row64 = ((64, LATENT), BF16)
    row128 = ((128, LATENT), BF16)
    w0h, w0l, w1h, w1l, hots, veh, vel, evh, evl, path, columns, slots, cent, rad_w = order(
        prep_kernel,
        [
            wide, wide, wide, wide, ((288, LATENT), BF16), row128, row128, row64, row64,
            ((576, 128), F32), ((128, 128), F32), ((1, EDGES), jnp.int32), ((8, EDGES), F32),
            ((8, LATENT), F32),
        ],
        (latent_weight, embed_center, embed_neigh, embed_radial, value_proj.T,
         jnp.swapaxes(env_weight, 1, 2), neighbours, positions, spec_row,
         cotangent.reshape(1, ATOMS), path_weight, out_weight.reshape(8, 128),
         scale_table.reshape(1, NSPEC), shift_table.reshape(1, NSPEC)),
        [
            vm((NSPEC, LATENT), F32), vm((NSPEC, LATENT), F32), vm((CHANNELS, LATENT), F32),
            vm((2, CHANNELS, LATENT), F32), vm((NB, ATOMS), jnp.int32), vm((3, ATOMS), F32),
            vm((1, ATOMS), jnp.int32), vm((1, ATOMS), F32), vm((9, CHANNELS), F32),
            vm((8, 128), F32), vm((1, NSPEC), F32), vm((1, NSPEC), F32), vm((128, 128), F32),
            sem.DMA((13,)),
        ],
        hbm=range(1, 14),
        us=4,
    )

    x0h, x0l, x1h, x1l, z0, pre, vw, w1, geo, g0, g1, f1 = order(
        fwd_kernel,
        [
            wide, wide, wide, wide,
            ((LATENT, EDGES), F32), ((LATENT, EDGES), F32), ((128, EDGES), F32),
            ((64, EDGES), F32), ((G_ROWS, EDGES), F32), ((576, 128), F32), ((576, 128), F32),
            ((576, EDGES), F32),
        ],
        (place, table, even, odd, slots, cent, w0h, w0l, hots, veh, vel, evh, evl, path, columns),
        [vm((8, EDGES), F32)],
        scalar=True,
        us=22,
    )

    big = (0, 0, 1, 0)
    few = (1, 1)

    def unit(name, xh, xl, qh, ql, more=None, width=QUARTER):
        rows = WIDE if more is None else WIDE + 2 * 192
        keep, send = order(
            grad_kernel if more is None else grad_more_kernel,
            [((rows, width), F32)] * 2,
            (place, xh, xl, qh, ql) + (() if more is None else (more,)),
            scalar=True,
            us=5,
        )
        return Sum(name, order, place, route, keep, send, big)

    def early(h):
        return order(
            functools.partial(early_kernel, h),
            [((HALF, EDGES), F32), half, half, ((8, EDGES), F32)],
            (q1h, q1l, w1h, w1l, evh, evl, dw1h, dw1l, columns, geo, z0),
            us=5,
        )

    q1h, q1l, sl, dout = order(
        late_kernel,
        [
            ((LATENT, EDGES), BF16), ((LATENT, EDGES), BF16), ((8, EDGES), F32),
            ((8, LATENT), F32),
        ],
        (x1h, x1l, w1h, w1l, columns, geo),
        [vm((LATENT, 128), F32)],
        us=12,
    )
    a = unit("a", x1h, x1l, q1h, q1l, width=HALF)
    ds1, dw1h, dw1l, dy1 = order(
        mid_kernel,
        [((192, EDGES), F32), ((64, EDGES), BF16), ((64, EDGES), BF16), ((16, EDGES), F32)],
        (q1h, q1l, w1h, w1l, f1, g1, w1, geo),
        [vm((576, 128), F32)],
        us=3,
    )
    dla, rah, ral, sea = early(0)
    a.land()
    c = unit("c", x0h, x0l, rah, ral)
    dlb, rbh, rbl, seb = early(1)
    c.land()
    dvwh, dvwl, dy, dpath = order(
        couple_kernel,
        [
            ((128, EDGES), BF16), ((128, EDGES), BF16), ((16, EDGES), F32), ((576, 128), F32),
        ],
        (rah, ral, rbh, rbl, w0h, w0l, vw, geo, g0, g1, ds1, path, dy1),
        [vm((192, EDGES), F32), vm((576, 128), F32), vm((16, EDGES), F32)],
        us=7,
    )
    a.land()
    (more,) = order(
        weights_kernel, [((192, LATENT), F32)], (dvwh, dvwl, x0h, x0l, dw1h, dw1l, x1h, x1l), us=3
    )
    d = unit("d", x0h, x0l, rbh, rbl, more)
    c.land()
    a.land()

    def before(h, dl):
        return order(
            functools.partial(pre_kernel, h),
            [half, half, ((8, EDGES), F32), ((8, EDGES), F32)],
            (rah, ral, rbh, rbl, w0h, w0l, veh, vel, dvwh, dvwl, dl, pre, geo, rad_w),
            us=6,
        )

    qpah, qpal, spa, drad_a = before(0, dla)
    d.land()
    c.land()
    qpbh, qpbl, spb, drad_b = before(1, dlb)
    a.land()
    c.land()
    small_keep, small_send, ghost, ghost_even, ghost_odd, own, energy = order(
        last_kernel,
        [
            ((144, HALF), F32), ((144, HALF), F32), ((8, 384), F32), ((8, 384), F32),
            ((8, 384), F32), ((8, 128), F32), ((8, 128), F32),
        ],
        (place, qpah, qpal, qpbh, qpbl, spa, spb, drad_a, drad_b, geo, slots, cent, sl, sea, seb,
         dy, dpath, columns, dout),
        [vm((8, NTAB), F32), vm((144, LATENT), F32)],
        scalar=True,
        us=5,
    )
    s = Sum("s", order, place, route, small_keep, small_send, few)
    ghost_even, ghost_odd = neighbours_of("gx", ghost_even, ghost_odd)
    d.land()
    a.land()
    s.land()
    c.land()
    s.land()
    d.land()
    a.land()
    s.land()
    c.land()
    ghost, ghost_even, ghost_odd = order(
        fold_y_kernel, [((8, 128), F32)] * 3, (place, ghost, ghost_even, ghost_odd),
        [vm((8, 384), F32)], scalar=True, us=0.3,
    )
    ghost_even, ghost_odd = neighbours_of("gy", ghost_even, ghost_odd)
    s.land()
    d.land()
    a.land()
    c.land()
    s.land()
    d.land()
    ghost, ghost_even, ghost_odd = order(
        fold_z_kernel, [((8, 128), F32)] * 3, (place, ghost, ghost_even, ghost_odd),
        scalar=True, us=0.3,
    )
    ghost_even, ghost_odd = neighbours_of("gz", ghost_even, ghost_odd)
    chains = [s, d, c, a]
    while any(not chain.over for chain in chains):
        for chain in chains:
            if not chain.over:
                chain.land()

    position_grad, energies = order(
        fold_end_kernel, [((3, ATOMS), F32), ((1, ATOMS), F32)],
        (ghost, ghost_even, ghost_odd, own, energy), plain=True, us=0.3,
    )

    def finish(layer, parts, done):
        args = (place, *[x for part in parts for x in (part.send, part.got)]) + done
        last = len(args) - 1
        return order(
            functools.partial(end_kernel, layer, 2 * len(parts), 3),
            [((2, WIDE, LATENT), F32)],
            args,
            [sem.DMA((4,))],
            scalar=True,
            hbm=(last,) if done else (),
            plain="hbm",
            alias={last: 0} if done else None,
            us=3,
        )

    d_latent = finish(1, (a,), ())
    (d_latent,) = finish(0, (c, d), tuple(d_latent))
    center, neigh, radial, value, env, path_grad, out, scale, shift = order(
        functools.partial(small_end_kernel, 3),
        [
            ((NSPEC, LATENT), F32), ((NSPEC, LATENT), F32), ((NBESSEL, LATENT), F32),
            ((CHANNELS, LATENT), F32), ((2, CHANNELS, LATENT), F32), ((9, CHANNELS), F32),
            ((8, 128), F32), ((1, NSPEC), F32), ((1, NSPEC), F32),
        ],
        (place, s.send, s.got, d.send, d.got),
        scalar=True,
        plain=True,
        us=2,
    )
    return (
        energies.reshape(ATOMS),
        position_grad,
        center,
        neigh,
        radial,
        value.T,
        jnp.swapaxes(env, 1, 2),
        d_latent,
        path_grad,
        out.reshape(LATENT),
        scale.reshape(NSPEC),
        shift.reshape(NSPEC),
    )


def solution(mesh):
    everything = ("gx", "gy", "gz")
    return jax.shard_map(
        per_device,
        mesh=mesh,
        in_specs=(
            P(None, everything),
            P(everything),
            P(None, everything),
            P(),
            P(),
            P(),
            P(),
            P(),
            P(),
            P(),
            P(),
            P(),
            P(),
            P(everything),
        ),
        out_specs=(
            P(everything),
            P(None, everything),
            P(),
            P(),
            P(),
            P(),
            P(),
            P(),
            P(),
            P(),
            P(),
            P(),
        ),
        check_vma=False,
    )
```

```python
import functools
import math

import jax
import jax.numpy as jnp
import numpy as np
from jax import lax
from jax.experimental import pallas as pl
from jax.experimental.pallas import tpu as pltpu
from jax.sharding import PartitionSpec as P

LATENT = 1024
CHANNELS = 64
NSPEC = 64
NBESSEL = 8
NB = 32
ATOMS = 32
EDGES = NB * ATOMS
WIDE = LATENT + 3 * CHANNELS
HALF = LATENT // 2
QUARTER = LATENT // 4
NTAB = 9 * 128
OWN = 4 * 128 + ATOMS

CUTOFF = 5.0
RH = 0.7071067811865476
HR = 0.7071067811865476
SR = 0.4082482904638631
R3 = math.sqrt(3.0)
Q75 = math.sqrt(7.5)
NORM = NB**-0.5
BESSEL = math.sqrt(2.0 / CUTOFF)

F32 = jnp.float32
BF16 = jnp.bfloat16

G_SMOOTH, G_LIVE, G_R, G_DISP, G_GRAD, G_RAD, G_GS, G_SPEC = 9, 10, 11, 12, 15, 16, 24, 25
G_ROWS = 32


def dot(a, b, ca, cb):
    return lax.dot_general(a, b, (((ca,), (cb,)), ((), ())), preferred_element_type=F32)


def dot3(ah, al, bh, bl, ca, cb):
    return dot(ah, bh, ca, cb) + dot(ah, bl, ca, cb) + dot(al, bh, ca, cb)


def split(x):
    hi = x.astype(BF16)
    return hi, (x - hi.astype(F32)).astype(BF16)


def pieces(x):
    hi = x.astype(BF16).astype(F32)
    rest = x - hi
    mid = rest.astype(BF16).astype(F32)
    return hi, mid, rest - mid


def sigmoid(x):
    return 0.5 * jnp.tanh(0.5 * x) + 0.5


def silu_both(x):
    sig = sigmoid(x)
    return x * sig, sig * (1.0 + x * (1.0 - sig))


def lanes(i, width):
    return pl.ds(pl.multiple_of(i * width, width), width)


def over(count, body):
    def step(i, carry):
        body(i)
        return carry

    lax.fori_loop(0, count, step, 0)


def staggered(count, bufs, first, second):
    first(0, bufs[0])
    for i in range(count):
        if i + 1 < count:
            first(i + 1, bufs[(i + 1) % 2])
        second(i, bufs[i % 2])


def iota(shape, dim):
    return lax.broadcasted_iota(jnp.int32, shape, dim)


def slot_total(x):
    x = x + pltpu.roll(x, 64, 1)
    return x + pltpu.roll(x, 32, 1)


def make_env(geo, w, env):
    for c in range(9):
        acc = None
        for k in range(8):
            cols = pl.ds(k * 128, 128)
            term = w[:, cols] if c == 0 else geo[c : c + 1, cols] * w[:, cols]
            acc = term if acc is None else acc + term
        env[c * 64 : (c + 1) * 64, :] = slot_total(acc) * NORM


def rows_of(ref, c, cols=slice(None)):
    return ref[c * 64 : (c + 1) * 64, cols]


def pack_kernel(pos, spec, out):
    out[...] = jnp.zeros_like(out)
    out[0:3, 0:ATOMS] = pos[...]
    out[3:4, 0:ATOMS] = spec[...].astype(F32)


def join_z_kernel(place, own, even_in, odd_in, out):
    is_odd = place[0] == 1
    left = jnp.where(is_odd, even_in[...], odd_in[...])
    right = jnp.where(is_odd, odd_in[...], even_in[...])
    out[...] = left + pltpu.roll(own[...], ATOMS, 1) + pltpu.roll(right, 2 * ATOMS, 1)


def join_y_kernel(place, own, even_in, odd_in, out):
    is_odd = place[1] == 1
    out[:, 0:128] = jnp.where(is_odd, even_in[...], odd_in[...])
    out[:, 128:256] = own[...]
    out[:, 256:384] = jnp.where(is_odd, odd_in[...], even_in[...])


def prep_kernel(
    w, ec_in, en_in, rad_in, vp_in, env_in, neigh_in, pos_in, spec_in, cot_in, path_in, outw_in,
    scale_in, shift_in,
    w0h, w0l, w1h, w1l, table, veh, vel, evh, evl, path_b, cols, slots, cent, rad_w,
    ec, en, vp, env, neigh, pos, spec, cot, path, outw, scale, shift, square, sem,
):
    pairs = (
        (ec_in, ec), (en_in, en), (rad_in, rad_w), (vp_in, vp), (env_in, env), (neigh_in, neigh),
        (pos_in, pos), (spec_in, spec), (cot_in, cot), (path_in, path), (outw_in, outw),
        (scale_in, scale), (shift_in, shift),
    )
    copies = [
        pltpu.make_async_copy(src, dst, sem.at[n]) for n, (src, dst) in enumerate(pairs)
    ]
    for copy in copies:
        copy.start()

    for layer, (hi, lo) in enumerate(((w0h, w0l), (w1h, w1l))):

        def part(i, layer=layer, hi=hi, lo=lo):
            rows = pl.ds(pl.multiple_of(i * 64, 64), 64)
            hi[rows, :], lo[rows, :] = split(w[layer, rows, :])

        over(WIDE // 64, part)
    for copy in copies:
        copy.wait()

    ech, ecl = split(ec[...])
    enh, enl = split(en[...])
    rh = rad_w[...].astype(BF16).astype(F32)
    rl = rad_w[...] - rh
    table[0:64, :] = ech
    table[64:128, :] = enh
    table[128:192, :] = ecl
    table[192:256, :] = enl
    table[256:288, :] = jnp.concatenate([rh, rl, rh, jnp.zeros_like(rh)], 0).astype(BF16)
    veh[0:64, :], vel[0:64, :] = split(vp[...])
    veh[64:128, :], vel[64:128, :] = split(env[0])
    evh[...], evl[...] = split(env[1])

    square[...] = jnp.zeros_like(square)
    square[0:8, :] = outw[...]
    square[8:9, 0:64] = scale[...]
    square[9:10, 0:64] = shift[...]
    square[16:25, 0:64] = path[...]
    turned = square[...].T
    cols[...] = turned
    for n in range(9):
        path_b[n * 64 : (n + 1) * 64, :] = jnp.broadcast_to(
            turned[0:64, 16 + n : 17 + n], (64, 128)
        )

    square[0:32, :] = jnp.zeros((32, 128), F32)
    square[0:32, 0:ATOMS] = neigh[...].astype(F32)
    row = square[pl.ds(0, 8, 4), :]
    for i in range(1, 4):
        row = row + pltpu.roll(square[pl.ds(i, 8, 4), :], i * ATOMS, 1)
    padded = row
    for m in range(1, 9):
        padded = padded + jnp.where(row >= 96.0 * m, 32.0, 0.0)
    padded = padded.astype(jnp.int32)
    square[0:8, :] = jnp.zeros((8, 128), F32)
    square[0:3, 0:ATOMS] = pos[...]
    square[3:4, 0:ATOMS] = spec[...].astype(F32)
    square[4:5, 0:ATOMS] = cot[...]
    own = square[0:8, :]
    own = own + pltpu.roll(own, 32, 1)
    own = own + pltpu.roll(own, 64, 1)
    for k in range(8):
        slots[:, k * 128 : (k + 1) * 128] = padded[k : k + 1]
        cent[:, k * 128 : (k + 1) * 128] = own


def embed_inputs(cent, geo, cols):
    kinds = iota((NSPEC, 256), 0).astype(F32)
    hot_c = jnp.where(kinds == cent[3:4, cols], 1.0, 0.0)
    hot_n = jnp.where(kinds == geo[25:26, cols], 1.0, 0.0)
    hots = jnp.concatenate([hot_c, hot_n], 0).astype(BF16)
    rad = geo[16:24, cols]
    rad_h = rad.astype(BF16).astype(F32)
    rads = jnp.concatenate([rad_h, rad_h, rad - rad_h, jnp.zeros_like(rad)], 0).astype(BF16)
    return jnp.concatenate([hots, hots, rads], 0)


def fwd_kernel(
    place, tab, even_in, odd_in, slots, cent, w0h, w0l, table, veh, vel, evh, evl, path, columns,
    x0h, x0l, x1h, x1l, z0, vw, w1, geo, g0, g1, f1,
    gat, za, zb,
):
    is_odd = place[2] == 1
    whole = jnp.concatenate(
        [
            jnp.where(is_odd, even_in[...], odd_in[...]),
            tab[...],
            jnp.where(is_odd, odd_in[...], even_in[...]),
        ],
        1,
    )
    hi, mid, lo = pieces(whole)
    tab24 = jnp.concatenate([hi, mid, lo], 0).astype(BF16)

    def gather(i):
        cols = lanes(i, 256)
        hot = jnp.where(iota((NTAB, 256), 0) == slots[:, cols], 1.0, 0.0).astype(BF16)
        got = dot(tab24, hot, 1, 0)
        gat[:, cols] = got[0:8] + got[8:16] + got[16:24]

    over(4, gather)

    live = jnp.where(slots[...] != OWN + iota((1, EDGES), 1) % ATOMS, 1.0, 0.0)
    dead = 1.0 - live
    dx = (gat[0:1, :] - cent[0:1, :]) * live + dead * 2.5
    dy = (gat[1:2, :] - cent[1:2, :]) * live
    dz = (gat[2:3, :] - cent[2:3, :]) * live
    r = jnp.sqrt(dx * dx + dy * dy + dz * dz)
    inv = 1.0 / r
    t = r / CUTOFF
    t2 = t * t
    t6 = t2 * t2 * t2
    smooth = live * (1.0 - 28.0 * t6 + 48.0 * t6 * t - 21.0 * t6 * t * t)
    ux, uy, uz = dx * inv, dy * inv, dz * inv
    geo[0:1, :] = jnp.ones_like(r)
    geo[1:2, :] = R3 * ux
    geo[2:3, :] = R3 * uy
    geo[3:4, :] = R3 * uz
    geo[4:5, :] = Q75 * HR * (ux * ux - uy * uy)
    geo[5:6, :] = Q75 * SR * (ux * ux + uy * uy - 2.0 * uz * uz)
    geo[6:7, :] = Q75 * 2.0 * HR * (ux * uy)
    geo[7:8, :] = Q75 * 2.0 * HR * (ux * uz)
    geo[8:9, :] = Q75 * 2.0 * HR * (uy * uz)
    geo[9:10, :] = smooth
    geo[10:11, :] = live
    geo[11:12, :] = r
    geo[12:13, :] = dx
    geo[13:14, :] = dy
    geo[14:15, :] = dz
    order = (iota((8, EDGES), 0) + 1).astype(F32) * (math.pi / CUTOFF)
    geo[16:24, :] = smooth * BESSEL * jnp.sin(order * r) * inv
    hot_c = jnp.where(iota((NSPEC, EDGES), 0).astype(F32) == cent[3:4, :], 1.0, 0.0)
    grad = cent[4:5, :] * jnp.sum(hot_c * columns[0:64, 8:9], 0, keepdims=True)
    geo[15:16, :] = grad
    geo[24:25, :] = grad * smooth
    geo[25:26, :] = gat[3:4, :]
    geo[26:32, :] = jnp.zeros((6, EDGES), F32)

    def embed_product(i, out):
        cols = pl.ds(i * 256, 256)
        out[...] = dot(table[...], embed_inputs(cent, geo, cols), 0, 0)

    def embed(i, before):
        cols = pl.ds(i * 256, 256)
        sm = geo[9:10, cols]
        for b in range(8):
            rows = pl.ds(b * 128, 128)
            p = before[rows, :]
            x0h[rows, cols], x0l[rows, cols] = split(p * sigmoid(p) * sm)
        vw[:, cols] = dot3(
            veh[...], vel[...], x0h[0:LATENT, cols], x0l[0:LATENT, cols], 1, 0
        )

    staggered(4, (za, zb), embed_product, embed)
    make_env(geo, vw.at[64:128, :], g0)

    def tensor(k):
        cols = lanes(k, 128)
        v = vw[0:64, cols]
        y = [geo[c : c + 1, cols] for c in range(9)]
        e0 = rows_of(g0, 0)
        e1, e2, e3 = rows_of(g0, 1), rows_of(g0, 2), rows_of(g0, 3)
        a, b, c = y[1] * e1, y[2] * e2, y[3] * e3
        vec = a + b + c
        quad = y[4] * rows_of(g0, 4)
        for m in range(5, 9):
            quad = quad + y[m] * rows_of(g0, m)
        x0h[1024:1088, cols], x0l[1024:1088, cols] = split(v * e0)
        x0h[1088:1152, cols], x0l[1088:1152, cols] = split(v * vec)
        x0h[1152:1216, cols], x0l[1152:1216, cols] = split(v * quad)
        p = [rows_of(path, n) for n in range(9)]
        e12, e13 = y[1] * e2, y[1] * e3
        e21, e23 = y[2] * e1, y[2] * e3
        e31, e32 = y[3] * e1, y[3] * e2
        q00 = HR * y[4] + SR * y[5]
        q11 = SR * y[5] - HR * y[4]
        q22 = -2.0 * SR * y[5]
        q01, q02, q12 = HR * y[6], HR * y[7], HR * y[8]
        f1[0:64, cols] = v * (p[0] * e0 + p[1] * vec)
        p3g = p[3] * e0
        f1[64:128, cols] = v * (
            p[2] * e1 + p3g * y[1] + p[4] * (e23 - e32) + p[5] * (q00 * e1 + q01 * e2 + q02 * e3)
        )
        f1[128:192, cols] = v * (
            p[2] * e2 + p3g * y[2] + p[4] * (e31 - e13) + p[5] * (q01 * e1 + q11 * e2 + q12 * e3)
        )
        f1[192:256, cols] = v * (
            p[2] * e3 + p3g * y[3] + p[4] * (e12 - e21) + p[5] * (q02 * e1 + q12 * e2 + q22 * e3)
        )
        p8g = p[8] * e0
        pair = (
            HR * (a - b),
            SR * (a + b - 2.0 * c),
            HR * (e12 + e21),
            HR * (e13 + e31),
            HR * (e23 + e32),
        )
        for m in range(5):
            f1[(4 + m) * 64 : (5 + m) * 64, cols] = v * (
                p[6] * pair[m] + p[7] * rows_of(g0, 4 + m) + p8g * y[4 + m]
            )

    over(8, tensor)

    def layer_product(i, out):
        cols = pl.ds(i * 256, 256)
        out[...] = dot3(w0h[...], w0l[...], x0h[:, cols], x0l[:, cols], 0, 0)

    def layer(i, zs):
        cols = pl.ds(i * 256, 256)
        sm = geo[9:10, cols]
        for b in range(8):
            rows = pl.ds(b * 128, 128)
            z = zs[rows, :]
            z0[rows, cols] = z
            old = x0h[rows, cols].astype(F32) + x0l[rows, cols].astype(F32)
            x1h[rows, cols], x1l[rows, cols] = split((old + sm * (z * sigmoid(z))) * RH)
        w1[:, cols] = dot3(
            evh[...], evl[...], x1h[0:LATENT, cols], x1l[0:LATENT, cols], 1, 0
        )

    staggered(4, (za, zb), layer_product, layer)
    make_env(geo, w1, g1)

    def scalars(k):
        cols = lanes(k, 128)
        s0 = rows_of(f1, 0, cols) * rows_of(g1, 0)
        s1 = rows_of(f1, 1, cols) * rows_of(g1, 1)
        for c in range(2, 4):
            s1 = s1 + rows_of(f1, c, cols) * rows_of(g1, c)
        s2 = rows_of(f1, 4, cols) * rows_of(g1, 4)
        for c in range(5, 9):
            s2 = s2 + rows_of(f1, c, cols) * rows_of(g1, c)
        x1h[1024:1088, cols], x1l[1024:1088, cols] = split(s0)
        x1h[1088:1152, cols], x1l[1088:1152, cols] = split(s1)
        x1h[1152:1216, cols], x1l[1152:1216, cols] = split(s2)

    over(8, scalars)


def grad_kernel(mine, place, xh, xl, qh, ql, out):
    block = place[3] if mine else 1 - place[3]
    for n in range(0, HALF, QUARTER):
        rows = pl.ds(pl.multiple_of(block * HALF, HALF) + n, QUARTER)
        out[:, n : n + QUARTER] = dot3(xh[...], xl[...], qh[rows, :], ql[rows, :], 1, 1)


def late_kernel(x1h, x1l, wh, wl, columns, geo, qh, ql, side, dout, acc, za, zb):
    acc[...] = jnp.zeros_like(acc)
    side[...] = jnp.zeros_like(side)

    def product(i, out):
        cols = pl.ds(i * 256, 256)
        out[...] = dot3(wh[...], wl[...], x1h[:, cols], x1l[:, cols], 0, 0)

    def step(i, zs):
        cols = pl.ds(i * 256, 256)
        sm = geo[9:10, cols]
        gs = geo[24:25, cols]
        scale = gs * sm * RH
        reach = jnp.zeros((8, 256), F32)
        total = jnp.zeros((8, 256), F32)
        for b in range(8):
            rows = pl.ds(b * 128, 128)
            si, dsi = silu_both(zs[rows, :])
            ow = columns[:, b : b + 1]
            qh[rows, cols], ql[rows, cols] = split((ow * scale) * dsi)
            lat = (x1h[rows, cols].astype(F32) + x1l[rows, cols].astype(F32) + sm * si) * RH
            part = gs * lat
            acc[rows, :] += part[:, 0:128] + part[:, 128:256]
            reach = reach + jnp.sum((ow * si).reshape(16, 8, 256), 0)
            total = total + jnp.sum((ow * lat).reshape(16, 8, 256), 0)
        side[0:1, cols] = jnp.sum(reach, 0, keepdims=True)
        side[1:2, cols] = jnp.sum(total, 0, keepdims=True)

    staggered(4, (za, zb), product, step)
    dout[...] = jnp.broadcast_to(jnp.sum(acc[...].T, 0, keepdims=True), dout.shape)


def mid_kernel(qh, ql, wh, wl, f1, g1, w1, geo, ds1, dwh, dwl, dy, denv):
    def scal(i):
        cols = lanes(i, 256)
        ds1[:, cols] = dot3(wh[1024:1216, :], wl[1024:1216, :], qh[:, cols], ql[:, cols], 1, 0)

    over(4, scal)
    for c in range(9):
        kind = 0 if c == 0 else (1 if c < 4 else 2)
        acc = None
        for k in range(8):
            cols = pl.ds(k * 128, 128)
            term = rows_of(ds1, kind, cols) * rows_of(f1, c, cols)
            acc = term if acc is None else acc + term
        denv[c * 64 : (c + 1) * 64, :] = slot_total(acc) * NORM
    env_back(geo, w1, denv, dwh, dwl, dy, None)


def env_back(geo, w, denv, dwh, dwl, dy, more):
    def step(k):
        cols = lanes(k, 128)
        acc = rows_of(denv, 0)
        wk = w[:, cols]
        rows = [jnp.zeros((1, 128), F32)]
        for c in range(1, 9):
            d = rows_of(denv, c)
            acc = acc + geo[c : c + 1, cols] * d
            rows.append(jnp.sum(wk * d, 0, keepdims=True))
        dwh[:, cols], dwl[:, cols] = split(acc)
        for c in range(1, 9):
            if more is None:
                dy[c : c + 1, cols] = rows[c]
            else:
                dy[c : c + 1, cols] = rows[c] + more[c : c + 1, cols]

    over(8, step)


def early_kernel(
    q1h, q1l, wh, wl, evh, evl, dwh, dwl, columns, geo, z0, dlat, qh, ql, side, da, db
):
    side[...] = jnp.zeros_like(side)

    def product(i, out):
        cols = pl.ds(i * 256, 256)
        out[...] = dot3(
            wh[0:LATENT, :], wl[0:LATENT, :], q1h[:, cols], q1l[:, cols], 1, 0
        ) + dot3(evh[...], evl[...], dwh[:, cols], dwl[:, cols], 0, 0)

    def step(i, ds):
        cols = pl.ds(i * 256, 256)
        sm = geo[9:10, cols] * RH
        gs = geo[24:25, cols] * RH
        total = jnp.zeros((8, 256), F32)
        for b in range(8):
            rows = pl.ds(b * 128, 128)
            dl = ds[rows, :] + columns[:, b : b + 1] * gs
            dlat[rows, cols] = dl * RH
            si, dsi = silu_both(z0[rows, cols])
            qh[rows, cols], ql[rows, cols] = split(dl * dsi * sm)
            total = total + jnp.sum((dl * si).reshape(16, 8, 256), 0)
        side[0:1, cols] = jnp.sum(total, 0, keepdims=True) * RH

    staggered(4, (da, db), product, step)


def couple_kernel(
    qh, ql, wh, wl, vw, geo, g0, g1, ds1, path, dy1,
    dvwh, dvwl, dy, dpath,
    ds0, denv, dyv,
):
    def scal(i):
        cols = lanes(i, 256)
        ds0[:, cols] = dot3(wh[1024:1216, :], wl[1024:1216, :], qh[:, cols], ql[:, cols], 1, 0)

    over(4, scal)
    denv[...] = jnp.zeros_like(denv)
    dpath[...] = jnp.zeros_like(dpath)

    def step(k):
        cols = lanes(k, 128)
        v = vw[0:64, cols]
        y = [geo[c : c + 1, cols] for c in range(9)]
        e = [rows_of(g0, c) for c in range(9)]
        p = [rows_of(path, n) for n in range(9)]
        s = [rows_of(ds0, n, cols) for n in range(3)]
        u = [rows_of(ds1, n, cols) for n in range(3)]
        f0 = u[0] * rows_of(g1, 0)
        fv = [u[1] * rows_of(g1, c) for c in range(1, 4)]
        fq = [u[2] * rows_of(g1, c) for c in range(4, 9)]
        yv, yq, ev_, eq = y[1:4], y[4:9], e[1:4], e[4:9]

        def dot_of(a, b):
            out = a[0] * b[0]
            for i in range(1, len(a)):
                out = out + a[i] * b[i]
            return out

        m00 = HR * yq[0] + SR * yq[1]
        m11 = SR * yq[1] - HR * yq[0]
        m22 = -2.0 * SR * yq[1]
        m01, m02, m12 = HR * yq[2], HR * yq[3], HR * yq[4]
        t00 = HR * fq[0] + SR * fq[1]
        t11 = SR * fq[1] - HR * fq[0]
        t22 = (-2.0 * SR) * fq[1]
        t01, t02, t12 = HR * fq[2], HR * fq[3], HR * fq[4]

        te = [
            t00 * ev_[0] + t01 * ev_[1] + t02 * ev_[2],
            t01 * ev_[0] + t11 * ev_[1] + t12 * ev_[2],
            t02 * ev_[0] + t12 * ev_[1] + t22 * ev_[2],
        ]
        ty = [
            t00 * yv[0] + t01 * yv[1] + t02 * yv[2],
            t01 * yv[0] + t11 * yv[1] + t12 * yv[2],
            t02 * yv[0] + t12 * yv[1] + t22 * yv[2],
        ]
        mf = [
            m00 * fv[0] + m01 * fv[1] + m02 * fv[2],
            m01 * fv[0] + m11 * fv[1] + m12 * fv[2],
            m02 * fv[0] + m12 * fv[1] + m22 * fv[2],
        ]
        ef = [
            ev_[1] * fv[2] - ev_[2] * fv[1],
            ev_[2] * fv[0] - ev_[0] * fv[2],
            ev_[0] * fv[1] - ev_[1] * fv[0],
        ]
        fy = [
            fv[1] * yv[2] - fv[2] * yv[1],
            fv[2] * yv[0] - fv[0] * yv[2],
            fv[0] * yv[1] - fv[1] * yv[0],
        ]
        e_fv = dot_of(ev_, fv)
        y_fv = dot_of(yv, fv)
        e_fq = dot_of(eq, fq)
        y_fq = dot_of(yq, fq)
        vec = dot_of(yv, ev_)
        y_te = dot_of(yv, te)
        e_mf = dot_of(ev_, mf)
        y_ef = dot_of(yv, ef)

        grads = (
            e[0] * f0,
            vec * f0,
            e_fv,
            e[0] * y_fv,
            y_ef,
            e_mf,
            y_te,
            e_fq,
            e[0] * y_fq,
        )
        for n in range(9):
            dpath[n * 64 : (n + 1) * 64, :] += v * grads[n]

        p1f = p[1] * f0
        d0 = s[0] * e[0] + p[0] * e[0] * f0 + p[2] * e_fv + p[7] * e_fq
        p3e = p[3] * e[0]
        p8e = p[8] * e[0]
        s1f = s[1] + p1f
        dv = d0
        for i in range(3):
            di = s1f * ev_[i] + p3e * fv[i] + p[4] * ef[i] + p[6] * te[i]
            dv = dv + yv[i] * di
            dyv[1 + i : 2 + i, cols] = jnp.sum(v * di, 0, keepdims=True)
        a, b, c = fv[0] * ev_[0], fv[1] * ev_[1], fv[2] * ev_[2]
        bil = (
            HR * (a - b),
            SR * (a + b - 2.0 * c),
            HR * (fv[0] * ev_[1] + fv[1] * ev_[0]),
            HR * (fv[0] * ev_[2] + fv[2] * ev_[0]),
            HR * (fv[1] * ev_[2] + fv[2] * ev_[1]),
        )
        for m in range(5):
            dm = s[2] * eq[m] + p[5] * bil[m] + p8e * fq[m]
            dv = dv + yq[m] * dm
            dyv[4 + m : 5 + m, cols] = jnp.sum(v * dm, 0, keepdims=True)
        dvwh[0:64, cols], dvwl[0:64, cols] = split(dv)

        denv[0:64, :] += v * (s[0] + p[0] * f0 + p[3] * y_fv + p[8] * y_fq)
        for i in range(3):
            denv[(1 + i) * 64 : (2 + i) * 64, :] += v * (
                s1f * yv[i] + p[2] * fv[i] + p[4] * fy[i] + p[5] * mf[i] + p[6] * ty[i]
            )
        for m in range(5):
            denv[(4 + m) * 64 : (5 + m) * 64, :] += v * (s[2] * yq[m] + p[7] * fq[m])

    over(8, step)
    for c in range(9):
        denv[c * 64 : (c + 1) * 64, :] = slot_total(rows_of(denv, c)) * NORM
    dyv[0:1, :] = jnp.zeros((1, EDGES), F32)
    dyv[...] += dy1[...]
    env_back(geo, vw.at[64:128, :], denv, dvwh.at[64:128, :], dvwl.at[64:128, :], dy, dyv)


def pre_kernel(
    half, qh, ql, wh, wl, veh, vel, dvwh, dvwl, dl, table, cent, geo, rad_w,
    qph, qpl, side, drad, da, db, pre,
):
    base = half * HALF
    wr = slice(base, base + HALF)
    rwh, rwl = split(jnp.concatenate([rad_w[:, wr], jnp.zeros((8, HALF), F32)], 0))
    side[...] = jnp.zeros_like(side)

    def product(i, out):
        cols = pl.ds(i * 256, 256)
        out[...] = dot3(wh[wr, :], wl[wr, :], qh[:, cols], ql[:, cols], 1, 0) + dot3(
            veh[:, wr], vel[:, wr], dvwh[:, cols], dvwl[:, cols], 0, 0
        )

    def step(i, ds):
        cols = pl.ds(i * 256, 256)
        sm = geo[9:10, cols]
        total = jnp.zeros((8, 256), F32)
        pre[...] = dot(table[:, wr], embed_inputs(cent, geo, cols), 0, 0)
        for b in range(4):
            rows = pl.ds(b * 128, 128)
            dd = ds[rows, :] + dl[pl.ds(base + b * 128, 128), cols]
            si, dsi = silu_both(pre[rows, :])
            qph[rows, cols], qpl[rows, cols] = split(dd * dsi * sm)
            total = total + jnp.sum((dd * si).reshape(16, 8, 256), 0)
        side[0:1, cols] = jnp.sum(total, 0, keepdims=True)
        drad[:, cols] = dot3(rwh, rwl, qph[:, cols], qpl[:, cols], 1, 0)[0:8]

    staggered(4, (da, db), product, step)


def last_kernel(
    rows_y, rows_z, place, qps, sides, drads, geo, slots, cent, sl, se, dy,
    dpath, columns, dout, more,
    small_keep, small_send, energy,
    ghost, small, spread,
):
    kinds = iota((NSPEC, EDGES), 0).astype(F32)
    hot_c = jnp.where(kinds == cent[3:4, :], 1.0, 0.0)
    hot_n = jnp.where(kinds == geo[25:26, :], 1.0, 0.0)
    hots = jnp.concatenate([hot_c, hot_n], 0).astype(BF16)
    rad = geo[16:24, :]
    rad_h = rad.astype(BF16).astype(F32)
    rads = jnp.concatenate([rad_h, rad - rad_h], 0).astype(BF16)
    left = jnp.concatenate([hots, rads], 0)
    for n, (qh, ql) in enumerate(zip(qps[0::2], qps[1::2])):
        full = dot(left, qh[...], 1, 1)
        rest = dot(left, ql[...], 1, 1)
        part = slice(n * HALF, (n + 1) * HALF)
        small[0:128, part] = full[0:128] + rest[0:128]
        small[128:136, part] = full[128:136] + full[136:144] + rest[128:136]

    live, r, smooth = geo[10:11, :], geo[11:12, :], geo[9:10, :]
    inv = 1.0 / r
    grad = geo[15:16, :]
    reach = sl[0:1, :]
    lat_out = sl[1:2, :]
    order = (iota((8, EDGES), 0) + 1).astype(F32) * (math.pi / CUTOFF)
    angle = order * r
    sine = jnp.sin(angle) * inv
    cosine = jnp.cos(angle) * inv
    dr8 = drads[0][...] + drads[1][...]
    d_s = (
        grad * lat_out
        + grad * smooth * RH * reach
        + se[0:1, :]
        + sides[0][0:1, :]
        + sides[1][0:1, :]
        + BESSEL * jnp.sum(dr8 * sine, 0, keepdims=True)
    )
    t = r / CUTOFF
    t2 = t * t
    gap = 1.0 - t
    d_r = d_s * (live * (-168.0 / CUTOFF) * (t2 * t2 * t) * (gap * gap)) + (
        smooth * BESSEL
    ) * jnp.sum(dr8 * (order * cosine - sine * inv), 0, keepdims=True)
    ux, uy, uz = geo[12:13, :] * inv, geo[13:14, :] * inv, geo[14:15, :] * inv
    yy = [dy[c : c + 1, :] for c in range(9)]
    h2, s2 = 2.0 * HR * Q75, 2.0 * SR * Q75
    gx = R3 * yy[1] + ux * (h2 * yy[4] + s2 * yy[5]) + h2 * (uy * yy[6] + uz * yy[7])
    gy = R3 * yy[2] + uy * (s2 * yy[5] - h2 * yy[4]) + h2 * (ux * yy[6] + uz * yy[8])
    gz = R3 * yy[3] - 2.0 * s2 * uz * yy[5] + h2 * (ux * yy[7] + uy * yy[8])
    along = ux * gx + uy * gy + uz * gz
    zero = jnp.zeros((5, EDGES), F32)
    disp = jnp.concatenate(
        [
            live * ((gx - ux * along) * inv + ux * d_r),
            live * ((gy - uy * along) * inv + uy * d_r),
            live * ((gz - uz * along) * inv + uz * d_r),
            zero,
        ],
        0,
    )
    hi, mid, lo = pieces(disp)
    disp24 = jnp.concatenate([hi, mid, lo], 0).astype(BF16)
    acc = None
    mine = None
    for k in range(8):
        term = disp[:, k * 128 : (k + 1) * 128]
        mine = term if mine is None else mine + term
    mine = slot_total(mine)
    for i in range(4):
        cols = pl.ds(i * 256, 256)
        hot = jnp.where(iota((NTAB, 256), 0) == slots[:, cols], 1.0, 0.0).astype(BF16)
        term = dot(disp24[:, i * 256 : (i + 1) * 256], hot, 1, 1)
        acc = term if acc is None else acc + term
    ghost[...] = acc[0:8] + acc[8:16] + acc[16:24]
    lane = iota((8, 128), 1)
    middle = ghost[:, 512:640] - jnp.where(
        (lane >= ATOMS) & (lane < 2 * ATOMS), pltpu.roll(mine, ATOMS, 1), 0.0
    )
    ghost[:, 512:640] = middle
    atoms = spread.shape[1]
    spread[...] = jnp.zeros_like(spread)
    total = jnp.zeros_like(spread)
    for bx in range(3):
        for by in range(3):
            block = 3 * bx + by
            spread[:, 0:128] = ghost[:, block * 128 : (block + 1) * 128]
            start = place[4] + ((bx - 1) * rows_y + by - 1) * rows_z * ATOMS - ATOMS
            total = total + pltpu.roll(spread[...], lax.rem(start + 2 * atoms, atoms), 1)
    for n in range(atoms // LATENT):
        small[144 + 8 * n : 152 + 8 * n, :] = total[:, n * LATENT : (n + 1) * LATENT]

    edge_energy = smooth * lat_out
    total = None
    for k in range(8):
        term = edge_energy[:, k * 128 : (k + 1) * 128]
        total = term if total is None else total + term
    total = slot_total(jnp.broadcast_to(total, (8, 128)))[0:1]
    hot = jnp.where(iota((NSPEC, 128), 0).astype(F32) == cent[3:4, 0:128], 1.0, 0.0)
    energy[...] = jnp.broadcast_to(
        jnp.sum(hot * columns[0:64, 8:9], 0, keepdims=True) * total
        + jnp.sum(hot * columns[0:64, 9:10], 0, keepdims=True),
        energy.shape,
    )
    cot = cent[4:5, 0:128] * jnp.where(iota((1, 128), 1) < ATOMS, 1.0, 0.0)
    stack = jnp.concatenate(
        [dpath[...], hot * (cot * total), hot * cot, jnp.zeros((64, 128), F32)], 0
    )
    row = jnp.sum(stack.T, 0, keepdims=True)
    small[136:144, :] = jnp.zeros((8, LATENT), F32)
    small[136:137, 0:768] = row
    small[137:138, :] = dout[0:1, :]
    mine = pl.ds(pl.multiple_of(place[3] * HALF, HALF), HALF)
    other = pl.ds(pl.multiple_of((1 - place[3]) * HALF, HALF), HALF)
    for out, cols in ((small_keep, mine), (small_send, other)):
        out[0:192, :] = more[:, cols]
        out[192:, :] = small[:, cols]


def weights_kernel(dvwh, dvwl, x0h, x0l, dw1h, dw1l, x1h, x1l, out):
    out[0:128, :] = dot3(dvwh[...], dvwl[...], x0h[0:LATENT, :], x0l[0:LATENT, :], 1, 1)
    out[128:192, :] = dot3(dw1h[...], dw1l[...], x1h[0:LATENT, :], x1l[0:LATENT, :], 1, 1)


def halves(shape, dim):
    rows, cols = shape
    return (rows // 2, cols) if dim == 0 else (rows, cols // 2) if dim == 1 else shape


def half_of(shape, dim, bit):
    rows, cols = shape
    if dim == 0:
        rows //= 2
        return pl.ds(pl.multiple_of(bit * rows, 8), rows), slice(None)
    cols //= 2
    return slice(None), pl.ds(pl.multiple_of(bit * cols, 128), cols)


def down_kernel(dim, flag, place, keep, got, *outs):
    if dim is None:
        outs[0][...] = keep[...] + got[...]
        return
    for out, bit in zip(outs, (1 - place[flag], place[flag])):
        index = half_of(keep.shape, dim, bit)
        out[...] = keep[index] + got[index]


def up_kernel(dim, flag, place, mine, got, out):
    out[half_of(out.shape, dim, place[flag])] = mine[...]
    out[half_of(out.shape, dim, 1 - place[flag])] = got[...]


def end_kernel(parts, place, *refs):
    srcs, out, sem = refs[: len(parts)], refs[-2], refs[-1]
    copies = []
    for n, ((layer, start, mine), src) in enumerate(zip(parts, srcs)):
        block = place[3] if mine else 1 - place[3]
        cols = pl.ds(pl.multiple_of(block * HALF, HALF), HALF)
        rows = pl.ds(start, src.shape[0])
        copies.append(pltpu.make_async_copy(src, out.at[layer, rows, cols], sem.at[n]))
    for copy in copies:
        copy.start()
    for copy in copies:
        copy.wait()


def small_end_kernel(
    core_at, place, mine, got, energy,
    center, neigh, radial, value, env, path, out, scale, shift, grad, energies,
):
    for src, b in ((mine, place[core_at]), (got, 1 - place[core_at])):
        cols = pl.ds(pl.multiple_of(b * HALF, HALF), HALF)
        value[:, cols] = src[0:64, :]
        env[0, :, cols] = src[64:128, :]
        env[1, :, cols] = src[128:192, :]
        center[:, cols] = src[192:256, :]
        neigh[:, cols] = src[256:320, :]
        radial[:, cols] = src[320:328, :]
    is_first = place[core_at] == 0

    def whole(rows):
        first = jnp.where(is_first, mine[rows, :], got[rows, :])
        second = jnp.where(is_first, got[rows, :], mine[rows, :])
        return jnp.concatenate([first, second], 1)

    base = 336 + 8 * (place[4] // LATENT)
    spread = whole(pl.ds(pl.multiple_of(base, 8), 8))
    shift_by = LATENT - lax.rem(place[4], LATENT)
    grad[...] = pltpu.roll(spread, lax.rem(shift_by, LATENT), 1)[0:3, 0:ATOMS]
    energies[...] = energy[0:1, 0:ATOMS]
    row = whole(slice(328, 336))
    for n in range(9):
        path[n : n + 1, :] = row[0:1, n * 64 : (n + 1) * 64]
    scale[...] = row[0:1, 576:640]
    shift[...] = row[0:1, 640:704]
    for n in range(8):
        out[n : n + 1, :] = row[1:2, n * 128 : (n + 1) * 128]


VSPEC = pl.BlockSpec(memory_space=pltpu.VMEM)
SSPEC = pl.BlockSpec(memory_space=pltpu.SMEM)
ASPEC = pl.BlockSpec(memory_space=pl.ANY)
HSPEC = pl.BlockSpec(memory_space=pltpu.HBM)


class Order:
    def __init__(self):
        self.token = None
        self.free = False

    def __call__(
        self, body, outs, args, scratch=(), scalar=False, hbm=(), plain=False, alias=None, us=1,
        limit=6, name=None,
    ):
        specs = [HSPEC if n in hbm else VSPEC for n in range(len(args))]
        if scalar:
            specs[0] = SSPEC
        count, given = len(args), len(outs)
        tokens = () if self.token is None or self.free else (self.token,)

        def kernel(*refs):
            after = refs[count + len(tokens) :]
            if self.free:
                return body(*refs[:count], *after)
            after[given][...] = jnp.zeros((8, 128), F32)
            body(*refs[:count], *after[:given], *after[given + 1 :])

        if plain:
            shapes = [jax.ShapeDtypeStruct(shape, dtype) for shape, dtype in outs]
        else:
            shapes = [pltpu.VMEM(shape, dtype) for shape, dtype in outs]
        out_spec = HSPEC if plain == "hbm" else VSPEC
        got = pl.pallas_call(
            kernel,
            name=name or getattr(body, "func", body).__name__,
            out_shape=shapes + ([] if self.free else [pltpu.VMEM((8, 128), F32)]),
            in_specs=specs + [ASPEC] * len(tokens),
            out_specs=[out_spec] * given + ([] if self.free else [VSPEC]),
            scratch_shapes=list(scratch),
            input_output_aliases=alias or {},
            compiler_params=pltpu.CompilerParams(vmem_limit_bytes=limit << 20),
            cost_estimate=pl.CostEstimate(
                flops=int(us * 3e9), bytes_accessed=1 << 20, transcendentals=0
            ),
        )(*args, *tokens)
        if self.free:
            return got
        self.token = got[-1]
        return got[:-1]


def is_up(axis, bit):
    return (lax.axis_index(axis) // bit) & 1


def even_pairs(axis):
    return [(i, i ^ 1) for i in range(lax.axis_size(axis))]


def odd_pairs(axis):
    count = lax.axis_size(axis)
    return [p for i in range(1, count - 1, 2) for p in ((i, i + 1), (i + 1, i))]


def neighbours_of(axis, even, odd):
    pairs = odd_pairs(axis)
    return (
        lax.ppermute(even, axis, even_pairs(axis)),
        lax.ppermute(odd, axis, pairs) if pairs else jnp.zeros_like(odd),
    )


class Route:
    def __init__(self, mesh_sizes, base, tall_first=False):
        sizes = dict(mesh_sizes)
        names = list(sizes)

        def bits(axis, least=1):
            return [(axis, 1 << n) for n in range(20) if least <= 1 << n < sizes[axis]]

        flat, tall = bits("gx"), bits("gy") + bits("gz", 2)
        first = [("gz", 1)]
        one, two = (flat, tall), (flat[::-1], tall[::-1])
        if tall_first:
            one, two = one[::-1], two[::-1]
        self.steps = list(zip(first + one[0] + one[1], first + two[0] + two[1]))
        self.count = len(self.steps)
        self.base = base
        self.names = tuple(names)
        coords = [()]
        for name in names:
            coords = [c + (i,) for c in coords for i in range(sizes[name])]
        index = {c: n for n, c in enumerate(coords)}
        self.pairs = []
        for step in self.steps:
            pairs = []
            for c in coords:
                axis, bit = step[c[names.index("gz")] & 1]
                at = names.index(axis)
                pairs.append((index[c], index[c[:at] + (c[at] ^ bit,) + c[at + 1 :]]))
            self.pairs.append(pairs)

    def flags(self):
        core = is_up("gz", 1)
        return [jnp.where(core == 1, is_up(*two), is_up(*one)) for one, two in self.steps]

    def swap(self, x, at):
        return lax.ppermute(x, self.names, self.pairs[at])


class Sum:
    def __init__(self, name, order, place, route, send, dims):
        self.name = name
        self.order, self.place, self.route = order, place, route
        self.dims = (1,) + dims + (None,) * (route.count - 1 - len(dims))
        self.keep, self.send = None, send
        self.at, self.rising = 0, False
        self.shapes = []
        self.launch()

    def launch(self):
        with jax.named_scope(f"sum_{self.name}_{'up' if self.rising else 'down'}_{self.at}"):
            self.got = self.route.swap(self.send, self.at)

    @property
    def over(self):
        return self.rising and self.at == 0

    def land(self):
        (self.climb if self.rising else self.descend)()
        self.launch()

    def call(self, body, dim, flag, shapes, args):
        return self.order(
            functools.partial(body, dim, flag),
            [(shape, F32) for shape in shapes],
            (self.place, *args),
            scalar=True,
            us=2,
            name=f"land_{self.name}_{'up' if self.rising else 'down'}_{self.at}",
        )

    def descend(self):
        self.shapes.append(self.keep.shape)
        self.at += 1
        last = self.at == self.route.count
        dim = None if last else self.dims[self.at]
        shapes = [halves(self.keep.shape, dim)] * (1 if dim is None else 2)
        outs = self.call(
            down_kernel, dim, self.route.base + self.at, shapes, (self.keep, self.got)
        )
        self.send, self.keep = outs[0], outs[-1]
        if last:
            self.rising = True
            self.rise()

    def rise(self):
        self.at -= 1
        while self.at > 0 and self.dims[self.at] is None:
            self.at -= 1

    def climb(self):
        (self.send,) = self.call(
            up_kernel,
            self.dims[self.at],
            self.route.base + self.at,
            [self.shapes[self.at - 1]],
            (self.send, self.got),
        )
        self.rise()


def per_device(
    positions,
    species,
    neighbours,
    embed_center,
    embed_neigh,
    embed_radial,
    value_proj,
    env_weight,
    latent_weight,
    path_weight,
    out_weight,
    scale_table,
    shift_table,
    cotangent,
):
    vm, sem = pltpu.VMEM, pltpu.SemaphoreType
    order = Order()
    sizes = [(axis, lax.axis_size(axis)) for axis in ("gx", "gy", "gz")]
    route = Route(sizes, 5)
    steep = Route(sizes, 5 + route.count, tall_first=True)
    first_atom = lax.axis_index(("gx", "gy", "gz")) * ATOMS
    place = [is_up("gz", 1), is_up("gy", 1), is_up("gx", 1), is_up("gz", 1), first_atom]
    place = jnp.stack(place + route.flags() + steep.flags()).astype(jnp.int32)
    spec_row = species.reshape(1, ATOMS)

    (table,) = order(pack_kernel, [((8, 128), F32)], (positions, spec_row), us=0.3)
    even, odd = neighbours_of("gz", table, table)
    (table,) = order(
        join_z_kernel, [((8, 128), F32)], (place, table, even, odd), scalar=True, us=0.3
    )
    even, odd = neighbours_of("gy", table, table)
    (table,) = order(
        join_y_kernel,
        [((8, 384), F32)],
        (place, table, even, odd),
        scalar=True,
        us=0.3,
    )
    even, odd = neighbours_of("gx", table, table)

    wide = ((WIDE, EDGES), BF16)
    half = ((HALF, EDGES), BF16)
    row64 = ((64, LATENT), BF16)
    row128 = ((128, LATENT), BF16)
    w0h, w0l, w1h, w1l, hots, veh, vel, evh, evl, path, columns, slots, cent, rad_w = order(
        prep_kernel,
        [
            wide, wide, wide, wide, ((288, LATENT), BF16), row128, row128, row64, row64,
            ((576, 128), F32), ((128, 128), F32), ((1, EDGES), jnp.int32), ((8, EDGES), F32),
            ((8, LATENT), F32),
        ],
        (latent_weight, embed_center, embed_neigh, embed_radial, value_proj.T,
         jnp.swapaxes(env_weight, 1, 2), neighbours, positions, spec_row,
         cotangent.reshape(1, ATOMS), path_weight, out_weight.reshape(8, 128),
         scale_table.reshape(1, NSPEC), shift_table.reshape(1, NSPEC)),
        [
            vm((NSPEC, LATENT), F32), vm((NSPEC, LATENT), F32), vm((CHANNELS, LATENT), F32),
            vm((2, CHANNELS, LATENT), F32), vm((NB, ATOMS), jnp.int32), vm((3, ATOMS), F32),
            vm((1, ATOMS), jnp.int32), vm((1, ATOMS), F32), vm((9, CHANNELS), F32),
            vm((8, 128), F32), vm((1, NSPEC), F32), vm((1, NSPEC), F32), vm((128, 128), F32),
            sem.DMA((13,)),
        ],
        hbm=range(1, 14),
        us=4,
    )

    x0h, x0l, x1h, x1l, z0, vw, w1, geo, g0, g1, f1 = order(
        fwd_kernel,
        [
            wide, wide, wide, wide,
            ((LATENT, EDGES), F32), ((128, EDGES), F32), ((64, EDGES), F32), ((G_ROWS, EDGES), F32), ((576, 128), F32), ((576, 128), F32),
            ((576, EDGES), F32),
        ],
        (place, table, even, odd, slots, cent, w0h, w0l, hots, veh, vel, evh, evl, path, columns),
        [vm((8, EDGES), F32), vm((LATENT, 256), F32), vm((LATENT, 256), F32)],
        scalar=True,
        us=22,
        limit=18,
    )

    chains = {}

    def grad(mine, xh, xl, qh, ql):
        return order(
            functools.partial(grad_kernel, mine),
            [((WIDE, HALF), F32)],
            (place, xh, xl, qh, ql),
            scalar=True,
            us=4.6,
        )[0]

    def send(name, *args):
        chains[name] = Sum(name, order, place, route, grad(False, *args), (0, 0, 0, 1))

    def keep(name, *args):
        chains[name].keep = grad(True, *args)

    def late():
        return order(
            late_kernel,
            [
                ((LATENT, EDGES), BF16), ((LATENT, EDGES), BF16), ((8, EDGES), F32),
                ((8, LATENT), F32),
            ],
            (x1h, x1l, w1h, w1l, columns, geo),
            [vm((LATENT, 128), F32), vm((LATENT, 256), F32), vm((LATENT, 256), F32)],
            us=13,
            limit=17,
        )

    def mid():
        return order(
            mid_kernel,
            [((192, EDGES), F32), ((64, EDGES), BF16), ((64, EDGES), BF16), ((16, EDGES), F32)],
            (q1h, q1l, w1h, w1l, f1, g1, w1, geo),
            [vm((576, 128), F32)],
            us=3,
        )

    def early():
        return order(
            early_kernel,
            [
                ((LATENT, EDGES), F32), ((LATENT, EDGES), BF16), ((LATENT, EDGES), BF16),
                ((8, EDGES), F32),
            ],
            (q1h, q1l, w1h, w1l, evh, evl, dw1h, dw1l, columns, geo, z0),
            [vm((LATENT, 256), F32), vm((LATENT, 256), F32)],
            us=10,
            limit=12,
        )

    def couple():
        return order(
            couple_kernel,
            [
                ((128, EDGES), BF16), ((128, EDGES), BF16), ((16, EDGES), F32),
                ((576, 128), F32),
            ],
            (q0h, q0l, w0h, w0l, vw, geo, g0, g1, ds1, path, dy1),
            [vm((192, EDGES), F32), vm((576, 128), F32), vm((16, EDGES), F32)],
            us=6.3,
        )

    def before(h):
        return order(
            functools.partial(pre_kernel, h),
            [half, half, ((8, EDGES), F32), ((8, EDGES), F32)],
            (q0h, q0l, w0h, w0l, veh, vel, dvwh, dvwl, dlat, hots, cent, geo, rad_w),
            [vm((HALF, 256), F32), vm((HALF, 256), F32), vm((HALF, 256), F32)],
            us=7,
        )

    def land(names):
        for name in names.split():
            if not chains[name].over:
                chains[name].land()

    q1h, q1l, sl, dout = late()
    send("a", x1h, x1l, q1h, q1l)
    keep("a", x1h, x1l, q1h, q1l)
    ds1, dw1h, dw1l, dy1 = mid()
    land("a")
    dlat, q0h, q0l, se = early()
    send("c", x0h, x0l, q0h, q0l)
    land("a")
    keep("c", x0h, x0l, q0h, q0l)
    land("c a")
    dvwh, dvwl, dy, dpath = couple()
    land("a")
    (more,) = order(
        weights_kernel, [((192, LATENT), F32)], (dvwh, dvwl, x0h, x0l, dw1h, dw1l, x1h, x1l), us=4
    )
    pres = [before(0)]
    land("c a")
    pres.append(before(1))
    land("c")
    atoms = ATOMS * math.prod(size for _, size in sizes)
    height = 144 + 8 * (atoms // LATENT)
    qps = [x for got in pres for x in got[0:2]]
    small_keep, small_send, energy = order(
        lambda place, *refs: last_kernel(
            sizes[1][1], sizes[2][1], place, refs[0:4], refs[4:6], refs[6:8], *refs[8:]
        ),
        [((192 + height, HALF), F32), ((192 + height, HALF), F32), ((8, 128), F32)],
        (place, *qps, *[got[2] for got in pres], *[got[3] for got in pres], geo, slots, cent, sl,
         se, dy, dpath, columns, dout, more),
        [vm((8, NTAB), F32), vm((height, LATENT), F32), vm((8, atoms), F32)],
        scalar=True,
        us=5,
        name="last_kernel",
    )
    chains["s"] = s = Sum("s", order, place, route, small_send, (1, 1))
    s.keep = small_keep
    land("c s a")
    order.free = True
    land("s c a c s a s c s c s a s a")
    a, c = chains["a"], chains["c"]
    while not (a.over and s.over):
        for chain in (a, s):
            if not chain.over:
                chain.land()

    def finish(parts, arrays, done=()):
        last = 1 + len(arrays)
        return order(
            functools.partial(end_kernel, parts),
            [((2, WIDE, LATENT), F32)],
            (place, *arrays, *done),
            [sem.DMA((len(parts),))],
            scalar=True,
            hbm=(last,) if done else (),
            plain="hbm",
            alias={last: 0} if done else None,
            us=3,
        )

    d_latent = finish(((1, 0, True), (1, 0, False)), (a.send, a.got))
    center, neigh, radial, value, env, path_grad, out, scale, shift, position_grad, energies = order(
        functools.partial(small_end_kernel, 3),
        [
            ((NSPEC, LATENT), F32), ((NSPEC, LATENT), F32), ((NBESSEL, LATENT), F32),
            ((CHANNELS, LATENT), F32), ((2, CHANNELS, LATENT), F32), ((9, CHANNELS), F32),
            ((8, 128), F32), ((1, NSPEC), F32), ((1, NSPEC), F32), ((3, ATOMS), F32),
            ((1, ATOMS), F32),
        ],
        (place, s.send, s.got, energy),
        scalar=True,
        plain=True,
        us=2,
    )
    while not c.over:
        c.land()
    d_latent = finish(((0, 0, True),), (c.send,), tuple(d_latent))
    (d_latent,) = finish(((0, 0, False),), (c.got,), tuple(d_latent))
    return (
        energies.reshape(ATOMS),
        position_grad,
        center,
        neigh,
        radial,
        value.T,
        jnp.swapaxes(env, 1, 2),
        d_latent,
        path_grad,
        out.reshape(LATENT),
        scale.reshape(NSPEC),
        shift.reshape(NSPEC),
    )


def solution(mesh):
    everything = ("gx", "gy", "gz")
    return jax.shard_map(
        per_device,
        mesh=mesh,
        in_specs=(
            P(None, everything),
            P(everything),
            P(None, everything),
            P(),
            P(),
            P(),
            P(),
            P(),
            P(),
            P(),
            P(),
            P(),
            P(),
            P(everything),
        ),
        out_specs=(
            P(everything),
            P(None, everything),
            P(),
            P(),
            P(),
            P(),
            P(),
            P(),
            P(),
            P(),
            P(),
            P(),
        ),
        check_vma=False,
    )
```

```python
import functools
import math
import types

import jax
import jax.numpy as jnp
import numpy as np
from jax import lax
from jax.experimental import pallas as pl
from jax.experimental.pallas import tpu as pltpu
from jax.sharding import PartitionSpec as P

LATENT = 1024
CHANNELS = 64
NSPEC = 64
NBESSEL = 8
NB = 32
ATOMS = 32
EDGES = NB * ATOMS
WIDE = LATENT + 3 * CHANNELS
HALF = LATENT // 2
QUARTER = LATENT // 4
NTAB = 9 * 128
OWN = 4 * 128 + ATOMS

CUTOFF = 5.0
RH = 0.7071067811865476
HR = 0.7071067811865476
SR = 0.4082482904638631
R3 = math.sqrt(3.0)
Q75 = math.sqrt(7.5)
NORM = NB**-0.5
BESSEL = math.sqrt(2.0 / CUTOFF)

F32 = jnp.float32
BF16 = jnp.bfloat16

G_SMOOTH, G_LIVE, G_R, G_DISP, G_GRAD, G_RAD, G_GS, G_SPEC = 9, 10, 11, 12, 15, 16, 24, 25
G_ROWS = 32


def dot(a, b, ca, cb):
    return lax.dot_general(a, b, (((ca,), (cb,)), ((), ())), preferred_element_type=F32)


def dot3(ah, al, bh, bl, ca, cb):
    return dot(ah, bh, ca, cb) + dot(ah, bl, ca, cb) + dot(al, bh, ca, cb)


def split(x):
    hi = x.astype(BF16)
    return hi, (x - hi.astype(F32)).astype(BF16)


def pieces(x):
    hi = x.astype(BF16).astype(F32)
    rest = x - hi
    mid = rest.astype(BF16).astype(F32)
    return hi, mid, rest - mid


def sigmoid(x):
    return 0.5 * jnp.tanh(0.5 * x) + 0.5


def silu_both(x):
    sig = sigmoid(x)
    return x * sig, sig * (1.0 + x * (1.0 - sig))


def lanes(i, width):
    return pl.ds(pl.multiple_of(i * width, width), width)


def over(count, body):
    def step(i, carry):
        body(i)
        return carry

    lax.fori_loop(0, count, step, 0)


def staggered(count, bufs, first, second):
    first(0, bufs[0])
    for i in range(count):
        if i + 1 < count:
            first(i + 1, bufs[(i + 1) % 2])
        second(i, bufs[i % 2])


def iota(shape, dim):
    return lax.broadcasted_iota(jnp.int32, shape, dim)


def slot_total(x):
    x = x + pltpu.roll(x, 64, 1)
    return x + pltpu.roll(x, 32, 1)


def make_env(geo, w, env):
    for c in range(9):
        acc = None
        for k in range(8):
            cols = pl.ds(k * 128, 128)
            term = w[:, cols] if c == 0 else geo[c : c + 1, cols] * w[:, cols]
            acc = term if acc is None else acc + term
        env[c * 64 : (c + 1) * 64, :] = slot_total(acc) * NORM


def rows_of(ref, c, cols=slice(None)):
    return ref[c * 64 : (c + 1) * 64, cols]


def pack_kernel(pos, spec, out):
    out[...] = jnp.zeros_like(out)
    out[0:3, 0:ATOMS] = pos[...]
    out[3:4, 0:ATOMS] = spec[...].astype(F32)


def join_z_kernel(place, own, even_in, odd_in, out):
    is_odd = place[0] == 1
    left = jnp.where(is_odd, even_in[...], odd_in[...])
    right = jnp.where(is_odd, odd_in[...], even_in[...])
    out[...] = left + pltpu.roll(own[...], ATOMS, 1) + pltpu.roll(right, 2 * ATOMS, 1)


def join_y_kernel(place, own, even_in, odd_in, out):
    is_odd = place[1] == 1
    out[:, 0:128] = jnp.where(is_odd, even_in[...], odd_in[...])
    out[:, 128:256] = own[...]
    out[:, 256:384] = jnp.where(is_odd, odd_in[...], even_in[...])


def prep_kernel(
    w, ec_in, en_in, rad_in, vp_in, env_in, neigh_in, pos_in, spec_in, cot_in, path_in, outw_in,
    scale_in, shift_in,
    w0h, w0l, w1h, w1l, table, veh, vel, evh, evl, path_b, cols, slots, cent, rad_w,
    ec, en, vp, env, neigh, pos, spec, cot, path, outw, scale, shift, square, sem,
):
    pairs = (
        (ec_in, ec), (en_in, en), (rad_in, rad_w), (vp_in, vp), (env_in, env), (neigh_in, neigh),
        (pos_in, pos), (spec_in, spec), (cot_in, cot), (path_in, path), (outw_in, outw),
        (scale_in, scale), (shift_in, shift),
    )
    copies = [
        pltpu.make_async_copy(src, dst, sem.at[n]) for n, (src, dst) in enumerate(pairs)
    ]
    for copy in copies:
        copy.start()

    for layer, (hi, lo) in enumerate(((w0h, w0l), (w1h, w1l))):

        def part(i, layer=layer, hi=hi, lo=lo):
            rows = pl.ds(pl.multiple_of(i * 64, 64), 64)
            hi[rows, :], lo[rows, :] = split(w[layer, rows, :])

        over(WIDE // 64, part)
    for copy in copies:
        copy.wait()

    ech, ecl = split(ec[...])
    enh, enl = split(en[...])
    rh = rad_w[...].astype(BF16).astype(F32)
    rl = rad_w[...] - rh
    table[0:64, :] = ech
    table[64:128, :] = enh
    table[128:192, :] = ecl
    table[192:256, :] = enl
    table[256:288, :] = jnp.concatenate([rh, rl, rh, jnp.zeros_like(rh)], 0).astype(BF16)
    veh[0:64, :], vel[0:64, :] = split(vp[...])
    veh[64:128, :], vel[64:128, :] = split(env[0])
    evh[...], evl[...] = split(env[1])

    square[...] = jnp.zeros_like(square)
    square[0:8, :] = outw[...]
    square[8:9, 0:64] = scale[...]
    square[9:10, 0:64] = shift[...]
    square[16:25, 0:64] = path[...]
    turned = square[...].T
    cols[...] = turned
    for n in range(9):
        path_b[n * 64 : (n + 1) * 64, :] = jnp.broadcast_to(
            turned[0:64, 16 + n : 17 + n], (64, 128)
        )

    square[0:32, :] = jnp.zeros((32, 128), F32)
    square[0:32, 0:ATOMS] = neigh[...].astype(F32)
    row = square[pl.ds(0, 8, 4), :]
    for i in range(1, 4):
        row = row + pltpu.roll(square[pl.ds(i, 8, 4), :], i * ATOMS, 1)
    padded = row
    for m in range(1, 9):
        padded = padded + jnp.where(row >= 96.0 * m, 32.0, 0.0)
    padded = padded.astype(jnp.int32)
    square[0:8, :] = jnp.zeros((8, 128), F32)
    square[0:3, 0:ATOMS] = pos[...]
    square[3:4, 0:ATOMS] = spec[...].astype(F32)
    square[4:5, 0:ATOMS] = cot[...]
    own = square[0:8, :]
    own = own + pltpu.roll(own, 32, 1)
    own = own + pltpu.roll(own, 64, 1)
    for k in range(8):
        slots[:, k * 128 : (k + 1) * 128] = padded[k : k + 1]
        cent[:, k * 128 : (k + 1) * 128] = own


def embed_inputs(cent, geo, cols):
    kinds = iota((NSPEC, 256), 0).astype(F32)
    hot_c = jnp.where(kinds == cent[3:4, cols], 1.0, 0.0)
    hot_n = jnp.where(kinds == geo[25:26, cols], 1.0, 0.0)
    hots = jnp.concatenate([hot_c, hot_n], 0).astype(BF16)
    rad = geo[16:24, cols]
    rad_h = rad.astype(BF16).astype(F32)
    rads = jnp.concatenate([rad_h, rad_h, rad - rad_h, jnp.zeros_like(rad)], 0).astype(BF16)
    return jnp.concatenate([hots, hots, rads], 0)


def fwd_kernel(
    place, tab, even_in, odd_in, slots, cent, w0h, w0l, table, veh, vel, evh, evl, path, columns,
    x0h, x0l, x1h, x1l, z0, vw, w1, geo, g0, g1, f1,
    gat, za, zb,
):
    is_odd = place[2] == 1
    whole = jnp.concatenate(
        [
            jnp.where(is_odd, even_in[...], odd_in[...]),
            tab[...],
            jnp.where(is_odd, odd_in[...], even_in[...]),
        ],
        1,
    )
    hi, mid, lo = pieces(whole)
    tab24 = jnp.concatenate([hi, mid, lo], 0).astype(BF16)

    def gather(i):
        cols = lanes(i, 256)
        hot = jnp.where(iota((NTAB, 256), 0) == slots[:, cols], 1.0, 0.0).astype(BF16)
        got = dot(tab24, hot, 1, 0)
        gat[:, cols] = got[0:8] + got[8:16] + got[16:24]

    over(4, gather)

    live = jnp.where(slots[...] != OWN + iota((1, EDGES), 1) % ATOMS, 1.0, 0.0)
    dead = 1.0 - live
    dx = (gat[0:1, :] - cent[0:1, :]) * live + dead * 2.5
    dy = (gat[1:2, :] - cent[1:2, :]) * live
    dz = (gat[2:3, :] - cent[2:3, :]) * live
    r = jnp.sqrt(dx * dx + dy * dy + dz * dz)
    inv = 1.0 / r
    t = r / CUTOFF
    t2 = t * t
    t6 = t2 * t2 * t2
    smooth = live * (1.0 - 28.0 * t6 + 48.0 * t6 * t - 21.0 * t6 * t * t)
    ux, uy, uz = dx * inv, dy * inv, dz * inv
    geo[0:1, :] = jnp.ones_like(r)
    geo[1:2, :] = R3 * ux
    geo[2:3, :] = R3 * uy
    geo[3:4, :] = R3 * uz
    geo[4:5, :] = Q75 * HR * (ux * ux - uy * uy)
    geo[5:6, :] = Q75 * SR * (ux * ux + uy * uy - 2.0 * uz * uz)
    geo[6:7, :] = Q75 * 2.0 * HR * (ux * uy)
    geo[7:8, :] = Q75 * 2.0 * HR * (ux * uz)
    geo[8:9, :] = Q75 * 2.0 * HR * (uy * uz)
    geo[9:10, :] = smooth
    geo[10:11, :] = live
    geo[11:12, :] = r
    geo[12:13, :] = dx
    geo[13:14, :] = dy
    geo[14:15, :] = dz
    order = (iota((8, EDGES), 0) + 1).astype(F32) * (math.pi / CUTOFF)
    geo[16:24, :] = smooth * BESSEL * jnp.sin(order * r) * inv
    hot_c = jnp.where(iota((NSPEC, EDGES), 0).astype(F32) == cent[3:4, :], 1.0, 0.0)
    grad = cent[4:5, :] * jnp.sum(hot_c * columns[0:64, 8:9], 0, keepdims=True)
    geo[15:16, :] = grad
    geo[24:25, :] = grad * smooth
    geo[25:26, :] = gat[3:4, :]
    geo[26:32, :] = jnp.zeros((6, EDGES), F32)

    def embed_product(i, out):
        cols = pl.ds(i * 256, 256)
        out[...] = dot(table[...], embed_inputs(cent, geo, cols), 0, 0)

    def embed(i, before):
        cols = pl.ds(i * 256, 256)
        sm = geo[9:10, cols]
        for b in range(8):
            rows = pl.ds(b * 128, 128)
            p = before[rows, :]
            x0h[rows, cols], x0l[rows, cols] = split(p * sigmoid(p) * sm)
        vw[:, cols] = dot3(
            veh[...], vel[...], x0h[0:LATENT, cols], x0l[0:LATENT, cols], 1, 0
        )

    staggered(4, (za, zb), embed_product, embed)
    make_env(geo, vw.at[64:128, :], g0)

    def tensor(k):
        cols = lanes(k, 128)
        v = vw[0:64, cols]
        y = [geo[c : c + 1, cols] for c in range(9)]
        e0 = rows_of(g0, 0)
        e1, e2, e3 = rows_of(g0, 1), rows_of(g0, 2), rows_of(g0, 3)
        a, b, c = y[1] * e1, y[2] * e2, y[3] * e3
        vec = a + b + c
        quad = y[4] * rows_of(g0, 4)
        for m in range(5, 9):
            quad = quad + y[m] * rows_of(g0, m)
        x0h[1024:1088, cols], x0l[1024:1088, cols] = split(v * e0)
        x0h[1088:1152, cols], x0l[1088:1152, cols] = split(v * vec)
        x0h[1152:1216, cols], x0l[1152:1216, cols] = split(v * quad)
        p = [rows_of(path, n) for n in range(9)]
        e12, e13 = y[1] * e2, y[1] * e3
        e21, e23 = y[2] * e1, y[2] * e3
        e31, e32 = y[3] * e1, y[3] * e2
        q00 = HR * y[4] + SR * y[5]
        q11 = SR * y[5] - HR * y[4]
        q22 = -2.0 * SR * y[5]
        q01, q02, q12 = HR * y[6], HR * y[7], HR * y[8]
        f1[0:64, cols] = v * (p[0] * e0 + p[1] * vec)
        p3g = p[3] * e0
        f1[64:128, cols] = v * (
            p[2] * e1 + p3g * y[1] + p[4] * (e23 - e32) + p[5] * (q00 * e1 + q01 * e2 + q02 * e3)
        )
        f1[128:192, cols] = v * (
            p[2] * e2 + p3g * y[2] + p[4] * (e31 - e13) + p[5] * (q01 * e1 + q11 * e2 + q12 * e3)
        )
        f1[192:256, cols] = v * (
            p[2] * e3 + p3g * y[3] + p[4] * (e12 - e21) + p[5] * (q02 * e1 + q12 * e2 + q22 * e3)
        )
        p8g = p[8] * e0
        pair = (
            HR * (a - b),
            SR * (a + b - 2.0 * c),
            HR * (e12 + e21),
            HR * (e13 + e31),
            HR * (e23 + e32),
        )
        for m in range(5):
            f1[(4 + m) * 64 : (5 + m) * 64, cols] = v * (
                p[6] * pair[m] + p[7] * rows_of(g0, 4 + m) + p8g * y[4 + m]
            )

    over(8, tensor)

    def layer_product(i, out):
        cols = pl.ds(i * 256, 256)
        out[...] = dot3(w0h[...], w0l[...], x0h[:, cols], x0l[:, cols], 0, 0)

    def layer(i, zs):
        cols = pl.ds(i * 256, 256)
        sm = geo[9:10, cols]
        for b in range(8):
            rows = pl.ds(b * 128, 128)
            z = zs[rows, :]
            z0[rows, cols] = z
            old = x0h[rows, cols].astype(F32) + x0l[rows, cols].astype(F32)
            x1h[rows, cols], x1l[rows, cols] = split((old + sm * (z * sigmoid(z))) * RH)
        w1[:, cols] = dot3(
            evh[...], evl[...], x1h[0:LATENT, cols], x1l[0:LATENT, cols], 1, 0
        )

    staggered(4, (za, zb), layer_product, layer)
    make_env(geo, w1, g1)

    def scalars(k):
        cols = lanes(k, 128)
        s0 = rows_of(f1, 0, cols) * rows_of(g1, 0)
        s1 = rows_of(f1, 1, cols) * rows_of(g1, 1)
        for c in range(2, 4):
            s1 = s1 + rows_of(f1, c, cols) * rows_of(g1, c)
        s2 = rows_of(f1, 4, cols) * rows_of(g1, 4)
        for c in range(5, 9):
            s2 = s2 + rows_of(f1, c, cols) * rows_of(g1, c)
        x1h[1024:1088, cols], x1l[1024:1088, cols] = split(s0)
        x1h[1088:1152, cols], x1l[1088:1152, cols] = split(s1)
        x1h[1152:1216, cols], x1l[1152:1216, cols] = split(s2)

    over(8, scalars)


def grad_kernel(mine, place, xh, xl, qh, ql, out):
    block = place[3] if mine else 1 - place[3]
    for n in range(0, HALF, QUARTER):
        rows = pl.ds(pl.multiple_of(block * HALF, HALF) + n, QUARTER)
        out[:, n : n + QUARTER] = dot3(xh[...], xl[...], qh[rows, :], ql[rows, :], 1, 1)


def late_kernel(x1h, x1l, wh, wl, columns, geo, qh, ql, side, dout, acc, za, zb):
    acc[...] = jnp.zeros_like(acc)
    side[...] = jnp.zeros_like(side)

    def product(i, out):
        cols = pl.ds(i * 256, 256)
        out[...] = dot3(wh[...], wl[...], x1h[:, cols], x1l[:, cols], 0, 0)

    def step(i, zs):
        cols = pl.ds(i * 256, 256)
        sm = geo[9:10, cols]
        gs = geo[24:25, cols]
        scale = gs * sm * RH
        reach = jnp.zeros((8, 256), F32)
        total = jnp.zeros((8, 256), F32)
        for b in range(8):
            rows = pl.ds(b * 128, 128)
            si, dsi = silu_both(zs[rows, :])
            ow = columns[:, b : b + 1]
            qh[rows, cols], ql[rows, cols] = split((ow * scale) * dsi)
            lat = (x1h[rows, cols].astype(F32) + x1l[rows, cols].astype(F32) + sm * si) * RH
            part = gs * lat
            acc[rows, :] += part[:, 0:128] + part[:, 128:256]
            reach = reach + jnp.sum((ow * si).reshape(16, 8, 256), 0)
            total = total + jnp.sum((ow * lat).reshape(16, 8, 256), 0)
        side[0:1, cols] = jnp.sum(reach, 0, keepdims=True)
        side[1:2, cols] = jnp.sum(total, 0, keepdims=True)

    staggered(4, (za, zb), product, step)
    dout[...] = jnp.broadcast_to(jnp.sum(acc[...].T, 0, keepdims=True), dout.shape)


def mid_kernel(qh, ql, wh, wl, f1, g1, w1, geo, ds1, dwh, dwl, dy, denv):
    def scal(i):
        cols = lanes(i, 256)
        ds1[:, cols] = dot3(wh[1024:1216, :], wl[1024:1216, :], qh[:, cols], ql[:, cols], 1, 0)

    over(4, scal)
    for c in range(9):
        kind = 0 if c == 0 else (1 if c < 4 else 2)
        acc = None
        for k in range(8):
            cols = pl.ds(k * 128, 128)
            term = rows_of(ds1, kind, cols) * rows_of(f1, c, cols)
            acc = term if acc is None else acc + term
        denv[c * 64 : (c + 1) * 64, :] = slot_total(acc) * NORM
    env_back(geo, w1, denv, dwh, dwl, dy, None)


def env_back(geo, w, denv, dwh, dwl, dy, more):
    def step(k):
        cols = lanes(k, 128)
        acc = rows_of(denv, 0)
        wk = w[:, cols]
        rows = [jnp.zeros((1, 128), F32)]
        for c in range(1, 9):
            d = rows_of(denv, c)
            acc = acc + geo[c : c + 1, cols] * d
            rows.append(jnp.sum(wk * d, 0, keepdims=True))
        dwh[:, cols], dwl[:, cols] = split(acc)
        for c in range(1, 9):
            if more is None:
                dy[c : c + 1, cols] = rows[c]
            else:
                dy[c : c + 1, cols] = rows[c] + more[c : c + 1, cols]

    over(8, step)


def early_kernel(
    q1h, q1l, wh, wl, evh, evl, dwh, dwl, columns, geo, z0, dlat, qh, ql, side, da, db
):
    side[...] = jnp.zeros_like(side)

    def product(i, out):
        cols = pl.ds(i * 256, 256)
        out[...] = dot3(
            wh[0:LATENT, :], wl[0:LATENT, :], q1h[:, cols], q1l[:, cols], 1, 0
        ) + dot3(evh[...], evl[...], dwh[:, cols], dwl[:, cols], 0, 0)

    def step(i, ds):
        cols = pl.ds(i * 256, 256)
        sm = geo[9:10, cols] * RH
        gs = geo[24:25, cols] * RH
        total = jnp.zeros((8, 256), F32)
        for b in range(8):
            rows = pl.ds(b * 128, 128)
            dl = ds[rows, :] + columns[:, b : b + 1] * gs
            dlat[rows, cols] = dl * RH
            si, dsi = silu_both(z0[rows, cols])
            qh[rows, cols], ql[rows, cols] = split(dl * dsi * sm)
            total = total + jnp.sum((dl * si).reshape(16, 8, 256), 0)
        side[0:1, cols] = jnp.sum(total, 0, keepdims=True) * RH

    staggered(4, (da, db), product, step)


def couple_kernel(
    qh, ql, wh, wl, vw, geo, g0, g1, ds1, path, dy1,
    dvwh, dvwl, dy, dpath,
    ds0, denv, dyv,
):
    def scal(i):
        cols = lanes(i, 256)
        ds0[:, cols] = dot3(wh[1024:1216, :], wl[1024:1216, :], qh[:, cols], ql[:, cols], 1, 0)

    over(4, scal)
    denv[...] = jnp.zeros_like(denv)
    dpath[...] = jnp.zeros_like(dpath)

    def step(k):
        cols = lanes(k, 128)
        v = vw[0:64, cols]
        y = [geo[c : c + 1, cols] for c in range(9)]
        e = [rows_of(g0, c) for c in range(9)]
        p = [rows_of(path, n) for n in range(9)]
        s = [rows_of(ds0, n, cols) for n in range(3)]
        u = [rows_of(ds1, n, cols) for n in range(3)]
        f0 = u[0] * rows_of(g1, 0)
        fv = [u[1] * rows_of(g1, c) for c in range(1, 4)]
        fq = [u[2] * rows_of(g1, c) for c in range(4, 9)]
        yv, yq, ev_, eq = y[1:4], y[4:9], e[1:4], e[4:9]

        def dot_of(a, b):
            out = a[0] * b[0]
            for i in range(1, len(a)):
                out = out + a[i] * b[i]
            return out

        m00 = HR * yq[0] + SR * yq[1]
        m11 = SR * yq[1] - HR * yq[0]
        m22 = -2.0 * SR * yq[1]
        m01, m02, m12 = HR * yq[2], HR * yq[3], HR * yq[4]
        t00 = HR * fq[0] + SR * fq[1]
        t11 = SR * fq[1] - HR * fq[0]
        t22 = (-2.0 * SR) * fq[1]
        t01, t02, t12 = HR * fq[2], HR * fq[3], HR * fq[4]

        te = [
            t00 * ev_[0] + t01 * ev_[1] + t02 * ev_[2],
            t01 * ev_[0] + t11 * ev_[1] + t12 * ev_[2],
            t02 * ev_[0] + t12 * ev_[1] + t22 * ev_[2],
        ]
        ty = [
            t00 * yv[0] + t01 * yv[1] + t02 * yv[2],
            t01 * yv[0] + t11 * yv[1] + t12 * yv[2],
            t02 * yv[0] + t12 * yv[1] + t22 * yv[2],
        ]
        mf = [
            m00 * fv[0] + m01 * fv[1] + m02 * fv[2],
            m01 * fv[0] + m11 * fv[1] + m12 * fv[2],
            m02 * fv[0] + m12 * fv[1] + m22 * fv[2],
        ]
        ef = [
            ev_[1] * fv[2] - ev_[2] * fv[1],
            ev_[2] * fv[0] - ev_[0] * fv[2],
            ev_[0] * fv[1] - ev_[1] * fv[0],
        ]
        fy = [
            fv[1] * yv[2] - fv[2] * yv[1],
            fv[2] * yv[0] - fv[0] * yv[2],
            fv[0] * yv[1] - fv[1] * yv[0],
        ]
        e_fv = dot_of(ev_, fv)
        y_fv = dot_of(yv, fv)
        e_fq = dot_of(eq, fq)
        y_fq = dot_of(yq, fq)
        vec = dot_of(yv, ev_)
        y_te = dot_of(yv, te)
        e_mf = dot_of(ev_, mf)
        y_ef = dot_of(yv, ef)

        grads = (
            e[0] * f0,
            vec * f0,
            e_fv,
            e[0] * y_fv,
            y_ef,
            e_mf,
            y_te,
            e_fq,
            e[0] * y_fq,
        )
        for n in range(9):
            dpath[n * 64 : (n + 1) * 64, :] += v * grads[n]

        p1f = p[1] * f0
        d0 = s[0] * e[0] + p[0] * e[0] * f0 + p[2] * e_fv + p[7] * e_fq
        p3e = p[3] * e[0]
        p8e = p[8] * e[0]
        s1f = s[1] + p1f
        dv = d0
        for i in range(3):
            di = s1f * ev_[i] + p3e * fv[i] + p[4] * ef[i] + p[6] * te[i]
            dv = dv + yv[i] * di
            dyv[1 + i : 2 + i, cols] = jnp.sum(v * di, 0, keepdims=True)
        a, b, c = fv[0] * ev_[0], fv[1] * ev_[1], fv[2] * ev_[2]
        bil = (
            HR * (a - b),
            SR * (a + b - 2.0 * c),
            HR * (fv[0] * ev_[1] + fv[1] * ev_[0]),
            HR * (fv[0] * ev_[2] + fv[2] * ev_[0]),
            HR * (fv[1] * ev_[2] + fv[2] * ev_[1]),
        )
        for m in range(5):
            dm = s[2] * eq[m] + p[5] * bil[m] + p8e * fq[m]
            dv = dv + yq[m] * dm
            dyv[4 + m : 5 + m, cols] = jnp.sum(v * dm, 0, keepdims=True)
        dvwh[0:64, cols], dvwl[0:64, cols] = split(dv)

        denv[0:64, :] += v * (s[0] + p[0] * f0 + p[3] * y_fv + p[8] * y_fq)
        for i in range(3):
            denv[(1 + i) * 64 : (2 + i) * 64, :] += v * (
                s1f * yv[i] + p[2] * fv[i] + p[4] * fy[i] + p[5] * mf[i] + p[6] * ty[i]
            )
        for m in range(5):
            denv[(4 + m) * 64 : (5 + m) * 64, :] += v * (s[2] * yq[m] + p[7] * fq[m])

    over(8, step)
    for c in range(9):
        denv[c * 64 : (c + 1) * 64, :] = slot_total(rows_of(denv, c)) * NORM
    dyv[0:1, :] = jnp.zeros((1, EDGES), F32)
    dyv[...] += dy1[...]
    env_back(geo, vw.at[64:128, :], denv, dvwh.at[64:128, :], dvwl.at[64:128, :], dy, dyv)


def pre_kernel(
    half, qh, ql, wh, wl, veh, vel, dvwh, dvwl, dl, table, cent, geo, rad_w,
    qph, qpl, side, drad, da, db, pre,
):
    base = half * HALF
    wr = slice(base, base + HALF)
    rwh, rwl = split(jnp.concatenate([rad_w[:, wr], jnp.zeros((8, HALF), F32)], 0))
    side[...] = jnp.zeros_like(side)

    def product(i, out):
        cols = pl.ds(i * 256, 256)
        out[...] = dot3(wh[wr, :], wl[wr, :], qh[:, cols], ql[:, cols], 1, 0) + dot3(
            veh[:, wr], vel[:, wr], dvwh[:, cols], dvwl[:, cols], 0, 0
        )

    def step(i, ds):
        cols = pl.ds(i * 256, 256)
        sm = geo[9:10, cols]
        total = jnp.zeros((8, 256), F32)
        pre[...] = dot(table[:, wr], embed_inputs(cent, geo, cols), 0, 0)
        for b in range(4):
            rows = pl.ds(b * 128, 128)
            dd = ds[rows, :] + dl[pl.ds(base + b * 128, 128), cols]
            si, dsi = silu_both(pre[rows, :])
            qph[rows, cols], qpl[rows, cols] = split(dd * dsi * sm)
            total = total + jnp.sum((dd * si).reshape(16, 8, 256), 0)
        side[0:1, cols] = jnp.sum(total, 0, keepdims=True)
        drad[:, cols] = dot3(rwh, rwl, qph[:, cols], qpl[:, cols], 1, 0)[0:8]

    staggered(4, (da, db), product, step)


def last_kernel(
    rows_y, rows_z, place, qps, sides, drads, geo, slots, cent, sl, se, dy,
    dpath, columns, dout, more,
    small_keep, small_send, energy,
    ghost, small, spread,
):
    kinds = iota((NSPEC, EDGES), 0).astype(F32)
    hot_c = jnp.where(kinds == cent[3:4, :], 1.0, 0.0)
    hot_n = jnp.where(kinds == geo[25:26, :], 1.0, 0.0)
    hots = jnp.concatenate([hot_c, hot_n], 0).astype(BF16)
    rad = geo[16:24, :]
    rad_h = rad.astype(BF16).astype(F32)
    rads = jnp.concatenate([rad_h, rad - rad_h], 0).astype(BF16)
    left = jnp.concatenate([hots, rads], 0)
    for n, (qh, ql) in enumerate(zip(qps[0::2], qps[1::2])):
        full = dot(left, qh[...], 1, 1)
        rest = dot(left, ql[...], 1, 1)
        part = slice(n * HALF, (n + 1) * HALF)
        small[0:128, part] = full[0:128] + rest[0:128]
        small[128:136, part] = full[128:136] + full[136:144] + rest[128:136]

    live, r, smooth = geo[10:11, :], geo[11:12, :], geo[9:10, :]
    inv = 1.0 / r
    grad = geo[15:16, :]
    reach = sl[0:1, :]
    lat_out = sl[1:2, :]
    order = (iota((8, EDGES), 0) + 1).astype(F32) * (math.pi / CUTOFF)
    angle = order * r
    sine = jnp.sin(angle) * inv
    cosine = jnp.cos(angle) * inv
    dr8 = drads[0][...] + drads[1][...]
    d_s = (
        grad * lat_out
        + grad * smooth * RH * reach
        + se[0:1, :]
        + sides[0][0:1, :]
        + sides[1][0:1, :]
        + BESSEL * jnp.sum(dr8 * sine, 0, keepdims=True)
    )
    t = r / CUTOFF
    t2 = t * t
    gap = 1.0 - t
    d_r = d_s * (live * (-168.0 / CUTOFF) * (t2 * t2 * t) * (gap * gap)) + (
        smooth * BESSEL
    ) * jnp.sum(dr8 * (order * cosine - sine * inv), 0, keepdims=True)
    ux, uy, uz = geo[12:13, :] * inv, geo[13:14, :] * inv, geo[14:15, :] * inv
    yy = [dy[c : c + 1, :] for c in range(9)]
    h2, s2 = 2.0 * HR * Q75, 2.0 * SR * Q75
    gx = R3 * yy[1] + ux * (h2 * yy[4] + s2 * yy[5]) + h2 * (uy * yy[6] + uz * yy[7])
    gy = R3 * yy[2] + uy * (s2 * yy[5] - h2 * yy[4]) + h2 * (ux * yy[6] + uz * yy[8])
    gz = R3 * yy[3] - 2.0 * s2 * uz * yy[5] + h2 * (ux * yy[7] + uy * yy[8])
    along = ux * gx + uy * gy + uz * gz
    zero = jnp.zeros((5, EDGES), F32)
    disp = jnp.concatenate(
        [
            live * ((gx - ux * along) * inv + ux * d_r),
            live * ((gy - uy * along) * inv + uy * d_r),
            live * ((gz - uz * along) * inv + uz * d_r),
            zero,
        ],
        0,
    )
    hi, mid, lo = pieces(disp)
    disp24 = jnp.concatenate([hi, mid, lo], 0).astype(BF16)
    acc = None
    mine = None
    for k in range(8):
        term = disp[:, k * 128 : (k + 1) * 128]
        mine = term if mine is None else mine + term
    mine = slot_total(mine)
    for i in range(4):
        cols = pl.ds(i * 256, 256)
        hot = jnp.where(iota((NTAB, 256), 0) == slots[:, cols], 1.0, 0.0).astype(BF16)
        term = dot(disp24[:, i * 256 : (i + 1) * 256], hot, 1, 1)
        acc = term if acc is None else acc + term
    ghost[...] = acc[0:8] + acc[8:16] + acc[16:24]
    lane = iota((8, 128), 1)
    middle = ghost[:, 512:640] - jnp.where(
        (lane >= ATOMS) & (lane < 2 * ATOMS), pltpu.roll(mine, ATOMS, 1), 0.0
    )
    ghost[:, 512:640] = middle
    atoms = spread.shape[1]
    spread[...] = jnp.zeros_like(spread)
    total = jnp.zeros_like(spread)
    for bx in range(3):
        for by in range(3):
            block = 3 * bx + by
            spread[:, 0:128] = ghost[:, block * 128 : (block + 1) * 128]
            start = place[4] + ((bx - 1) * rows_y + by - 1) * rows_z * ATOMS - ATOMS
            total = total + pltpu.roll(spread[...], lax.rem(start + 2 * atoms, atoms), 1)
    for n in range(atoms // LATENT):
        small[144 + 8 * n : 152 + 8 * n, :] = total[:, n * LATENT : (n + 1) * LATENT]

    edge_energy = smooth * lat_out
    total = None
    for k in range(8):
        term = edge_energy[:, k * 128 : (k + 1) * 128]
        total = term if total is None else total + term
    total = slot_total(jnp.broadcast_to(total, (8, 128)))[0:1]
    hot = jnp.where(iota((NSPEC, 128), 0).astype(F32) == cent[3:4, 0:128], 1.0, 0.0)
    energy[...] = jnp.broadcast_to(
        jnp.sum(hot * columns[0:64, 8:9], 0, keepdims=True) * total
        + jnp.sum(hot * columns[0:64, 9:10], 0, keepdims=True),
        energy.shape,
    )
    cot = cent[4:5, 0:128] * jnp.where(iota((1, 128), 1) < ATOMS, 1.0, 0.0)
    stack = jnp.concatenate(
        [dpath[...], hot * (cot * total), hot * cot, jnp.zeros((64, 128), F32)], 0
    )
    row = jnp.sum(stack.T, 0, keepdims=True)
    small[136:144, :] = jnp.zeros((8, LATENT), F32)
    small[136:137, 0:768] = row
    small[137:138, :] = dout[0:1, :]
    mine = pl.ds(pl.multiple_of(place[3] * HALF, HALF), HALF)
    other = pl.ds(pl.multiple_of((1 - place[3]) * HALF, HALF), HALF)
    for out, cols in ((small_keep, mine), (small_send, other)):
        out[0:192, :] = more[:, cols]
        out[192:, :] = small[:, cols]


def weights_kernel(dvwh, dvwl, x0h, x0l, dw1h, dw1l, x1h, x1l, out):
    out[0:128, :] = dot3(dvwh[...], dvwl[...], x0h[0:LATENT, :], x0l[0:LATENT, :], 1, 1)
    out[128:192, :] = dot3(dw1h[...], dw1l[...], x1h[0:LATENT, :], x1l[0:LATENT, :], 1, 1)


def halves(shape, dim):
    rows, cols = shape
    return (rows // 2, cols) if dim == 0 else (rows, cols // 2) if dim == 1 else shape


def half_of(shape, dim, bit):
    rows, cols = shape
    if dim == 0:
        rows //= 2
        return pl.ds(pl.multiple_of(bit * rows, 8), rows), slice(None)
    cols //= 2
    return slice(None), pl.ds(pl.multiple_of(bit * cols, 128), cols)


def down_kernel(dim, flag, place, keep, got, *outs):
    if dim is None:
        outs[0][...] = keep[...] + got[...]
        return
    for out, bit in zip(outs, (1 - place[flag], place[flag])):
        index = half_of(keep.shape, dim, bit)
        out[...] = keep[index] + got[index]


def up_kernel(dim, flag, place, mine, got, out):
    out[half_of(out.shape, dim, place[flag])] = mine[...]
    out[half_of(out.shape, dim, 1 - place[flag])] = got[...]


def end_kernel(parts, place, *refs):
    srcs, out, sem = refs[: len(parts)], refs[-2], refs[-1]
    copies = []
    for n, ((layer, start, mine), src) in enumerate(zip(parts, srcs)):
        block = place[3] if mine else 1 - place[3]
        cols = pl.ds(pl.multiple_of(block * HALF, HALF), HALF)
        rows = pl.ds(start, src.shape[0])
        copies.append(pltpu.make_async_copy(src, out.at[layer, rows, cols], sem.at[n]))
    for copy in copies:
        copy.start()
    for copy in copies:
        copy.wait()


def small_end_kernel(
    core_at, place, mine, got, energy,
    center, neigh, radial, value, env, path, out, scale, shift, grad, energies,
):
    for src, b in ((mine, place[core_at]), (got, 1 - place[core_at])):
        cols = pl.ds(pl.multiple_of(b * HALF, HALF), HALF)
        value[:, cols] = src[0:64, :]
        env[0, :, cols] = src[64:128, :]
        env[1, :, cols] = src[128:192, :]
        center[:, cols] = src[192:256, :]
        neigh[:, cols] = src[256:320, :]
        radial[:, cols] = src[320:328, :]
    is_first = place[core_at] == 0

    def whole(rows):
        first = jnp.where(is_first, mine[rows, :], got[rows, :])
        second = jnp.where(is_first, got[rows, :], mine[rows, :])
        return jnp.concatenate([first, second], 1)

    base = 336 + 8 * (place[4] // LATENT)
    spread = whole(pl.ds(pl.multiple_of(base, 8), 8))
    shift_by = LATENT - lax.rem(place[4], LATENT)
    grad[...] = pltpu.roll(spread, lax.rem(shift_by, LATENT), 1)[0:3, 0:ATOMS]
    energies[...] = energy[0:1, 0:ATOMS]
    row = whole(slice(328, 336))
    for n in range(9):
        path[n : n + 1, :] = row[0:1, n * 64 : (n + 1) * 64]
    scale[...] = row[0:1, 576:640]
    shift[...] = row[0:1, 640:704]
    for n in range(8):
        out[n : n + 1, :] = row[1:2, n * 128 : (n + 1) * 128]


VSPEC = pl.BlockSpec(memory_space=pltpu.VMEM)
SSPEC = pl.BlockSpec(memory_space=pltpu.SMEM)
ASPEC = pl.BlockSpec(memory_space=pl.ANY)
HSPEC = pl.BlockSpec(memory_space=pltpu.HBM)


PROGRAM = (
    "late", "send_a", "keep_a", "mid", "a", "early", "send_c", "a", "keep_c", "c",
    "couple", "a", "pre0", "a", "weights", "c", "a", "pre1", "a", "c",
    "last", "c", "free", "a", "a", "a", "a", "end_a", "c", "s",
    "c", "s", "c", "s", "s", "c", "c", "s", "s", "s",
    "end_s", "c",
)


COST = {
    "late": 6.5, "send_a": 4.6, "keep_a": 0.57, "mid": 3, "early": 5.0, "send_c": 4.6,
    "keep_c": 4.6, "couple": 25.2, "weights": 4, "pre0": 3.5, "pre1": 3.5, "last": 5,
    "land_a": 8, "land_c": 2, "land_s": 3.0,
}


class Order:
    def __init__(self):
        self.token = None
        self.free = False
        self.extra = ()

    def __call__(
        self, body, outs, args, scratch=(), scalar=False, hbm=(), plain=False, alias=None, us=1,
        limit=6, name=None, mark=False,
    ):
        specs = [HSPEC if n in hbm else VSPEC for n in range(len(args))]
        if scalar:
            specs[0] = SSPEC
        count, given = len(args), len(outs)
        marked = mark or not self.free
        tokens = () if self.token is None or self.free else (self.token,)
        tokens, self.extra = tokens + self.extra, ()

        def kernel(*refs):
            after = refs[count + len(tokens) :]
            if not marked:
                return body(*refs[:count], *after)
            after[given][...] = jnp.zeros((8, 128), F32)
            body(*refs[:count], *after[:given], *after[given + 1 :])

        if plain:
            shapes = [jax.ShapeDtypeStruct(shape, dtype) for shape, dtype in outs]
        else:
            shapes = [pltpu.VMEM(shape, dtype) for shape, dtype in outs]
        out_spec = HSPEC if plain == "hbm" else VSPEC
        got = pl.pallas_call(
            kernel,
            name=name or getattr(body, "func", body).__name__,
            out_shape=shapes + ([pltpu.VMEM((8, 128), F32)] if marked else []),
            in_specs=specs + [ASPEC] * len(tokens),
            out_specs=[out_spec] * given + ([VSPEC] if marked else []),
            scratch_shapes=list(scratch),
            input_output_aliases=alias or {},
            compiler_params=pltpu.CompilerParams(vmem_limit_bytes=limit << 20),
            cost_estimate=pl.CostEstimate(
                flops=int(us * 3e9), bytes_accessed=1 << 20, transcendentals=0
            ),
        )(*args, *tokens)
        if not marked:
            return got
        self.token = got[-1]
        return got[:-1]


def is_up(axis, bit):
    return (lax.axis_index(axis) // bit) & 1


def even_pairs(axis):
    return [(i, i ^ 1) for i in range(lax.axis_size(axis))]


def odd_pairs(axis):
    count = lax.axis_size(axis)
    return [p for i in range(1, count - 1, 2) for p in ((i, i + 1), (i + 1, i))]


def neighbours_of(axis, even, odd):
    pairs = odd_pairs(axis)
    return (
        lax.ppermute(even, axis, even_pairs(axis)),
        lax.ppermute(odd, axis, pairs) if pairs else jnp.zeros_like(odd),
    )


class Route:
    def __init__(self, mesh_sizes, base, tall_first=False):
        sizes = dict(mesh_sizes)
        names = list(sizes)

        def bits(axis, least=1):
            return [(axis, 1 << n) for n in range(20) if least <= 1 << n < sizes[axis]]

        flat, tall = bits("gx"), bits("gy") + bits("gz", 2)
        first = [("gz", 1)]
        one, two = (flat, tall), (flat[::-1], tall[::-1])
        if tall_first:
            one, two = one[::-1], two[::-1]
        self.steps = list(zip(first + one[0] + one[1], first + two[0] + two[1]))
        self.count = len(self.steps)
        self.base = base
        self.names = tuple(names)
        coords = [()]
        for name in names:
            coords = [c + (i,) for c in coords for i in range(sizes[name])]
        index = {c: n for n, c in enumerate(coords)}
        self.pairs = []
        for step in self.steps:
            pairs = []
            for c in coords:
                axis, bit = step[c[names.index("gz")] & 1]
                at = names.index(axis)
                pairs.append((index[c], index[c[:at] + (c[at] ^ bit,) + c[at + 1 :]]))
            self.pairs.append(pairs)

    def flags(self):
        core = is_up("gz", 1)
        return [jnp.where(core == 1, is_up(*two), is_up(*one)) for one, two in self.steps]

    def swap(self, x, at):
        return lax.ppermute(x, self.names, self.pairs[at])


class Sum:
    def __init__(self, name, order, place, route, send, dims):
        self.name = name
        self.order, self.place, self.route = order, place, route
        self.dims = (1,) + dims + (None,) * (route.count - 1 - len(dims))
        self.keep, self.send = None, send
        self.at, self.rising = 0, False
        self.shapes = []
        self.launch()

    def launch(self):
        with jax.named_scope(f"sum_{self.name}_{'up' if self.rising else 'down'}_{self.at}"):
            self.got = self.route.swap(self.send, self.at)

    @property
    def over(self):
        return self.rising and self.at == 0

    def land(self):
        (self.climb if self.rising else self.descend)()
        self.launch()

    def call(self, body, dim, flag, shapes, args):
        return self.order(
            functools.partial(body, dim, flag),
            [(shape, F32) for shape in shapes],
            (self.place, *args),
            scalar=True,
            us=COST[f"land_{self.name}"],
            name=f"land_{self.name}_{'up' if self.rising else 'down'}_{self.at}",
        )

    def descend(self):
        self.shapes.append(self.keep.shape)
        self.at += 1
        last = self.at == self.route.count
        dim = None if last else self.dims[self.at]
        shapes = [halves(self.keep.shape, dim)] * (1 if dim is None else 2)
        outs = self.call(
            down_kernel, dim, self.route.base + self.at, shapes, (self.keep, self.got)
        )
        self.send, self.keep = outs[0], outs[-1]
        if last:
            self.rising = True
            self.rise()

    def rise(self):
        self.at -= 1
        while self.at > 0 and self.dims[self.at] is None:
            self.at -= 1

    def climb(self):
        (self.send,) = self.call(
            up_kernel,
            self.dims[self.at],
            self.route.base + self.at,
            [self.shapes[self.at - 1]],
            (self.send, self.got),
        )
        self.rise()


def per_device(
    positions,
    species,
    neighbours,
    embed_center,
    embed_neigh,
    embed_radial,
    value_proj,
    env_weight,
    latent_weight,
    path_weight,
    out_weight,
    scale_table,
    shift_table,
    cotangent,
):
    vm, sem = pltpu.VMEM, pltpu.SemaphoreType
    order = Order()
    sizes = [(axis, lax.axis_size(axis)) for axis in ("gx", "gy", "gz")]
    route = Route(sizes, 5)
    steep = Route(sizes, 5 + route.count, tall_first=True)
    first_atom = lax.axis_index(("gx", "gy", "gz")) * ATOMS
    place = [is_up("gz", 1), is_up("gy", 1), is_up("gx", 1), is_up("gz", 1), first_atom]
    place = jnp.stack(place + route.flags() + steep.flags()).astype(jnp.int32)
    spec_row = species.reshape(1, ATOMS)

    (table,) = order(pack_kernel, [((8, 128), F32)], (positions, spec_row), us=1)
    even, odd = neighbours_of("gz", table, table)
    (table,) = order(
        join_z_kernel, [((8, 128), F32)], (place, table, even, odd), scalar=True, us=1
    )
    even, odd = neighbours_of("gy", table, table)
    (table,) = order(
        join_y_kernel,
        [((8, 384), F32)],
        (place, table, even, odd),
        scalar=True,
        us=1,
    )
    even, odd = neighbours_of("gx", table, table)

    wide = ((WIDE, EDGES), BF16)
    half = ((HALF, EDGES), BF16)
    row64 = ((64, LATENT), BF16)
    row128 = ((128, LATENT), BF16)
    w0h, w0l, w1h, w1l, hots, veh, vel, evh, evl, path, columns, slots, cent, rad_w = order(
        prep_kernel,
        [
            wide, wide, wide, wide, ((288, LATENT), BF16), row128, row128, row64, row64,
            ((576, 128), F32), ((128, 128), F32), ((1, EDGES), jnp.int32), ((8, EDGES), F32),
            ((8, LATENT), F32),
        ],
        (latent_weight, embed_center, embed_neigh, embed_radial, value_proj.T,
         jnp.swapaxes(env_weight, 1, 2), neighbours, positions, spec_row,
         cotangent.reshape(1, ATOMS), path_weight, out_weight.reshape(8, 128),
         scale_table.reshape(1, NSPEC), shift_table.reshape(1, NSPEC)),
        [
            vm((NSPEC, LATENT), F32), vm((NSPEC, LATENT), F32), vm((CHANNELS, LATENT), F32),
            vm((2, CHANNELS, LATENT), F32), vm((NB, ATOMS), jnp.int32), vm((3, ATOMS), F32),
            vm((1, ATOMS), jnp.int32), vm((1, ATOMS), F32), vm((9, CHANNELS), F32),
            vm((8, 128), F32), vm((1, NSPEC), F32), vm((1, NSPEC), F32), vm((128, 128), F32),
            sem.DMA((13,)),
        ],
        hbm=range(1, 14),
        us=4,
    )

    x0h, x0l, x1h, x1l, z0, vw, w1, geo, g0, g1, f1 = order(
        fwd_kernel,
        [
            wide, wide, wide, wide,
            ((LATENT, EDGES), F32), ((128, EDGES), F32), ((64, EDGES), F32), ((G_ROWS, EDGES), F32), ((576, 128), F32), ((576, 128), F32),
            ((576, EDGES), F32),
        ],
        (place, table, even, odd, slots, cent, w0h, w0l, hots, veh, vel, evh, evl, path, columns),
        [vm((8, EDGES), F32), vm((LATENT, 256), F32), vm((LATENT, 256), F32)],
        scalar=True,
        us=22,
        limit=18,
    )

    chains = {}

    def grad(mine, cost, xh, xl, qh, ql):
        return order(
            functools.partial(grad_kernel, mine),
            [((WIDE, HALF), F32)],
            (place, xh, xl, qh, ql),
            scalar=True,
            us=cost,
        )[0]

    def send(name, *args):
        chains[name] = Sum(name, order, place, route, grad(False, COST[f"send_{name}"], *args), (0, 0, 0, 1))

    def keep(name, *args):
        chains[name].keep = grad(True, COST[f"keep_{name}"], *args)

    def late():
        return order(
            late_kernel,
            [
                ((LATENT, EDGES), BF16), ((LATENT, EDGES), BF16), ((8, EDGES), F32),
                ((8, LATENT), F32),
            ],
            (x1h, x1l, w1h, w1l, columns, geo),
            [vm((LATENT, 128), F32), vm((LATENT, 256), F32), vm((LATENT, 256), F32)],
            us=COST["late"],
            limit=17,
        )

    def mid():
        return order(
            mid_kernel,
            [((192, EDGES), F32), ((64, EDGES), BF16), ((64, EDGES), BF16), ((16, EDGES), F32)],
            (v.q1h, v.q1l, w1h, w1l, f1, g1, w1, geo),
            [vm((576, 128), F32)],
            us=COST["mid"],
        )

    def early():
        return order(
            early_kernel,
            [
                ((LATENT, EDGES), F32), ((LATENT, EDGES), BF16), ((LATENT, EDGES), BF16),
                ((8, EDGES), F32),
            ],
            (v.q1h, v.q1l, w1h, w1l, evh, evl, v.dw1h, v.dw1l, columns, geo, z0),
            [vm((LATENT, 256), F32), vm((LATENT, 256), F32)],
            us=COST["early"],
            limit=12,
        )

    def couple():
        return order(
            couple_kernel,
            [
                ((128, EDGES), BF16), ((128, EDGES), BF16), ((16, EDGES), F32),
                ((576, 128), F32),
            ],
            (v.q0h, v.q0l, w0h, w0l, vw, geo, g0, g1, v.ds1, path, v.dy1),
            [vm((192, EDGES), F32), vm((576, 128), F32), vm((16, EDGES), F32)],
            us=COST["couple"],
        )

    def before(h):
        return order(
            functools.partial(pre_kernel, h),
            [half, half, ((8, EDGES), F32), ((8, EDGES), F32)],
            (v.q0h, v.q0l, w0h, w0l, veh, vel, v.dvwh, v.dvwl, v.dlat, hots, cent, geo, rad_w),
            [vm((HALF, 256), F32), vm((HALF, 256), F32), vm((HALF, 256), F32)],
            us=COST[f"pre{h}"],
        )

    def run_late():
        v.q1h, v.q1l, v.sl, v.dout = late()

    def run_mid():
        v.ds1, v.dw1h, v.dw1l, v.dy1 = mid()

    def run_early():
        v.dlat, v.q0h, v.q0l, v.se = early()

    def run_couple():
        v.dvwh, v.dvwl, v.dy, v.dpath = couple()

    def run_weights():
        (v.more,) = order(
            weights_kernel,
            [((192, LATENT), F32)],
            (v.dvwh, v.dvwl, x0h, x0l, v.dw1h, v.dw1l, x1h, x1l),
            us=COST["weights"],
        )

    def run_last():
        atoms = ATOMS * math.prod(size for _, size in sizes)
        height = 144 + 8 * (atoms // LATENT)
        (ah, al, side_a, drad_a), (bh, bl, side_b, drad_b) = v.pres
        keep, send, v.energy = order(
            lambda place, *refs: last_kernel(
                sizes[1][1], sizes[2][1], place, refs[0:4], refs[4:6], refs[6:8], *refs[8:]
            ),
            [((192 + height, HALF), F32), ((192 + height, HALF), F32), ((8, 128), F32)],
            (place, ah, al, bh, bl, side_a, side_b, drad_a, drad_b, geo, slots, cent, v.sl, v.se,
             v.dy, v.dpath, columns, v.dout, v.more),
            [vm((8, NTAB), F32), vm((height, LATENT), F32), vm((8, atoms), F32)],
            scalar=True,
            us=COST["last"],
            name="last_kernel",
        )
        chains["s"] = Sum("s", order, place, route, send, (1, 1))
        chains["s"].keep = keep

    def finish(parts, arrays, mark=False):
        last = 1 + len(arrays)
        done = () if v.d_latent is None else (v.d_latent,)
        (v.d_latent,) = order(
            functools.partial(end_kernel, parts),
            [((2, WIDE, LATENT), F32)],
            (place, *arrays, *done),
            [sem.DMA((len(parts),))],
            scalar=True,
            hbm=(last,) if done else (),
            plain="hbm",
            alias={last: 0} if done else None,
            us=3,
            mark=mark,
        )

    def finish_small():
        s = chains["s"]
        v.small = order(
            functools.partial(small_end_kernel, 3),
            [
                ((NSPEC, LATENT), F32), ((NSPEC, LATENT), F32), ((NBESSEL, LATENT), F32),
                ((CHANNELS, LATENT), F32), ((2, CHANNELS, LATENT), F32), ((9, CHANNELS), F32),
                ((8, 128), F32), ((1, NSPEC), F32), ((1, NSPEC), F32), ((3, ATOMS), F32),
                ((1, ATOMS), F32),
            ],
            (place, s.send, s.got, v.energy),
            scalar=True,
            plain=True,
            us=2,
        )

    def land(name):
        chain = chains[name]
        if chain.over:
            return
        if name == "c" and chain.rising and chain.at == 1 and v.d_latent is not None:
            order.extra = (order.token,)
        chain.land()

    def settle(name):
        while not chains[name].over:
            land(name)

    def finish_a():
        settle("a")
        finish(((1, 0, True), (1, 0, False)), (chains["a"].send, chains["a"].got), mark=True)

    def finish_s():
        settle("s")
        finish_small()

    def set_free():
        order.free = True

    def set_bound():
        order.free = False

    v = types.SimpleNamespace(d_latent=None, pres=[])
    steps = {
        "late": run_late,
        "mid": run_mid,
        "early": run_early,
        "couple": run_couple,
        "weights": run_weights,
        "pre0": lambda: v.pres.append(before(0)),
        "pre1": lambda: v.pres.append(before(1)),
        "last": run_last,
        "send_a": lambda: send("a", x1h, x1l, v.q1h, v.q1l),
        "keep_a": lambda: keep("a", x1h, x1l, v.q1h, v.q1l),
        "send_c": lambda: send("c", x0h, x0l, v.q0h, v.q0l),
        "keep_c": lambda: keep("c", x0h, x0l, v.q0h, v.q0l),
        "a": lambda: land("a"),
        "c": lambda: land("c"),
        "s": lambda: land("s"),
        "free": set_free,
        "bind": set_bound,
        "end_a": finish_a,
        "end_s": finish_s,
    }
    for step in PROGRAM:
        steps[step]()
    settle("c")
    c = chains["c"]
    finish(((0, 0, True),), (c.send,))
    finish(((0, 0, False),), (c.got,))
    (center, neigh, radial, value, env, path_grad, out, scale, shift, position_grad,
     energies) = v.small
    d_latent = v.d_latent
    return (
        energies.reshape(ATOMS),
        position_grad,
        center,
        neigh,
        radial,
        value.T,
        jnp.swapaxes(env, 1, 2),
        d_latent,
        path_grad,
        out.reshape(LATENT),
        scale.reshape(NSPEC),
        shift.reshape(NSPEC),
    )


def solution(mesh):
    everything = ("gx", "gy", "gz")
    return jax.shard_map(
        per_device,
        mesh=mesh,
        in_specs=(
            P(None, everything),
            P(everything),
            P(None, everything),
            P(),
            P(),
            P(),
            P(),
            P(),
            P(),
            P(),
            P(),
            P(),
            P(),
            P(everything),
        ),
        out_specs=(
            P(everything),
            P(None, everything),
            P(),
            P(),
            P(),
            P(),
            P(),
            P(),
            P(),
            P(),
            P(),
            P(),
        ),
        check_vma=False,
    )
```

```python
import functools
import math
import types

import jax
import jax.numpy as jnp
import numpy as np
from jax import lax
from jax.experimental import pallas as pl
from jax.experimental.pallas import tpu as pltpu
from jax.sharding import PartitionSpec as P

LATENT = 1024
CHANNELS = 64
NSPEC = 64
NBESSEL = 8
NB = 32
ATOMS = 32
EDGES = NB * ATOMS
WIDE = LATENT + 3 * CHANNELS
HALF = LATENT // 2
QUARTER = LATENT // 4
NTAB = 9 * 128
OWN = 4 * 128 + ATOMS

CUTOFF = 5.0
RH = 0.7071067811865476
HR = 0.7071067811865476
SR = 0.4082482904638631
R3 = math.sqrt(3.0)
Q75 = math.sqrt(7.5)
NORM = NB**-0.5
BESSEL = math.sqrt(2.0 / CUTOFF)

F32 = jnp.float32
BF16 = jnp.bfloat16

G_SMOOTH, G_LIVE, G_R, G_DISP, G_GRAD, G_RAD, G_GS, G_SPEC = 9, 10, 11, 12, 15, 16, 24, 25
G_ROWS = 32


def dot(a, b, ca, cb):
    return lax.dot_general(a, b, (((ca,), (cb,)), ((), ())), preferred_element_type=F32)


def dot3(ah, al, bh, bl, ca, cb):
    return dot(ah, bh, ca, cb) + dot(ah, bl, ca, cb) + dot(al, bh, ca, cb)


def split(x):
    hi = x.astype(BF16)
    return hi, (x - hi.astype(F32)).astype(BF16)


def pieces(x):
    hi = x.astype(BF16).astype(F32)
    rest = x - hi
    mid = rest.astype(BF16).astype(F32)
    return hi, mid, rest - mid


def sigmoid(x):
    return 0.5 * jnp.tanh(0.5 * x) + 0.5


def silu_both(x):
    sig = sigmoid(x)
    return x * sig, sig * (1.0 + x * (1.0 - sig))


def lanes(i, width):
    return pl.ds(pl.multiple_of(i * width, width), width)


def over(count, body):
    def step(i, carry):
        body(i)
        return carry

    lax.fori_loop(0, count, step, 0)


def staggered(count, bufs, first, second):
    first(0, bufs[0])
    for i in range(count):
        if i + 1 < count:
            first(i + 1, bufs[(i + 1) % 2])
        second(i, bufs[i % 2])


def iota(shape, dim):
    return lax.broadcasted_iota(jnp.int32, shape, dim)


def slot_total(x):
    x = x + pltpu.roll(x, 64, 1)
    return x + pltpu.roll(x, 32, 1)


def make_env(geo, w, env):
    for c in range(9):
        acc = None
        for k in range(8):
            cols = pl.ds(k * 128, 128)
            term = w[:, cols] if c == 0 else geo[c : c + 1, cols] * w[:, cols]
            acc = term if acc is None else acc + term
        env[c * 64 : (c + 1) * 64, :] = slot_total(acc) * NORM


def rows_of(ref, c, cols=slice(None)):
    return ref[c * 64 : (c + 1) * 64, cols]


def pack_kernel(pos, spec, out):
    out[...] = jnp.zeros_like(out)
    out[0:3, 0:ATOMS] = pos[...]
    out[3:4, 0:ATOMS] = spec[...].astype(F32)


def join_z_kernel(place, own, even_in, odd_in, out):
    is_odd = place[0] == 1
    left = jnp.where(is_odd, even_in[...], odd_in[...])
    right = jnp.where(is_odd, odd_in[...], even_in[...])
    out[...] = left + pltpu.roll(own[...], ATOMS, 1) + pltpu.roll(right, 2 * ATOMS, 1)


def join_y_kernel(place, own, even_in, odd_in, out):
    is_odd = place[1] == 1
    out[:, 0:128] = jnp.where(is_odd, even_in[...], odd_in[...])
    out[:, 128:256] = own[...]
    out[:, 256:384] = jnp.where(is_odd, odd_in[...], even_in[...])


def prep_kernel(
    w, ec_in, en_in, rad_in, vp_in, env_in, neigh_in, pos_in, spec_in, cot_in, path_in, outw_in,
    scale_in, shift_in,
    w0h, w0l, w1h, w1l, table, veh, vel, evh, evl, path_b, cols, slots, cent, rad_w,
    ec, en, vp, env, neigh, pos, spec, cot, path, outw, scale, shift, square, sem,
):
    pairs = (
        (ec_in, ec), (en_in, en), (rad_in, rad_w), (vp_in, vp), (env_in, env), (neigh_in, neigh),
        (pos_in, pos), (spec_in, spec), (cot_in, cot), (path_in, path), (outw_in, outw),
        (scale_in, scale), (shift_in, shift),
    )
    copies = [
        pltpu.make_async_copy(src, dst, sem.at[n]) for n, (src, dst) in enumerate(pairs)
    ]
    for copy in copies:
        copy.start()

    for layer, (hi, lo) in enumerate(((w0h, w0l), (w1h, w1l))):

        def part(i, layer=layer, hi=hi, lo=lo):
            rows = pl.ds(pl.multiple_of(i * 64, 64), 64)
            hi[rows, :], lo[rows, :] = split(w[layer, rows, :])

        over(WIDE // 64, part)
    for copy in copies:
        copy.wait()

    ech, ecl = split(ec[...])
    enh, enl = split(en[...])
    rh = rad_w[...].astype(BF16).astype(F32)
    rl = rad_w[...] - rh
    table[0:64, :] = ech
    table[64:128, :] = enh
    table[128:192, :] = ecl
    table[192:256, :] = enl
    table[256:288, :] = jnp.concatenate([rh, rl, rh, jnp.zeros_like(rh)], 0).astype(BF16)
    veh[0:64, :], vel[0:64, :] = split(vp[...])
    veh[64:128, :], vel[64:128, :] = split(env[0])
    evh[...], evl[...] = split(env[1])

    square[...] = jnp.zeros_like(square)
    square[0:8, :] = outw[...]
    square[8:9, 0:64] = scale[...]
    square[9:10, 0:64] = shift[...]
    square[16:25, 0:64] = path[...]
    turned = square[...].T
    cols[...] = turned
    for n in range(9):
        path_b[n * 64 : (n + 1) * 64, :] = jnp.broadcast_to(
            turned[0:64, 16 + n : 17 + n], (64, 128)
        )

    square[0:32, :] = jnp.zeros((32, 128), F32)
    square[0:32, 0:ATOMS] = neigh[...].astype(F32)
    row = square[pl.ds(0, 8, 4), :]
    for i in range(1, 4):
        row = row + pltpu.roll(square[pl.ds(i, 8, 4), :], i * ATOMS, 1)
    padded = row
    for m in range(1, 9):
        padded = padded + jnp.where(row >= 96.0 * m, 32.0, 0.0)
    padded = padded.astype(jnp.int32)
    square[0:8, :] = jnp.zeros((8, 128), F32)
    square[0:3, 0:ATOMS] = pos[...]
    square[3:4, 0:ATOMS] = spec[...].astype(F32)
    square[4:5, 0:ATOMS] = cot[...]
    own = square[0:8, :]
    own = own + pltpu.roll(own, 32, 1)
    own = own + pltpu.roll(own, 64, 1)
    for k in range(8):
        slots[:, k * 128 : (k + 1) * 128] = padded[k : k + 1]
        cent[:, k * 128 : (k + 1) * 128] = own


def embed_inputs(cent, geo, cols):
    kinds = iota((NSPEC, 256), 0).astype(F32)
    hot_c = jnp.where(kinds == cent[3:4, cols], 1.0, 0.0)
    hot_n = jnp.where(kinds == geo[25:26, cols], 1.0, 0.0)
    hots = jnp.concatenate([hot_c, hot_n], 0).astype(BF16)
    rad = geo[16:24, cols]
    rad_h = rad.astype(BF16).astype(F32)
    rads = jnp.concatenate([rad_h, rad_h, rad - rad_h, jnp.zeros_like(rad)], 0).astype(BF16)
    return jnp.concatenate([hots, hots, rads], 0)


def fwd_kernel(
    place, tab, even_in, odd_in, slots, cent, w0h, w0l, table, veh, vel, evh, evl, path, columns,
    x0h, x0l, x1h, x1l, z0, vw, w1, geo, g0, g1, f1,
    gat, za, zb,
):
    is_odd = place[2] == 1
    whole = jnp.concatenate(
        [
            jnp.where(is_odd, even_in[...], odd_in[...]),
            tab[...],
            jnp.where(is_odd, odd_in[...], even_in[...]),
        ],
        1,
    )
    hi, mid, lo = pieces(whole)
    tab24 = jnp.concatenate([hi, mid, lo], 0).astype(BF16)

    def gather(i):
        cols = lanes(i, 256)
        hot = jnp.where(iota((NTAB, 256), 0) == slots[:, cols], 1.0, 0.0).astype(BF16)
        got = dot(tab24, hot, 1, 0)
        gat[:, cols] = got[0:8] + got[8:16] + got[16:24]

    over(4, gather)

    live = jnp.where(slots[...] != OWN + iota((1, EDGES), 1) % ATOMS, 1.0, 0.0)
    dead = 1.0 - live
    dx = (gat[0:1, :] - cent[0:1, :]) * live + dead * 2.5
    dy = (gat[1:2, :] - cent[1:2, :]) * live
    dz = (gat[2:3, :] - cent[2:3, :]) * live
    r = jnp.sqrt(dx * dx + dy * dy + dz * dz)
    inv = 1.0 / r
    t = r / CUTOFF
    t2 = t * t
    t6 = t2 * t2 * t2
    smooth = live * (1.0 - 28.0 * t6 + 48.0 * t6 * t - 21.0 * t6 * t * t)
    ux, uy, uz = dx * inv, dy * inv, dz * inv
    geo[0:1, :] = jnp.ones_like(r)
    geo[1:2, :] = R3 * ux
    geo[2:3, :] = R3 * uy
    geo[3:4, :] = R3 * uz
    geo[4:5, :] = Q75 * HR * (ux * ux - uy * uy)
    geo[5:6, :] = Q75 * SR * (ux * ux + uy * uy - 2.0 * uz * uz)
    geo[6:7, :] = Q75 * 2.0 * HR * (ux * uy)
    geo[7:8, :] = Q75 * 2.0 * HR * (ux * uz)
    geo[8:9, :] = Q75 * 2.0 * HR * (uy * uz)
    geo[9:10, :] = smooth
    geo[10:11, :] = live
    geo[11:12, :] = r
    geo[12:13, :] = dx
    geo[13:14, :] = dy
    geo[14:15, :] = dz
    order = (iota((8, EDGES), 0) + 1).astype(F32) * (math.pi / CUTOFF)
    geo[16:24, :] = smooth * BESSEL * jnp.sin(order * r) * inv
    hot_c = jnp.where(iota((NSPEC, EDGES), 0).astype(F32) == cent[3:4, :], 1.0, 0.0)
    grad = cent[4:5, :] * jnp.sum(hot_c * columns[0:64, 8:9], 0, keepdims=True)
    geo[15:16, :] = grad
    geo[24:25, :] = grad * smooth
    geo[25:26, :] = gat[3:4, :]
    geo[26:32, :] = jnp.zeros((6, EDGES), F32)

    def embed_product(i, out):
        cols = pl.ds(i * 256, 256)
        out[...] = dot(table[...], embed_inputs(cent, geo, cols), 0, 0)

    def embed(i, before):
        cols = pl.ds(i * 256, 256)
        sm = geo[9:10, cols]
        for b in range(8):
            rows = pl.ds(b * 128, 128)
            p = before[rows, :]
            x0h[rows, cols], x0l[rows, cols] = split(p * sigmoid(p) * sm)
        vw[:, cols] = dot3(
            veh[...], vel[...], x0h[0:LATENT, cols], x0l[0:LATENT, cols], 1, 0
        )

    staggered(4, (za, zb), embed_product, embed)
    make_env(geo, vw.at[64:128, :], g0)

    def tensor(k):
        cols = lanes(k, 128)
        v = vw[0:64, cols]
        y = [geo[c : c + 1, cols] for c in range(9)]
        e0 = rows_of(g0, 0)
        e1, e2, e3 = rows_of(g0, 1), rows_of(g0, 2), rows_of(g0, 3)
        a, b, c = y[1] * e1, y[2] * e2, y[3] * e3
        vec = a + b + c
        quad = y[4] * rows_of(g0, 4)
        for m in range(5, 9):
            quad = quad + y[m] * rows_of(g0, m)
        x0h[1024:1088, cols], x0l[1024:1088, cols] = split(v * e0)
        x0h[1088:1152, cols], x0l[1088:1152, cols] = split(v * vec)
        x0h[1152:1216, cols], x0l[1152:1216, cols] = split(v * quad)
        p = [rows_of(path, n) for n in range(9)]
        e12, e13 = y[1] * e2, y[1] * e3
        e21, e23 = y[2] * e1, y[2] * e3
        e31, e32 = y[3] * e1, y[3] * e2
        q00 = HR * y[4] + SR * y[5]
        q11 = SR * y[5] - HR * y[4]
        q22 = -2.0 * SR * y[5]
        q01, q02, q12 = HR * y[6], HR * y[7], HR * y[8]
        f1[0:64, cols] = v * (p[0] * e0 + p[1] * vec)
        p3g = p[3] * e0
        f1[64:128, cols] = v * (
            p[2] * e1 + p3g * y[1] + p[4] * (e23 - e32) + p[5] * (q00 * e1 + q01 * e2 + q02 * e3)
        )
        f1[128:192, cols] = v * (
            p[2] * e2 + p3g * y[2] + p[4] * (e31 - e13) + p[5] * (q01 * e1 + q11 * e2 + q12 * e3)
        )
        f1[192:256, cols] = v * (
            p[2] * e3 + p3g * y[3] + p[4] * (e12 - e21) + p[5] * (q02 * e1 + q12 * e2 + q22 * e3)
        )
        p8g = p[8] * e0
        pair = (
            HR * (a - b),
            SR * (a + b - 2.0 * c),
            HR * (e12 + e21),
            HR * (e13 + e31),
            HR * (e23 + e32),
        )
        for m in range(5):
            f1[(4 + m) * 64 : (5 + m) * 64, cols] = v * (
                p[6] * pair[m] + p[7] * rows_of(g0, 4 + m) + p8g * y[4 + m]
            )

    over(8, tensor)

    def layer_product(i, out):
        cols = pl.ds(i * 256, 256)
        out[...] = dot3(w0h[...], w0l[...], x0h[:, cols], x0l[:, cols], 0, 0)

    def layer(i, zs):
        cols = pl.ds(i * 256, 256)
        sm = geo[9:10, cols]
        for b in range(8):
            rows = pl.ds(b * 128, 128)
            z = zs[rows, :]
            z0[rows, cols] = z
            old = x0h[rows, cols].astype(F32) + x0l[rows, cols].astype(F32)
            x1h[rows, cols], x1l[rows, cols] = split((old + sm * (z * sigmoid(z))) * RH)
        w1[:, cols] = dot3(
            evh[...], evl[...], x1h[0:LATENT, cols], x1l[0:LATENT, cols], 1, 0
        )

    staggered(4, (za, zb), layer_product, layer)
    make_env(geo, w1, g1)

    def scalars(k):
        cols = lanes(k, 128)
        s0 = rows_of(f1, 0, cols) * rows_of(g1, 0)
        s1 = rows_of(f1, 1, cols) * rows_of(g1, 1)
        for c in range(2, 4):
            s1 = s1 + rows_of(f1, c, cols) * rows_of(g1, c)
        s2 = rows_of(f1, 4, cols) * rows_of(g1, 4)
        for c in range(5, 9):
            s2 = s2 + rows_of(f1, c, cols) * rows_of(g1, c)
        x1h[1024:1088, cols], x1l[1024:1088, cols] = split(s0)
        x1h[1088:1152, cols], x1l[1088:1152, cols] = split(s1)
        x1h[1152:1216, cols], x1l[1152:1216, cols] = split(s2)

    over(8, scalars)


def grad_kernel(mine, place, xh, xl, qh, ql, out):
    block = place[3] if mine else 1 - place[3]
    for n in range(0, HALF, QUARTER):
        rows = pl.ds(pl.multiple_of(block * HALF, HALF) + n, QUARTER)
        out[:, n : n + QUARTER] = dot3(xh[...], xl[...], qh[rows, :], ql[rows, :], 1, 1)


def late_kernel(x1h, x1l, wh, wl, columns, geo, qh, ql, side, dout, acc, za, zb):
    acc[...] = jnp.zeros_like(acc)
    side[...] = jnp.zeros_like(side)

    def product(i, out):
        cols = pl.ds(i * 256, 256)
        out[...] = dot3(wh[...], wl[...], x1h[:, cols], x1l[:, cols], 0, 0)

    def step(i, zs):
        cols = pl.ds(i * 256, 256)
        sm = geo[9:10, cols]
        gs = geo[24:25, cols]
        scale = gs * sm * RH
        reach = jnp.zeros((8, 256), F32)
        total = jnp.zeros((8, 256), F32)
        for b in range(8):
            rows = pl.ds(b * 128, 128)
            si, dsi = silu_both(zs[rows, :])
            ow = columns[:, b : b + 1]
            qh[rows, cols], ql[rows, cols] = split((ow * scale) * dsi)
            lat = (x1h[rows, cols].astype(F32) + x1l[rows, cols].astype(F32) + sm * si) * RH
            part = gs * lat
            acc[rows, :] += part[:, 0:128] + part[:, 128:256]
            reach = reach + jnp.sum((ow * si).reshape(16, 8, 256), 0)
            total = total + jnp.sum((ow * lat).reshape(16, 8, 256), 0)
        side[0:1, cols] = jnp.sum(reach, 0, keepdims=True)
        side[1:2, cols] = jnp.sum(total, 0, keepdims=True)

    staggered(4, (za, zb), product, step)
    dout[...] = jnp.broadcast_to(jnp.sum(acc[...].T, 0, keepdims=True), dout.shape)


def mid_kernel(qh, ql, wh, wl, f1, g1, w1, geo, ds1, dwh, dwl, dy, denv):
    def scal(i):
        cols = lanes(i, 256)
        ds1[:, cols] = dot3(wh[1024:1216, :], wl[1024:1216, :], qh[:, cols], ql[:, cols], 1, 0)

    over(4, scal)
    for c in range(9):
        kind = 0 if c == 0 else (1 if c < 4 else 2)
        acc = None
        for k in range(8):
            cols = pl.ds(k * 128, 128)
            term = rows_of(ds1, kind, cols) * rows_of(f1, c, cols)
            acc = term if acc is None else acc + term
        denv[c * 64 : (c + 1) * 64, :] = slot_total(acc) * NORM
    env_back(geo, w1, denv, dwh, dwl, dy, None)


def env_back(geo, w, denv, dwh, dwl, dy, more):
    def step(k):
        cols = lanes(k, 128)
        acc = rows_of(denv, 0)
        wk = w[:, cols]
        rows = [jnp.zeros((1, 128), F32)]
        for c in range(1, 9):
            d = rows_of(denv, c)
            acc = acc + geo[c : c + 1, cols] * d
            rows.append(jnp.sum(wk * d, 0, keepdims=True))
        dwh[:, cols], dwl[:, cols] = split(acc)
        for c in range(1, 9):
            if more is None:
                dy[c : c + 1, cols] = rows[c]
            else:
                dy[c : c + 1, cols] = rows[c] + more[c : c + 1, cols]

    over(8, step)


def early_kernel(
    q1h, q1l, wh, wl, evh, evl, dwh, dwl, columns, geo, z0, dlat, qh, ql, side, da, db
):
    side[...] = jnp.zeros_like(side)

    def product(i, out):
        cols = pl.ds(i * 256, 256)
        out[...] = dot3(
            wh[0:LATENT, :], wl[0:LATENT, :], q1h[:, cols], q1l[:, cols], 1, 0
        ) + dot3(evh[...], evl[...], dwh[:, cols], dwl[:, cols], 0, 0)

    def step(i, ds):
        cols = pl.ds(i * 256, 256)
        sm = geo[9:10, cols] * RH
        gs = geo[24:25, cols] * RH
        total = jnp.zeros((8, 256), F32)
        for b in range(8):
            rows = pl.ds(b * 128, 128)
            dl = ds[rows, :] + columns[:, b : b + 1] * gs
            dlat[rows, cols] = dl * RH
            si, dsi = silu_both(z0[rows, cols])
            qh[rows, cols], ql[rows, cols] = split(dl * dsi * sm)
            total = total + jnp.sum((dl * si).reshape(16, 8, 256), 0)
        side[0:1, cols] = jnp.sum(total, 0, keepdims=True) * RH

    staggered(4, (da, db), product, step)


def couple_kernel(
    qh, ql, wh, wl, vw, geo, g0, g1, ds1, path, dy1,
    dvwh, dvwl, dy, dpath,
    ds0, denv, dyv,
):
    def scal(i):
        cols = lanes(i, 256)
        ds0[:, cols] = dot3(wh[1024:1216, :], wl[1024:1216, :], qh[:, cols], ql[:, cols], 1, 0)

    over(4, scal)
    denv[...] = jnp.zeros_like(denv)
    dpath[...] = jnp.zeros_like(dpath)

    def step(k):
        cols = lanes(k, 128)
        v = vw[0:64, cols]
        y = [geo[c : c + 1, cols] for c in range(9)]
        e = [rows_of(g0, c) for c in range(9)]
        p = [rows_of(path, n) for n in range(9)]
        s = [rows_of(ds0, n, cols) for n in range(3)]
        u = [rows_of(ds1, n, cols) for n in range(3)]
        f0 = u[0] * rows_of(g1, 0)
        fv = [u[1] * rows_of(g1, c) for c in range(1, 4)]
        fq = [u[2] * rows_of(g1, c) for c in range(4, 9)]
        yv, yq, ev_, eq = y[1:4], y[4:9], e[1:4], e[4:9]

        def dot_of(a, b):
            out = a[0] * b[0]
            for i in range(1, len(a)):
                out = out + a[i] * b[i]
            return out

        m00 = HR * yq[0] + SR * yq[1]
        m11 = SR * yq[1] - HR * yq[0]
        m22 = -2.0 * SR * yq[1]
        m01, m02, m12 = HR * yq[2], HR * yq[3], HR * yq[4]
        t00 = HR * fq[0] + SR * fq[1]
        t11 = SR * fq[1] - HR * fq[0]
        t22 = (-2.0 * SR) * fq[1]
        t01, t02, t12 = HR * fq[2], HR * fq[3], HR * fq[4]

        te = [
            t00 * ev_[0] + t01 * ev_[1] + t02 * ev_[2],
            t01 * ev_[0] + t11 * ev_[1] + t12 * ev_[2],
            t02 * ev_[0] + t12 * ev_[1] + t22 * ev_[2],
        ]
        ty = [
            t00 * yv[0] + t01 * yv[1] + t02 * yv[2],
            t01 * yv[0] + t11 * yv[1] + t12 * yv[2],
            t02 * yv[0] + t12 * yv[1] + t22 * yv[2],
        ]
        mf = [
            m00 * fv[0] + m01 * fv[1] + m02 * fv[2],
            m01 * fv[0] + m11 * fv[1] + m12 * fv[2],
            m02 * fv[0] + m12 * fv[1] + m22 * fv[2],
        ]
        ef = [
            ev_[1] * fv[2] - ev_[2] * fv[1],
            ev_[2] * fv[0] - ev_[0] * fv[2],
            ev_[0] * fv[1] - ev_[1] * fv[0],
        ]
        fy = [
            fv[1] * yv[2] - fv[2] * yv[1],
            fv[2] * yv[0] - fv[0] * yv[2],
            fv[0] * yv[1] - fv[1] * yv[0],
        ]
        e_fv = dot_of(ev_, fv)
        y_fv = dot_of(yv, fv)
        e_fq = dot_of(eq, fq)
        y_fq = dot_of(yq, fq)
        vec = dot_of(yv, ev_)
        y_te = dot_of(yv, te)
        e_mf = dot_of(ev_, mf)
        y_ef = dot_of(yv, ef)

        grads = (
            e[0] * f0,
            vec * f0,
            e_fv,
            e[0] * y_fv,
            y_ef,
            e_mf,
            y_te,
            e_fq,
            e[0] * y_fq,
        )
        for n in range(9):
            dpath[n * 64 : (n + 1) * 64, :] += v * grads[n]

        p1f = p[1] * f0
        d0 = s[0] * e[0] + p[0] * e[0] * f0 + p[2] * e_fv + p[7] * e_fq
        p3e = p[3] * e[0]
        p8e = p[8] * e[0]
        s1f = s[1] + p1f
        dv = d0
        for i in range(3):
            di = s1f * ev_[i] + p3e * fv[i] + p[4] * ef[i] + p[6] * te[i]
            dv = dv + yv[i] * di
            dyv[1 + i : 2 + i, cols] = jnp.sum(v * di, 0, keepdims=True)
        a, b, c = fv[0] * ev_[0], fv[1] * ev_[1], fv[2] * ev_[2]
        bil = (
            HR * (a - b),
            SR * (a + b - 2.0 * c),
            HR * (fv[0] * ev_[1] + fv[1] * ev_[0]),
            HR * (fv[0] * ev_[2] + fv[2] * ev_[0]),
            HR * (fv[1] * ev_[2] + fv[2] * ev_[1]),
        )
        for m in range(5):
            dm = s[2] * eq[m] + p[5] * bil[m] + p8e * fq[m]
            dv = dv + yq[m] * dm
            dyv[4 + m : 5 + m, cols] = jnp.sum(v * dm, 0, keepdims=True)
        dvwh[0:64, cols], dvwl[0:64, cols] = split(dv)

        denv[0:64, :] += v * (s[0] + p[0] * f0 + p[3] * y_fv + p[8] * y_fq)
        for i in range(3):
            denv[(1 + i) * 64 : (2 + i) * 64, :] += v * (
                s1f * yv[i] + p[2] * fv[i] + p[4] * fy[i] + p[5] * mf[i] + p[6] * ty[i]
            )
        for m in range(5):
            denv[(4 + m) * 64 : (5 + m) * 64, :] += v * (s[2] * yq[m] + p[7] * fq[m])

    over(8, step)
    for c in range(9):
        denv[c * 64 : (c + 1) * 64, :] = slot_total(rows_of(denv, c)) * NORM
    dyv[0:1, :] = jnp.zeros((1, EDGES), F32)
    dyv[...] += dy1[...]
    env_back(geo, vw.at[64:128, :], denv, dvwh.at[64:128, :], dvwl.at[64:128, :], dy, dyv)


def pre_kernel(
    half, qh, ql, wh, wl, veh, vel, dvwh, dvwl, dl, table, cent, geo, rad_w,
    qph, qpl, side, drad, da, db, pre,
):
    base = half * HALF
    wr = slice(base, base + HALF)
    rwh, rwl = split(jnp.concatenate([rad_w[:, wr], jnp.zeros((8, HALF), F32)], 0))
    side[...] = jnp.zeros_like(side)

    def product(i, out):
        cols = pl.ds(i * 256, 256)
        out[...] = dot3(wh[wr, :], wl[wr, :], qh[:, cols], ql[:, cols], 1, 0) + dot3(
            veh[:, wr], vel[:, wr], dvwh[:, cols], dvwl[:, cols], 0, 0
        )

    def step(i, ds):
        cols = pl.ds(i * 256, 256)
        sm = geo[9:10, cols]
        total = jnp.zeros((8, 256), F32)
        pre[...] = dot(table[:, wr], embed_inputs(cent, geo, cols), 0, 0)
        for b in range(4):
            rows = pl.ds(b * 128, 128)
            dd = ds[rows, :] + dl[pl.ds(base + b * 128, 128), cols]
            si, dsi = silu_both(pre[rows, :])
            qph[rows, cols], qpl[rows, cols] = split(dd * dsi * sm)
            total = total + jnp.sum((dd * si).reshape(16, 8, 256), 0)
        side[0:1, cols] = jnp.sum(total, 0, keepdims=True)
        drad[:, cols] = dot3(rwh, rwl, qph[:, cols], qpl[:, cols], 1, 0)[0:8]

    staggered(4, (da, db), product, step)


def last_kernel(
    rows_y, rows_z, place, qps, sides, drads, geo, slots, cent, sl, se, dy,
    dpath, columns, dout, more,
    small_keep, small_send, energy,
    ghost, small, spread,
):
    kinds = iota((NSPEC, EDGES), 0).astype(F32)
    hot_c = jnp.where(kinds == cent[3:4, :], 1.0, 0.0)
    hot_n = jnp.where(kinds == geo[25:26, :], 1.0, 0.0)
    hots = jnp.concatenate([hot_c, hot_n], 0).astype(BF16)
    rad = geo[16:24, :]
    rad_h = rad.astype(BF16).astype(F32)
    rads = jnp.concatenate([rad_h, rad - rad_h], 0).astype(BF16)
    left = jnp.concatenate([hots, rads], 0)
    for n, (qh, ql) in enumerate(zip(qps[0::2], qps[1::2])):
        full = dot(left, qh[...], 1, 1)
        rest = dot(left, ql[...], 1, 1)
        part = slice(n * HALF, (n + 1) * HALF)
        small[0:128, part] = full[0:128] + rest[0:128]
        small[128:136, part] = full[128:136] + full[136:144] + rest[128:136]

    live, r, smooth = geo[10:11, :], geo[11:12, :], geo[9:10, :]
    inv = 1.0 / r
    grad = geo[15:16, :]
    reach = sl[0:1, :]
    lat_out = sl[1:2, :]
    order = (iota((8, EDGES), 0) + 1).astype(F32) * (math.pi / CUTOFF)
    angle = order * r
    sine = jnp.sin(angle) * inv
    cosine = jnp.cos(angle) * inv
    dr8 = drads[0][...] + drads[1][...]
    d_s = (
        grad * lat_out
        + grad * smooth * RH * reach
        + se[0:1, :]
        + sides[0][0:1, :]
        + sides[1][0:1, :]
        + BESSEL * jnp.sum(dr8 * sine, 0, keepdims=True)
    )
    t = r / CUTOFF
    t2 = t * t
    gap = 1.0 - t
    d_r = d_s * (live * (-168.0 / CUTOFF) * (t2 * t2 * t) * (gap * gap)) + (
        smooth * BESSEL
    ) * jnp.sum(dr8 * (order * cosine - sine * inv), 0, keepdims=True)
    ux, uy, uz = geo[12:13, :] * inv, geo[13:14, :] * inv, geo[14:15, :] * inv
    yy = [dy[c : c + 1, :] for c in range(9)]
    h2, s2 = 2.0 * HR * Q75, 2.0 * SR * Q75
    gx = R3 * yy[1] + ux * (h2 * yy[4] + s2 * yy[5]) + h2 * (uy * yy[6] + uz * yy[7])
    gy = R3 * yy[2] + uy * (s2 * yy[5] - h2 * yy[4]) + h2 * (ux * yy[6] + uz * yy[8])
    gz = R3 * yy[3] - 2.0 * s2 * uz * yy[5] + h2 * (ux * yy[7] + uy * yy[8])
    along = ux * gx + uy * gy + uz * gz
    zero = jnp.zeros((5, EDGES), F32)
    disp = jnp.concatenate(
        [
            live * ((gx - ux * along) * inv + ux * d_r),
            live * ((gy - uy * along) * inv + uy * d_r),
            live * ((gz - uz * along) * inv + uz * d_r),
            zero,
        ],
        0,
    )
    hi, mid, lo = pieces(disp)
    disp24 = jnp.concatenate([hi, mid, lo], 0).astype(BF16)
    acc = None
    mine = None
    for k in range(8):
        term = disp[:, k * 128 : (k + 1) * 128]
        mine = term if mine is None else mine + term
    mine = slot_total(mine)
    for i in range(4):
        cols = pl.ds(i * 256, 256)
        hot = jnp.where(iota((NTAB, 256), 0) == slots[:, cols], 1.0, 0.0).astype(BF16)
        term = dot(disp24[:, i * 256 : (i + 1) * 256], hot, 1, 1)
        acc = term if acc is None else acc + term
    ghost[...] = acc[0:8] + acc[8:16] + acc[16:24]
    lane = iota((8, 128), 1)
    middle = ghost[:, 512:640] - jnp.where(
        (lane >= ATOMS) & (lane < 2 * ATOMS), pltpu.roll(mine, ATOMS, 1), 0.0
    )
    ghost[:, 512:640] = middle
    atoms = spread.shape[1]
    spread[...] = jnp.zeros_like(spread)
    total = jnp.zeros_like(spread)
    for bx in range(3):
        for by in range(3):
            block = 3 * bx + by
            spread[:, 0:128] = ghost[:, block * 128 : (block + 1) * 128]
            start = place[4] + ((bx - 1) * rows_y + by - 1) * rows_z * ATOMS - ATOMS
            total = total + pltpu.roll(spread[...], lax.rem(start + 2 * atoms, atoms), 1)
    for n in range(atoms // LATENT):
        small[144 + 8 * n : 152 + 8 * n, :] = total[:, n * LATENT : (n + 1) * LATENT]

    edge_energy = smooth * lat_out
    total = None
    for k in range(8):
        term = edge_energy[:, k * 128 : (k + 1) * 128]
        total = term if total is None else total + term
    total = slot_total(jnp.broadcast_to(total, (8, 128)))[0:1]
    hot = jnp.where(iota((NSPEC, 128), 0).astype(F32) == cent[3:4, 0:128], 1.0, 0.0)
    energy[...] = jnp.broadcast_to(
        jnp.sum(hot * columns[0:64, 8:9], 0, keepdims=True) * total
        + jnp.sum(hot * columns[0:64, 9:10], 0, keepdims=True),
        energy.shape,
    )
    cot = cent[4:5, 0:128] * jnp.where(iota((1, 128), 1) < ATOMS, 1.0, 0.0)
    stack = jnp.concatenate(
        [dpath[...], hot * (cot * total), hot * cot, jnp.zeros((64, 128), F32)], 0
    )
    row = jnp.sum(stack.T, 0, keepdims=True)
    small[136:144, :] = jnp.zeros((8, LATENT), F32)
    small[136:137, 0:768] = row
    small[137:138, :] = dout[0:1, :]
    mine = pl.ds(pl.multiple_of(place[3] * HALF, HALF), HALF)
    other = pl.ds(pl.multiple_of((1 - place[3]) * HALF, HALF), HALF)
    for out, cols in ((small_keep, mine), (small_send, other)):
        out[0:192, :] = more[:, cols]
        out[192:, :] = small[:, cols]


def weights_kernel(dvwh, dvwl, x0h, x0l, dw1h, dw1l, x1h, x1l, out):
    out[0:128, :] = dot3(dvwh[...], dvwl[...], x0h[0:LATENT, :], x0l[0:LATENT, :], 1, 1)
    out[128:192, :] = dot3(dw1h[...], dw1l[...], x1h[0:LATENT, :], x1l[0:LATENT, :], 1, 1)


def halves(shape, dim):
    rows, cols = shape
    return (rows // 2, cols) if dim == 0 else (rows, cols // 2) if dim == 1 else shape


def half_of(shape, dim, bit):
    rows, cols = shape
    if dim == 0:
        rows //= 2
        return pl.ds(pl.multiple_of(bit * rows, 8), rows), slice(None)
    cols //= 2
    return slice(None), pl.ds(pl.multiple_of(bit * cols, 128), cols)


def down_kernel(dim, flag, place, keep, got, *outs):
    if dim is None:
        outs[0][...] = keep[...] + got[...]
        return
    for out, bit in zip(outs, (1 - place[flag], place[flag])):
        index = half_of(keep.shape, dim, bit)
        out[...] = keep[index] + got[index]


def up_kernel(dim, flag, place, mine, got, out):
    out[half_of(out.shape, dim, place[flag])] = mine[...]
    out[half_of(out.shape, dim, 1 - place[flag])] = got[...]


def end_kernel(parts, place, *refs):
    srcs, out, sem = refs[: len(parts)], refs[-2], refs[-1]
    copies = []
    for n, ((layer, start, mine), src) in enumerate(zip(parts, srcs)):
        block = place[3] if mine else 1 - place[3]
        cols = pl.ds(pl.multiple_of(block * HALF, HALF), HALF)
        rows = pl.ds(start, src.shape[0])
        copies.append(pltpu.make_async_copy(src, out.at[layer, rows, cols], sem.at[n]))
    for copy in copies:
        copy.start()
    for copy in copies:
        copy.wait()


def small_end_kernel(
    core_at, place, mine, got, energy,
    center, neigh, radial, value, env, path, out, scale, shift, grad, energies,
):
    for src, b in ((mine, place[core_at]), (got, 1 - place[core_at])):
        cols = pl.ds(pl.multiple_of(b * HALF, HALF), HALF)
        value[:, cols] = src[0:64, :]
        env[0, :, cols] = src[64:128, :]
        env[1, :, cols] = src[128:192, :]
        center[:, cols] = src[192:256, :]
        neigh[:, cols] = src[256:320, :]
        radial[:, cols] = src[320:328, :]
    is_first = place[core_at] == 0

    def whole(rows):
        first = jnp.where(is_first, mine[rows, :], got[rows, :])
        second = jnp.where(is_first, got[rows, :], mine[rows, :])
        return jnp.concatenate([first, second], 1)

    base = 336 + 8 * (place[4] // LATENT)
    spread = whole(pl.ds(pl.multiple_of(base, 8), 8))
    shift_by = LATENT - lax.rem(place[4], LATENT)
    grad[...] = pltpu.roll(spread, lax.rem(shift_by, LATENT), 1)[0:3, 0:ATOMS]
    energies[...] = energy[0:1, 0:ATOMS]
    row = whole(slice(328, 336))
    for n in range(9):
        path[n : n + 1, :] = row[0:1, n * 64 : (n + 1) * 64]
    scale[...] = row[0:1, 576:640]
    shift[...] = row[0:1, 640:704]
    for n in range(8):
        out[n : n + 1, :] = row[1:2, n * 128 : (n + 1) * 128]


VSPEC = pl.BlockSpec(memory_space=pltpu.VMEM)
SSPEC = pl.BlockSpec(memory_space=pltpu.SMEM)
ASPEC = pl.BlockSpec(memory_space=pl.ANY)
HSPEC = pl.BlockSpec(memory_space=pltpu.HBM)


PROGRAM = (
    "late", "send_a", "keep_a", "mid", "a", "early", "send_c", "a", "keep_c", "c",
    "a", "couple", "a", "pre0", "c", "a", "weights", "a", "pre1", "c",
    "a", "last", "c", "free", "a", "a", "a", "a", "end_a", "c",
    "s", "c", "s", "c", "s", "s", "c", "c", "s", "s",
    "s", "end_s", "c",
)


COST = {
    "late": 6.5, "send_a": 4.6, "keep_a": 0.57, "mid": 3, "early": 5.0, "send_c": 4.6,
    "keep_c": 4.6, "couple": 25.2, "weights": 4, "pre0": 3.5, "pre1": 3.5, "last": 5,
    "land_a": 8, "land_c": 2, "land_s": 3.0,
}


class Order:
    def __init__(self):
        self.token = None
        self.free = False
        self.extra = ()

    def __call__(
        self, body, outs, args, scratch=(), scalar=False, hbm=(), plain=False, alias=None, us=1,
        limit=6, name=None, mark=False,
    ):
        specs = [HSPEC if n in hbm else VSPEC for n in range(len(args))]
        if scalar:
            specs[0] = SSPEC
        count, given = len(args), len(outs)
        marked = mark or not self.free
        tokens = () if self.token is None or self.free else (self.token,)
        tokens, self.extra = tokens + self.extra, ()

        def kernel(*refs):
            after = refs[count + len(tokens) :]
            if not marked:
                return body(*refs[:count], *after)
            after[given][...] = jnp.zeros((8, 128), F32)
            body(*refs[:count], *after[:given], *after[given + 1 :])

        if plain:
            shapes = [jax.ShapeDtypeStruct(shape, dtype) for shape, dtype in outs]
        else:
            shapes = [pltpu.VMEM(shape, dtype) for shape, dtype in outs]
        out_spec = HSPEC if plain == "hbm" else VSPEC
        got = pl.pallas_call(
            kernel,
            name=name or getattr(body, "func", body).__name__,
            out_shape=shapes + ([pltpu.VMEM((8, 128), F32)] if marked else []),
            in_specs=specs + [ASPEC] * len(tokens),
            out_specs=[out_spec] * given + ([VSPEC] if marked else []),
            scratch_shapes=list(scratch),
            input_output_aliases=alias or {},
            compiler_params=pltpu.CompilerParams(vmem_limit_bytes=limit << 20),
            cost_estimate=pl.CostEstimate(
                flops=int(us * 3e9), bytes_accessed=1 << 20, transcendentals=0
            ),
        )(*args, *tokens)
        if not marked:
            return got
        self.token = got[-1]
        return got[:-1]


def is_up(axis, bit):
    return (lax.axis_index(axis) // bit) & 1


def even_pairs(axis):
    return [(i, i ^ 1) for i in range(lax.axis_size(axis))]


def odd_pairs(axis):
    count = lax.axis_size(axis)
    return [p for i in range(1, count - 1, 2) for p in ((i, i + 1), (i + 1, i))]


def neighbours_of(axis, even, odd):
    pairs = odd_pairs(axis)
    return (
        lax.ppermute(even, axis, even_pairs(axis)),
        lax.ppermute(odd, axis, pairs) if pairs else jnp.zeros_like(odd),
    )


class Route:
    def __init__(self, mesh_sizes, base, tall_first=False):
        sizes = dict(mesh_sizes)
        names = list(sizes)

        def bits(axis, least=1):
            return [(axis, 1 << n) for n in range(20) if least <= 1 << n < sizes[axis]]

        flat, tall = bits("gx"), bits("gy") + bits("gz", 2)
        first = [("gz", 1)]
        one, two = (flat, tall), (flat[::-1], tall)
        if tall_first:
            one, two = one[::-1], two[::-1]
        self.steps = list(zip(first + one[0] + one[1], first + two[0] + two[1]))
        self.count = len(self.steps)
        self.base = base
        self.names = tuple(names)
        coords = [()]
        for name in names:
            coords = [c + (i,) for c in coords for i in range(sizes[name])]
        index = {c: n for n, c in enumerate(coords)}
        self.pairs = []
        for step in self.steps:
            pairs = []
            for c in coords:
                axis, bit = step[c[names.index("gz")] & 1]
                at = names.index(axis)
                pairs.append((index[c], index[c[:at] + (c[at] ^ bit,) + c[at + 1 :]]))
            self.pairs.append(pairs)

    def flags(self):
        core = is_up("gz", 1)
        return [jnp.where(core == 1, is_up(*two), is_up(*one)) for one, two in self.steps]

    def swap(self, x, at):
        return lax.ppermute(x, self.names, self.pairs[at])


class Sum:
    def __init__(self, name, order, place, route, send, dims):
        self.name = name
        self.order, self.place, self.route = order, place, route
        self.dims = (1,) + dims + (None,) * (route.count - 1 - len(dims))
        self.keep, self.send = None, send
        self.at, self.rising = 0, False
        self.shapes = []
        self.launch()

    def launch(self):
        with jax.named_scope(f"sum_{self.name}_{'up' if self.rising else 'down'}_{self.at}"):
            self.got = self.route.swap(self.send, self.at)

    @property
    def over(self):
        return self.rising and self.at == 0

    def land(self):
        (self.climb if self.rising else self.descend)()
        self.launch()

    def call(self, body, dim, flag, shapes, args):
        return self.order(
            functools.partial(body, dim, flag),
            [(shape, F32) for shape in shapes],
            (self.place, *args),
            scalar=True,
            us=COST[f"land_{self.name}"],
            name=f"land_{self.name}_{'up' if self.rising else 'down'}_{self.at}",
        )

    def descend(self):
        self.shapes.append(self.keep.shape)
        self.at += 1
        last = self.at == self.route.count
        dim = None if last else self.dims[self.at]
        shapes = [halves(self.keep.shape, dim)] * (1 if dim is None else 2)
        outs = self.call(
            down_kernel, dim, self.route.base + self.at, shapes, (self.keep, self.got)
        )
        self.send, self.keep = outs[0], outs[-1]
        if last:
            self.rising = True
            self.rise()

    def rise(self):
        self.at -= 1
        while self.at > 0 and self.dims[self.at] is None:
            self.at -= 1

    def climb(self):
        (self.send,) = self.call(
            up_kernel,
            self.dims[self.at],
            self.route.base + self.at,
            [self.shapes[self.at - 1]],
            (self.send, self.got),
        )
        self.rise()


def per_device(
    positions,
    species,
    neighbours,
    embed_center,
    embed_neigh,
    embed_radial,
    value_proj,
    env_weight,
    latent_weight,
    path_weight,
    out_weight,
    scale_table,
    shift_table,
    cotangent,
):
    vm, sem = pltpu.VMEM, pltpu.SemaphoreType
    order = Order()
    sizes = [(axis, lax.axis_size(axis)) for axis in ("gx", "gy", "gz")]
    route = Route(sizes, 5)
    steep = Route(sizes, 5 + route.count, tall_first=True)
    first_atom = lax.axis_index(("gx", "gy", "gz")) * ATOMS
    place = [is_up("gz", 1), is_up("gy", 1), is_up("gx", 1), is_up("gz", 1), first_atom]
    place = jnp.stack(place + route.flags() + steep.flags()).astype(jnp.int32)
    spec_row = species.reshape(1, ATOMS)

    (table,) = order(pack_kernel, [((8, 128), F32)], (positions, spec_row), us=1)
    even, odd = neighbours_of("gz", table, table)
    (table,) = order(
        join_z_kernel, [((8, 128), F32)], (place, table, even, odd), scalar=True, us=1
    )
    even, odd = neighbours_of("gy", table, table)
    (table,) = order(
        join_y_kernel,
        [((8, 384), F32)],
        (place, table, even, odd),
        scalar=True,
        us=1,
    )
    even, odd = neighbours_of("gx", table, table)

    wide = ((WIDE, EDGES), BF16)
    half = ((HALF, EDGES), BF16)
    row64 = ((64, LATENT), BF16)
    row128 = ((128, LATENT), BF16)
    w0h, w0l, w1h, w1l, hots, veh, vel, evh, evl, path, columns, slots, cent, rad_w = order(
        prep_kernel,
        [
            wide, wide, wide, wide, ((288, LATENT), BF16), row128, row128, row64, row64,
            ((576, 128), F32), ((128, 128), F32), ((1, EDGES), jnp.int32), ((8, EDGES), F32),
            ((8, LATENT), F32),
        ],
        (latent_weight, embed_center, embed_neigh, embed_radial, value_proj.T,
         jnp.swapaxes(env_weight, 1, 2), neighbours, positions, spec_row,
         cotangent.reshape(1, ATOMS), path_weight, out_weight.reshape(8, 128),
         scale_table.reshape(1, NSPEC), shift_table.reshape(1, NSPEC)),
        [
            vm((NSPEC, LATENT), F32), vm((NSPEC, LATENT), F32), vm((CHANNELS, LATENT), F32),
            vm((2, CHANNELS, LATENT), F32), vm((NB, ATOMS), jnp.int32), vm((3, ATOMS), F32),
            vm((1, ATOMS), jnp.int32), vm((1, ATOMS), F32), vm((9, CHANNELS), F32),
            vm((8, 128), F32), vm((1, NSPEC), F32), vm((1, NSPEC), F32), vm((128, 128), F32),
            sem.DMA((13,)),
        ],
        hbm=range(1, 14),
        us=4,
    )

    x0h, x0l, x1h, x1l, z0, vw, w1, geo, g0, g1, f1 = order(
        fwd_kernel,
        [
            wide, wide, wide, wide,
            ((LATENT, EDGES), F32), ((128, EDGES), F32), ((64, EDGES), F32), ((G_ROWS, EDGES), F32), ((576, 128), F32), ((576, 128), F32),
            ((576, EDGES), F32),
        ],
        (place, table, even, odd, slots, cent, w0h, w0l, hots, veh, vel, evh, evl, path, columns),
        [vm((8, EDGES), F32), vm((LATENT, 256), F32), vm((LATENT, 256), F32)],
        scalar=True,
        us=22,
        limit=18,
    )

    chains = {}

    def grad(mine, cost, xh, xl, qh, ql):
        return order(
            functools.partial(grad_kernel, mine),
            [((WIDE, HALF), F32)],
            (place, xh, xl, qh, ql),
            scalar=True,
            us=cost,
        )[0]

    def send(name, *args):
        chains[name] = Sum(name, order, place, route, grad(False, COST[f"send_{name}"], *args), (0, 0, 0, 1))

    def keep(name, *args):
        chains[name].keep = grad(True, COST[f"keep_{name}"], *args)

    def late():
        return order(
            late_kernel,
            [
                ((LATENT, EDGES), BF16), ((LATENT, EDGES), BF16), ((8, EDGES), F32),
                ((8, LATENT), F32),
            ],
            (x1h, x1l, w1h, w1l, columns, geo),
            [vm((LATENT, 128), F32), vm((LATENT, 256), F32), vm((LATENT, 256), F32)],
            us=COST["late"],
            limit=17,
        )

    def mid():
        return order(
            mid_kernel,
            [((192, EDGES), F32), ((64, EDGES), BF16), ((64, EDGES), BF16), ((16, EDGES), F32)],
            (v.q1h, v.q1l, w1h, w1l, f1, g1, w1, geo),
            [vm((576, 128), F32)],
            us=COST["mid"],
        )

    def early():
        return order(
            early_kernel,
            [
                ((LATENT, EDGES), F32), ((LATENT, EDGES), BF16), ((LATENT, EDGES), BF16),
                ((8, EDGES), F32),
            ],
            (v.q1h, v.q1l, w1h, w1l, evh, evl, v.dw1h, v.dw1l, columns, geo, z0),
            [vm((LATENT, 256), F32), vm((LATENT, 256), F32)],
            us=COST["early"],
            limit=12,
        )

    def couple():
        return order(
            couple_kernel,
            [
                ((128, EDGES), BF16), ((128, EDGES), BF16), ((16, EDGES), F32),
                ((576, 128), F32),
            ],
            (v.q0h, v.q0l, w0h, w0l, vw, geo, g0, g1, v.ds1, path, v.dy1),
            [vm((192, EDGES), F32), vm((576, 128), F32), vm((16, EDGES), F32)],
            us=COST["couple"],
        )

    def before(h):
        return order(
            functools.partial(pre_kernel, h),
            [half, half, ((8, EDGES), F32), ((8, EDGES), F32)],
            (v.q0h, v.q0l, w0h, w0l, veh, vel, v.dvwh, v.dvwl, v.dlat, hots, cent, geo, rad_w),
            [vm((HALF, 256), F32), vm((HALF, 256), F32), vm((HALF, 256), F32)],
            us=COST[f"pre{h}"],
        )

    def run_late():
        v.q1h, v.q1l, v.sl, v.dout = late()

    def run_mid():
        v.ds1, v.dw1h, v.dw1l, v.dy1 = mid()

    def run_early():
        v.dlat, v.q0h, v.q0l, v.se = early()

    def run_couple():
        v.dvwh, v.dvwl, v.dy, v.dpath = couple()

    def run_weights():
        (v.more,) = order(
            weights_kernel,
            [((192, LATENT), F32)],
            (v.dvwh, v.dvwl, x0h, x0l, v.dw1h, v.dw1l, x1h, x1l),
            us=COST["weights"],
        )

    def run_last():
        atoms = ATOMS * math.prod(size for _, size in sizes)
        height = 144 + 8 * (atoms // LATENT)
        (ah, al, side_a, drad_a), (bh, bl, side_b, drad_b) = v.pres
        keep, send, v.energy = order(
            lambda place, *refs: last_kernel(
                sizes[1][1], sizes[2][1], place, refs[0:4], refs[4:6], refs[6:8], *refs[8:]
            ),
            [((192 + height, HALF), F32), ((192 + height, HALF), F32), ((8, 128), F32)],
            (place, ah, al, bh, bl, side_a, side_b, drad_a, drad_b, geo, slots, cent, v.sl, v.se,
             v.dy, v.dpath, columns, v.dout, v.more),
            [vm((8, NTAB), F32), vm((height, LATENT), F32), vm((8, atoms), F32)],
            scalar=True,
            us=COST["last"],
            name="last_kernel",
        )
        chains["s"] = Sum("s", order, place, route, send, (1, 1))
        chains["s"].keep = keep

    def finish(parts, arrays, mark=False):
        last = 1 + len(arrays)
        done = () if v.d_latent is None else (v.d_latent,)
        (v.d_latent,) = order(
            functools.partial(end_kernel, parts),
            [((2, WIDE, LATENT), F32)],
            (place, *arrays, *done),
            [sem.DMA((len(parts),))],
            scalar=True,
            hbm=(last,) if done else (),
            plain="hbm",
            alias={last: 0} if done else None,
            us=3,
            mark=mark,
        )

    def finish_small():
        s = chains["s"]
        v.small = order(
            functools.partial(small_end_kernel, 3),
            [
                ((NSPEC, LATENT), F32), ((NSPEC, LATENT), F32), ((NBESSEL, LATENT), F32),
                ((CHANNELS, LATENT), F32), ((2, CHANNELS, LATENT), F32), ((9, CHANNELS), F32),
                ((8, 128), F32), ((1, NSPEC), F32), ((1, NSPEC), F32), ((3, ATOMS), F32),
                ((1, ATOMS), F32),
            ],
            (place, s.send, s.got, v.energy),
            scalar=True,
            plain=True,
            us=2,
        )

    def land(name):
        chain = chains[name]
        if chain.over:
            return
        if name == "c" and chain.rising and chain.at == 1 and v.d_latent is not None:
            order.extra = (order.token,)
        chain.land()

    def settle(name):
        while not chains[name].over:
            land(name)

    def finish_a():
        settle("a")
        finish(((1, 0, True), (1, 0, False)), (chains["a"].send, chains["a"].got), mark=True)

    def finish_s():
        settle("s")
        finish_small()

    def set_free():
        order.free = True

    def set_bound():
        order.free = False

    v = types.SimpleNamespace(d_latent=None, pres=[])
    steps = {
        "late": run_late,
        "mid": run_mid,
        "early": run_early,
        "couple": run_couple,
        "weights": run_weights,
        "pre0": lambda: v.pres.append(before(0)),
        "pre1": lambda: v.pres.append(before(1)),
        "last": run_last,
        "send_a": lambda: send("a", x1h, x1l, v.q1h, v.q1l),
        "keep_a": lambda: keep("a", x1h, x1l, v.q1h, v.q1l),
        "send_c": lambda: send("c", x0h, x0l, v.q0h, v.q0l),
        "keep_c": lambda: keep("c", x0h, x0l, v.q0h, v.q0l),
        "a": lambda: land("a"),
        "c": lambda: land("c"),
        "s": lambda: land("s"),
        "free": set_free,
        "bind": set_bound,
        "end_a": finish_a,
        "end_s": finish_s,
    }
    for step in PROGRAM:
        steps[step]()
    settle("c")
    c = chains["c"]
    finish(((0, 0, True),), (c.send,))
    finish(((0, 0, False),), (c.got,))
    (center, neigh, radial, value, env, path_grad, out, scale, shift, position_grad,
     energies) = v.small
    d_latent = v.d_latent
    return (
        energies.reshape(ATOMS),
        position_grad,
        center,
        neigh,
        radial,
        value.T,
        jnp.swapaxes(env, 1, 2),
        d_latent,
        path_grad,
        out.reshape(LATENT),
        scale.reshape(NSPEC),
        shift.reshape(NSPEC),
    )


def solution(mesh):
    everything = ("gx", "gy", "gz")
    return jax.shard_map(
        per_device,
        mesh=mesh,
        in_specs=(
            P(None, everything),
            P(everything),
            P(None, everything),
            P(),
            P(),
            P(),
            P(),
            P(),
            P(),
            P(),
            P(),
            P(),
            P(),
            P(everything),
        ),
        out_specs=(
            P(everything),
            P(None, everything),
            P(),
            P(),
            P(),
            P(),
            P(),
            P(),
            P(),
            P(),
            P(),
            P(),
        ),
        check_vma=False,
    )
```

```python
import functools
import math
import types

import jax
import jax.numpy as jnp
import numpy as np
from jax import lax
from jax.experimental import pallas as pl
from jax.experimental.pallas import tpu as pltpu
from jax.sharding import PartitionSpec as P

LATENT = 1024
CHANNELS = 64
NSPEC = 64
NBESSEL = 8
NB = 32
ATOMS = 32
EDGES = NB * ATOMS
WIDE = LATENT + 3 * CHANNELS
HALF = LATENT // 2
QUARTER = LATENT // 4
NTAB = 9 * 128
OWN = 4 * 128 + ATOMS

CUTOFF = 5.0
RH = 0.7071067811865476
HR = 0.7071067811865476
SR = 0.4082482904638631
R3 = math.sqrt(3.0)
Q75 = math.sqrt(7.5)
NORM = NB**-0.5
BESSEL = math.sqrt(2.0 / CUTOFF)

F32 = jnp.float32
BF16 = jnp.bfloat16

G_SMOOTH, G_LIVE, G_R, G_DISP, G_GRAD, G_RAD, G_GS, G_SPEC = 9, 10, 11, 12, 15, 16, 24, 25
G_ROWS = 32


def dot(a, b, ca, cb):
    return lax.dot_general(a, b, (((ca,), (cb,)), ((), ())), preferred_element_type=F32)


def dot3(ah, al, bh, bl, ca, cb):
    return dot(ah, bh, ca, cb) + dot(ah, bl, ca, cb) + dot(al, bh, ca, cb)


def split(x):
    hi = x.astype(BF16)
    return hi, (x - hi.astype(F32)).astype(BF16)


def pieces(x):
    hi = x.astype(BF16).astype(F32)
    rest = x - hi
    mid = rest.astype(BF16).astype(F32)
    return hi, mid, rest - mid


def sigmoid(x):
    return 0.5 * jnp.tanh(0.5 * x) + 0.5


def silu_both(x):
    sig = sigmoid(x)
    return x * sig, sig * (1.0 + x * (1.0 - sig))


def lanes(i, width):
    return pl.ds(pl.multiple_of(i * width, width), width)


def over(count, body):
    def step(i, carry):
        body(i)
        return carry

    lax.fori_loop(0, count, step, 0)


def staggered(count, bufs, first, second):
    first(0, bufs[0])
    for i in range(count):
        if i + 1 < count:
            first(i + 1, bufs[(i + 1) % 2])
        second(i, bufs[i % 2])


def iota(shape, dim):
    return lax.broadcasted_iota(jnp.int32, shape, dim)


def slot_total(x):
    x = x + pltpu.roll(x, 64, 1)
    return x + pltpu.roll(x, 32, 1)


def make_env(geo, w, env):
    for c in range(9):
        acc = None
        for k in range(8):
            cols = pl.ds(k * 128, 128)
            term = w[:, cols] if c == 0 else geo[c : c + 1, cols] * w[:, cols]
            acc = term if acc is None else acc + term
        env[c * 64 : (c + 1) * 64, :] = slot_total(acc) * NORM


def rows_of(ref, c, cols=slice(None)):
    return ref[c * 64 : (c + 1) * 64, cols]


def pack_kernel(pos, spec, out):
    out[...] = jnp.zeros_like(out)
    out[0:3, 0:ATOMS] = pos[...]
    out[3:4, 0:ATOMS] = spec[...].astype(F32)


def join_z_kernel(place, own, even_in, odd_in, out):
    is_odd = place[0] == 1
    left = jnp.where(is_odd, even_in[...], odd_in[...])
    right = jnp.where(is_odd, odd_in[...], even_in[...])
    out[...] = left + pltpu.roll(own[...], ATOMS, 1) + pltpu.roll(right, 2 * ATOMS, 1)


def join_y_kernel(place, own, even_in, odd_in, out):
    is_odd = place[1] == 1
    out[:, 0:128] = jnp.where(is_odd, even_in[...], odd_in[...])
    out[:, 128:256] = own[...]
    out[:, 256:384] = jnp.where(is_odd, odd_in[...], even_in[...])


def prep_kernel(
    w, ec_in, en_in, rad_in, vp_in, env_in, neigh_in, pos_in, spec_in, cot_in, path_in, outw_in,
    scale_in, shift_in,
    w0h, w0l, w1h, w1l, table, veh, vel, evh, evl, path_b, cols, slots, cent, rad_w,
    ec, en, vp, env, neigh, pos, spec, cot, path, outw, scale, shift, square, sem,
):
    pairs = (
        (ec_in, ec), (en_in, en), (rad_in, rad_w), (vp_in, vp), (env_in, env), (neigh_in, neigh),
        (pos_in, pos), (spec_in, spec), (cot_in, cot), (path_in, path), (outw_in, outw),
        (scale_in, scale), (shift_in, shift),
    )
    copies = [
        pltpu.make_async_copy(src, dst, sem.at[n]) for n, (src, dst) in enumerate(pairs)
    ]
    for copy in copies:
        copy.start()

    for layer, (hi, lo) in enumerate(((w0h, w0l), (w1h, w1l))):

        def part(i, layer=layer, hi=hi, lo=lo):
            rows = pl.ds(pl.multiple_of(i * 64, 64), 64)
            hi[rows, :], lo[rows, :] = split(w[layer, rows, :])

        over(WIDE // 64, part)
    for copy in copies:
        copy.wait()

    ech, ecl = split(ec[...])
    enh, enl = split(en[...])
    rh = rad_w[...].astype(BF16).astype(F32)
    rl = rad_w[...] - rh
    table[0:64, :] = ech
    table[64:128, :] = enh
    table[128:192, :] = ecl
    table[192:256, :] = enl
    table[256:288, :] = jnp.concatenate([rh, rl, rh, jnp.zeros_like(rh)], 0).astype(BF16)
    veh[0:64, :], vel[0:64, :] = split(vp[...])
    veh[64:128, :], vel[64:128, :] = split(env[0])
    evh[...], evl[...] = split(env[1])

    square[...] = jnp.zeros_like(square)
    square[0:8, :] = outw[...]
    square[8:9, 0:64] = scale[...]
    square[9:10, 0:64] = shift[...]
    square[16:25, 0:64] = path[...]
    turned = square[...].T
    cols[...] = turned
    for n in range(9):
        path_b[n * 64 : (n + 1) * 64, :] = jnp.broadcast_to(
            turned[0:64, 16 + n : 17 + n], (64, 128)
        )

    square[0:32, :] = jnp.zeros((32, 128), F32)
    square[0:32, 0:ATOMS] = neigh[...].astype(F32)
    row = square[pl.ds(0, 8, 4), :]
    for i in range(1, 4):
        row = row + pltpu.roll(square[pl.ds(i, 8, 4), :], i * ATOMS, 1)
    padded = row
    for m in range(1, 9):
        padded = padded + jnp.where(row >= 96.0 * m, 32.0, 0.0)
    padded = padded.astype(jnp.int32)
    square[0:8, :] = jnp.zeros((8, 128), F32)
    square[0:3, 0:ATOMS] = pos[...]
    square[3:4, 0:ATOMS] = spec[...].astype(F32)
    square[4:5, 0:ATOMS] = cot[...]
    own = square[0:8, :]
    own = own + pltpu.roll(own, 32, 1)
    own = own + pltpu.roll(own, 64, 1)
    for k in range(8):
        slots[:, k * 128 : (k + 1) * 128] = padded[k : k + 1]
        cent[:, k * 128 : (k + 1) * 128] = own


def embed_inputs(cent, geo, cols):
    kinds = iota((NSPEC, 256), 0).astype(F32)
    hot_c = jnp.where(kinds == cent[3:4, cols], 1.0, 0.0)
    hot_n = jnp.where(kinds == geo[25:26, cols], 1.0, 0.0)
    hots = jnp.concatenate([hot_c, hot_n], 0).astype(BF16)
    rad = geo[16:24, cols]
    rad_h = rad.astype(BF16).astype(F32)
    rads = jnp.concatenate([rad_h, rad_h, rad - rad_h, jnp.zeros_like(rad)], 0).astype(BF16)
    return jnp.concatenate([hots, hots, rads], 0)


def fwd_kernel(
    place, tab, even_in, odd_in, slots, cent, w0h, w0l, table, veh, vel, evh, evl, path, columns,
    x0h, x0l, x1h, x1l, z0, vw, w1, geo, g0, g1, f1,
    gat, za, zb,
):
    is_odd = place[2] == 1
    whole = jnp.concatenate(
        [
            jnp.where(is_odd, even_in[...], odd_in[...]),
            tab[...],
            jnp.where(is_odd, odd_in[...], even_in[...]),
        ],
        1,
    )
    hi, mid, lo = pieces(whole)
    tab24 = jnp.concatenate([hi, mid, lo], 0).astype(BF16)

    def gather(i):
        cols = lanes(i, 256)
        hot = jnp.where(iota((NTAB, 256), 0) == slots[:, cols], 1.0, 0.0).astype(BF16)
        got = dot(tab24, hot, 1, 0)
        gat[:, cols] = got[0:8] + got[8:16] + got[16:24]

    over(4, gather)

    live = jnp.where(slots[...] != OWN + iota((1, EDGES), 1) % ATOMS, 1.0, 0.0)
    dead = 1.0 - live
    dx = (gat[0:1, :] - cent[0:1, :]) * live + dead * 2.5
    dy = (gat[1:2, :] - cent[1:2, :]) * live
    dz = (gat[2:3, :] - cent[2:3, :]) * live
    r = jnp.sqrt(dx * dx + dy * dy + dz * dz)
    inv = 1.0 / r
    t = r / CUTOFF
    t2 = t * t
    t6 = t2 * t2 * t2
    smooth = live * (1.0 - 28.0 * t6 + 48.0 * t6 * t - 21.0 * t6 * t * t)
    ux, uy, uz = dx * inv, dy * inv, dz * inv
    geo[0:1, :] = jnp.ones_like(r)
    geo[1:2, :] = R3 * ux
    geo[2:3, :] = R3 * uy
    geo[3:4, :] = R3 * uz
    geo[4:5, :] = Q75 * HR * (ux * ux - uy * uy)
    geo[5:6, :] = Q75 * SR * (ux * ux + uy * uy - 2.0 * uz * uz)
    geo[6:7, :] = Q75 * 2.0 * HR * (ux * uy)
    geo[7:8, :] = Q75 * 2.0 * HR * (ux * uz)
    geo[8:9, :] = Q75 * 2.0 * HR * (uy * uz)
    geo[9:10, :] = smooth
    geo[10:11, :] = live
    geo[11:12, :] = r
    geo[12:13, :] = dx
    geo[13:14, :] = dy
    geo[14:15, :] = dz
    order = (iota((8, EDGES), 0) + 1).astype(F32) * (math.pi / CUTOFF)
    geo[16:24, :] = smooth * BESSEL * jnp.sin(order * r) * inv
    hot_c = jnp.where(iota((NSPEC, EDGES), 0).astype(F32) == cent[3:4, :], 1.0, 0.0)
    grad = cent[4:5, :] * jnp.sum(hot_c * columns[0:64, 8:9], 0, keepdims=True)
    geo[15:16, :] = grad
    geo[24:25, :] = grad * smooth
    geo[25:26, :] = gat[3:4, :]
    geo[26:32, :] = jnp.zeros((6, EDGES), F32)

    def embed_product(i, out):
        cols = pl.ds(i * 256, 256)
        out[...] = dot(table[...], embed_inputs(cent, geo, cols), 0, 0)

    def embed(i, before):
        cols = pl.ds(i * 256, 256)
        sm = geo[9:10, cols]
        for b in range(8):
            rows = pl.ds(b * 128, 128)
            p = before[rows, :]
            x0h[rows, cols], x0l[rows, cols] = split(p * sigmoid(p) * sm)
        vw[:, cols] = dot3(
            veh[...], vel[...], x0h[0:LATENT, cols], x0l[0:LATENT, cols], 1, 0
        )

    staggered(4, (za, zb), embed_product, embed)
    make_env(geo, vw.at[64:128, :], g0)

    def tensor(k):
        cols = lanes(k, 128)
        v = vw[0:64, cols]
        y = [geo[c : c + 1, cols] for c in range(9)]
        e0 = rows_of(g0, 0)
        e1, e2, e3 = rows_of(g0, 1), rows_of(g0, 2), rows_of(g0, 3)
        a, b, c = y[1] * e1, y[2] * e2, y[3] * e3
        vec = a + b + c
        quad = y[4] * rows_of(g0, 4)
        for m in range(5, 9):
            quad = quad + y[m] * rows_of(g0, m)
        x0h[1024:1088, cols], x0l[1024:1088, cols] = split(v * e0)
        x0h[1088:1152, cols], x0l[1088:1152, cols] = split(v * vec)
        x0h[1152:1216, cols], x0l[1152:1216, cols] = split(v * quad)
        p = [rows_of(path, n) for n in range(9)]
        e12, e13 = y[1] * e2, y[1] * e3
        e21, e23 = y[2] * e1, y[2] * e3
        e31, e32 = y[3] * e1, y[3] * e2
        q00 = HR * y[4] + SR * y[5]
        q11 = SR * y[5] - HR * y[4]
        q22 = -2.0 * SR * y[5]
        q01, q02, q12 = HR * y[6], HR * y[7], HR * y[8]
        f1[0:64, cols] = v * (p[0] * e0 + p[1] * vec)
        p3g = p[3] * e0
        f1[64:128, cols] = v * (
            p[2] * e1 + p3g * y[1] + p[4] * (e23 - e32) + p[5] * (q00 * e1 + q01 * e2 + q02 * e3)
        )
        f1[128:192, cols] = v * (
            p[2] * e2 + p3g * y[2] + p[4] * (e31 - e13) + p[5] * (q01 * e1 + q11 * e2 + q12 * e3)
        )
        f1[192:256, cols] = v * (
            p[2] * e3 + p3g * y[3] + p[4] * (e12 - e21) + p[5] * (q02 * e1 + q12 * e2 + q22 * e3)
        )
        p8g = p[8] * e0
        pair = (
            HR * (a - b),
            SR * (a + b - 2.0 * c),
            HR * (e12 + e21),
            HR * (e13 + e31),
            HR * (e23 + e32),
        )
        for m in range(5):
            f1[(4 + m) * 64 : (5 + m) * 64, cols] = v * (
                p[6] * pair[m] + p[7] * rows_of(g0, 4 + m) + p8g * y[4 + m]
            )

    over(8, tensor)

    def layer_product(i, out):
        cols = pl.ds(i * 256, 256)
        out[...] = dot3(w0h[...], w0l[...], x0h[:, cols], x0l[:, cols], 0, 0)

    def layer(i, zs):
        cols = pl.ds(i * 256, 256)
        sm = geo[9:10, cols]
        for b in range(8):
            rows = pl.ds(b * 128, 128)
            z = zs[rows, :]
            z0[rows, cols] = z
            old = x0h[rows, cols].astype(F32) + x0l[rows, cols].astype(F32)
            x1h[rows, cols], x1l[rows, cols] = split((old + sm * (z * sigmoid(z))) * RH)
        w1[:, cols] = dot3(
            evh[...], evl[...], x1h[0:LATENT, cols], x1l[0:LATENT, cols], 1, 0
        )

    staggered(4, (za, zb), layer_product, layer)
    make_env(geo, w1, g1)

    def scalars(k):
        cols = lanes(k, 128)
        s0 = rows_of(f1, 0, cols) * rows_of(g1, 0)
        s1 = rows_of(f1, 1, cols) * rows_of(g1, 1)
        for c in range(2, 4):
            s1 = s1 + rows_of(f1, c, cols) * rows_of(g1, c)
        s2 = rows_of(f1, 4, cols) * rows_of(g1, 4)
        for c in range(5, 9):
            s2 = s2 + rows_of(f1, c, cols) * rows_of(g1, c)
        x1h[1024:1088, cols], x1l[1024:1088, cols] = split(s0)
        x1h[1088:1152, cols], x1l[1088:1152, cols] = split(s1)
        x1h[1152:1216, cols], x1l[1152:1216, cols] = split(s2)

    over(8, scalars)


def grad_kernel(mine, place, xh, xl, qh, ql, out):
    block = place[3] if mine else 1 - place[3]
    for n in range(0, HALF, QUARTER):
        rows = pl.ds(pl.multiple_of(block * HALF, HALF) + n, QUARTER)
        out[:, n : n + QUARTER] = dot3(xh[...], xl[...], qh[rows, :], ql[rows, :], 1, 1)


def late_kernel(x1h, x1l, wh, wl, columns, geo, qh, ql, side, dout, acc, za, zb):
    acc[...] = jnp.zeros_like(acc)
    side[...] = jnp.zeros_like(side)

    def product(i, out):
        cols = pl.ds(i * 256, 256)
        out[...] = dot3(wh[...], wl[...], x1h[:, cols], x1l[:, cols], 0, 0)

    def step(i, zs):
        cols = pl.ds(i * 256, 256)
        sm = geo[9:10, cols]
        gs = geo[24:25, cols]
        scale = gs * sm * RH
        reach = jnp.zeros((8, 256), F32)
        total = jnp.zeros((8, 256), F32)
        for b in range(8):
            rows = pl.ds(b * 128, 128)
            si, dsi = silu_both(zs[rows, :])
            ow = columns[:, b : b + 1]
            qh[rows, cols], ql[rows, cols] = split((ow * scale) * dsi)
            lat = (x1h[rows, cols].astype(F32) + x1l[rows, cols].astype(F32) + sm * si) * RH
            part = gs * lat
            acc[rows, :] += part[:, 0:128] + part[:, 128:256]
            reach = reach + jnp.sum((ow * si).reshape(16, 8, 256), 0)
            total = total + jnp.sum((ow * lat).reshape(16, 8, 256), 0)
        side[0:1, cols] = jnp.sum(reach, 0, keepdims=True)
        side[1:2, cols] = jnp.sum(total, 0, keepdims=True)

    staggered(4, (za, zb), product, step)
    dout[...] = jnp.broadcast_to(jnp.sum(acc[...].T, 0, keepdims=True), dout.shape)


def mid_kernel(qh, ql, wh, wl, f1, g1, w1, geo, ds1, dwh, dwl, dy, denv):
    def scal(i):
        cols = lanes(i, 256)
        ds1[:, cols] = dot3(wh[1024:1216, :], wl[1024:1216, :], qh[:, cols], ql[:, cols], 1, 0)

    over(4, scal)
    for c in range(9):
        kind = 0 if c == 0 else (1 if c < 4 else 2)
        acc = None
        for k in range(8):
            cols = pl.ds(k * 128, 128)
            term = rows_of(ds1, kind, cols) * rows_of(f1, c, cols)
            acc = term if acc is None else acc + term
        denv[c * 64 : (c + 1) * 64, :] = slot_total(acc) * NORM
    env_back(geo, w1, denv, dwh, dwl, dy, None)


def env_back(geo, w, denv, dwh, dwl, dy, more):
    def step(k):
        cols = lanes(k, 128)
        acc = rows_of(denv, 0)
        wk = w[:, cols]
        rows = [jnp.zeros((1, 128), F32)]
        for c in range(1, 9):
            d = rows_of(denv, c)
            acc = acc + geo[c : c + 1, cols] * d
            rows.append(jnp.sum(wk * d, 0, keepdims=True))
        dwh[:, cols], dwl[:, cols] = split(acc)
        for c in range(1, 9):
            if more is None:
                dy[c : c + 1, cols] = rows[c]
            else:
                dy[c : c + 1, cols] = rows[c] + more[c : c + 1, cols]

    over(8, step)


def early_kernel(
    q1h, q1l, wh, wl, evh, evl, dwh, dwl, columns, geo, z0, dlat, qh, ql, side, da, db
):
    side[...] = jnp.zeros_like(side)

    def product(i, out):
        cols = pl.ds(i * 256, 256)
        out[...] = dot3(
            wh[0:LATENT, :], wl[0:LATENT, :], q1h[:, cols], q1l[:, cols], 1, 0
        ) + dot3(evh[...], evl[...], dwh[:, cols], dwl[:, cols], 0, 0)

    def step(i, ds):
        cols = pl.ds(i * 256, 256)
        sm = geo[9:10, cols] * RH
        gs = geo[24:25, cols] * RH
        total = jnp.zeros((8, 256), F32)
        for b in range(8):
            rows = pl.ds(b * 128, 128)
            dl = ds[rows, :] + columns[:, b : b + 1] * gs
            dlat[rows, cols] = dl * RH
            si, dsi = silu_both(z0[rows, cols])
            qh[rows, cols], ql[rows, cols] = split(dl * dsi * sm)
            total = total + jnp.sum((dl * si).reshape(16, 8, 256), 0)
        side[0:1, cols] = jnp.sum(total, 0, keepdims=True) * RH

    staggered(4, (da, db), product, step)


def couple_kernel(
    qh, ql, wh, wl, vw, geo, g0, g1, ds1, path, dy1,
    dvwh, dvwl, dy, dpath,
    ds0, denv, dyv,
):
    def scal(i):
        cols = lanes(i, 256)
        ds0[:, cols] = dot3(wh[1024:1216, :], wl[1024:1216, :], qh[:, cols], ql[:, cols], 1, 0)

    over(4, scal)
    denv[...] = jnp.zeros_like(denv)
    dpath[...] = jnp.zeros_like(dpath)

    def step(k):
        cols = lanes(k, 128)
        v = vw[0:64, cols]
        y = [geo[c : c + 1, cols] for c in range(9)]
        e = [rows_of(g0, c) for c in range(9)]
        p = [rows_of(path, n) for n in range(9)]
        s = [rows_of(ds0, n, cols) for n in range(3)]
        u = [rows_of(ds1, n, cols) for n in range(3)]
        f0 = u[0] * rows_of(g1, 0)
        fv = [u[1] * rows_of(g1, c) for c in range(1, 4)]
        fq = [u[2] * rows_of(g1, c) for c in range(4, 9)]
        yv, yq, ev_, eq = y[1:4], y[4:9], e[1:4], e[4:9]

        def dot_of(a, b):
            out = a[0] * b[0]
            for i in range(1, len(a)):
                out = out + a[i] * b[i]
            return out

        m00 = HR * yq[0] + SR * yq[1]
        m11 = SR * yq[1] - HR * yq[0]
        m22 = -2.0 * SR * yq[1]
        m01, m02, m12 = HR * yq[2], HR * yq[3], HR * yq[4]
        t00 = HR * fq[0] + SR * fq[1]
        t11 = SR * fq[1] - HR * fq[0]
        t22 = (-2.0 * SR) * fq[1]
        t01, t02, t12 = HR * fq[2], HR * fq[3], HR * fq[4]

        te = [
            t00 * ev_[0] + t01 * ev_[1] + t02 * ev_[2],
            t01 * ev_[0] + t11 * ev_[1] + t12 * ev_[2],
            t02 * ev_[0] + t12 * ev_[1] + t22 * ev_[2],
        ]
        ty = [
            t00 * yv[0] + t01 * yv[1] + t02 * yv[2],
            t01 * yv[0] + t11 * yv[1] + t12 * yv[2],
            t02 * yv[0] + t12 * yv[1] + t22 * yv[2],
        ]
        mf = [
            m00 * fv[0] + m01 * fv[1] + m02 * fv[2],
            m01 * fv[0] + m11 * fv[1] + m12 * fv[2],
            m02 * fv[0] + m12 * fv[1] + m22 * fv[2],
        ]
        ef = [
            ev_[1] * fv[2] - ev_[2] * fv[1],
            ev_[2] * fv[0] - ev_[0] * fv[2],
            ev_[0] * fv[1] - ev_[1] * fv[0],
        ]
        fy = [
            fv[1] * yv[2] - fv[2] * yv[1],
            fv[2] * yv[0] - fv[0] * yv[2],
            fv[0] * yv[1] - fv[1] * yv[0],
        ]
        e_fv = dot_of(ev_, fv)
        y_fv = dot_of(yv, fv)
        e_fq = dot_of(eq, fq)
        y_fq = dot_of(yq, fq)
        vec = dot_of(yv, ev_)
        y_te = dot_of(yv, te)
        e_mf = dot_of(ev_, mf)
        y_ef = dot_of(yv, ef)

        grads = (
            e[0] * f0,
            vec * f0,
            e_fv,
            e[0] * y_fv,
            y_ef,
            e_mf,
            y_te,
            e_fq,
            e[0] * y_fq,
        )
        for n in range(9):
            dpath[n * 64 : (n + 1) * 64, :] += v * grads[n]

        p1f = p[1] * f0
        d0 = s[0] * e[0] + p[0] * e[0] * f0 + p[2] * e_fv + p[7] * e_fq
        p3e = p[3] * e[0]
        p8e = p[8] * e[0]
        s1f = s[1] + p1f
        dv = d0
        for i in range(3):
            di = s1f * ev_[i] + p3e * fv[i] + p[4] * ef[i] + p[6] * te[i]
            dv = dv + yv[i] * di
            dyv[1 + i : 2 + i, cols] = jnp.sum(v * di, 0, keepdims=True)
        a, b, c = fv[0] * ev_[0], fv[1] * ev_[1], fv[2] * ev_[2]
        bil = (
            HR * (a - b),
            SR * (a + b - 2.0 * c),
            HR * (fv[0] * ev_[1] + fv[1] * ev_[0]),
            HR * (fv[0] * ev_[2] + fv[2] * ev_[0]),
            HR * (fv[1] * ev_[2] + fv[2] * ev_[1]),
        )
        for m in range(5):
            dm = s[2] * eq[m] + p[5] * bil[m] + p8e * fq[m]
            dv = dv + yq[m] * dm
            dyv[4 + m : 5 + m, cols] = jnp.sum(v * dm, 0, keepdims=True)
        dvwh[0:64, cols], dvwl[0:64, cols] = split(dv)

        denv[0:64, :] += v * (s[0] + p[0] * f0 + p[3] * y_fv + p[8] * y_fq)
        for i in range(3):
            denv[(1 + i) * 64 : (2 + i) * 64, :] += v * (
                s1f * yv[i] + p[2] * fv[i] + p[4] * fy[i] + p[5] * mf[i] + p[6] * ty[i]
            )
        for m in range(5):
            denv[(4 + m) * 64 : (5 + m) * 64, :] += v * (s[2] * yq[m] + p[7] * fq[m])

    over(8, step)
    for c in range(9):
        denv[c * 64 : (c + 1) * 64, :] = slot_total(rows_of(denv, c)) * NORM
    dyv[0:1, :] = jnp.zeros((1, EDGES), F32)
    dyv[...] += dy1[...]
    env_back(geo, vw.at[64:128, :], denv, dvwh.at[64:128, :], dvwl.at[64:128, :], dy, dyv)


def pre_kernel(
    half, qh, ql, wh, wl, veh, vel, dvwh, dvwl, dl, table, cent, geo, rad_w,
    qph, qpl, side, drad, da, db, pre,
):
    base = half * HALF
    wr = slice(base, base + HALF)
    rwh, rwl = split(jnp.concatenate([rad_w[:, wr], jnp.zeros((8, HALF), F32)], 0))
    side[...] = jnp.zeros_like(side)

    def product(i, out):
        cols = pl.ds(i * 256, 256)
        out[...] = dot3(wh[wr, :], wl[wr, :], qh[:, cols], ql[:, cols], 1, 0) + dot3(
            veh[:, wr], vel[:, wr], dvwh[:, cols], dvwl[:, cols], 0, 0
        )

    def step(i, ds):
        cols = pl.ds(i * 256, 256)
        sm = geo[9:10, cols]
        total = jnp.zeros((8, 256), F32)
        pre[...] = dot(table[:, wr], embed_inputs(cent, geo, cols), 0, 0)
        for b in range(4):
            rows = pl.ds(b * 128, 128)
            dd = ds[rows, :] + dl[pl.ds(base + b * 128, 128), cols]
            si, dsi = silu_both(pre[rows, :])
            qph[rows, cols], qpl[rows, cols] = split(dd * dsi * sm)
            total = total + jnp.sum((dd * si).reshape(16, 8, 256), 0)
        side[0:1, cols] = jnp.sum(total, 0, keepdims=True)
        drad[:, cols] = dot3(rwh, rwl, qph[:, cols], qpl[:, cols], 1, 0)[0:8]

    staggered(4, (da, db), product, step)


def last_kernel(
    rows_y, rows_z, place, qps, sides, drads, geo, slots, cent, sl, se, dy,
    dpath, columns, dout, more,
    small_keep, small_send, energy,
    ghost, small, spread,
):
    kinds = iota((NSPEC, EDGES), 0).astype(F32)
    hot_c = jnp.where(kinds == cent[3:4, :], 1.0, 0.0)
    hot_n = jnp.where(kinds == geo[25:26, :], 1.0, 0.0)
    hots = jnp.concatenate([hot_c, hot_n], 0).astype(BF16)
    rad = geo[16:24, :]
    rad_h = rad.astype(BF16).astype(F32)
    rads = jnp.concatenate([rad_h, rad - rad_h], 0).astype(BF16)
    left = jnp.concatenate([hots, rads], 0)
    for n, (qh, ql) in enumerate(zip(qps[0::2], qps[1::2])):
        full = dot(left, qh[...], 1, 1)
        rest = dot(left, ql[...], 1, 1)
        part = slice(n * HALF, (n + 1) * HALF)
        small[0:128, part] = full[0:128] + rest[0:128]
        small[128:136, part] = full[128:136] + full[136:144] + rest[128:136]

    live, r, smooth = geo[10:11, :], geo[11:12, :], geo[9:10, :]
    inv = 1.0 / r
    grad = geo[15:16, :]
    reach = sl[0:1, :]
    lat_out = sl[1:2, :]
    order = (iota((8, EDGES), 0) + 1).astype(F32) * (math.pi / CUTOFF)
    angle = order * r
    sine = jnp.sin(angle) * inv
    cosine = jnp.cos(angle) * inv
    dr8 = drads[0][...] + drads[1][...]
    d_s = (
        grad * lat_out
        + grad * smooth * RH * reach
        + se[0:1, :]
        + sides[0][0:1, :]
        + sides[1][0:1, :]
        + BESSEL * jnp.sum(dr8 * sine, 0, keepdims=True)
    )
    t = r / CUTOFF
    t2 = t * t
    gap = 1.0 - t
    d_r = d_s * (live * (-168.0 / CUTOFF) * (t2 * t2 * t) * (gap * gap)) + (
        smooth * BESSEL
    ) * jnp.sum(dr8 * (order * cosine - sine * inv), 0, keepdims=True)
    ux, uy, uz = geo[12:13, :] * inv, geo[13:14, :] * inv, geo[14:15, :] * inv
    yy = [dy[c : c + 1, :] for c in range(9)]
    h2, s2 = 2.0 * HR * Q75, 2.0 * SR * Q75
    gx = R3 * yy[1] + ux * (h2 * yy[4] + s2 * yy[5]) + h2 * (uy * yy[6] + uz * yy[7])
    gy = R3 * yy[2] + uy * (s2 * yy[5] - h2 * yy[4]) + h2 * (ux * yy[6] + uz * yy[8])
    gz = R3 * yy[3] - 2.0 * s2 * uz * yy[5] + h2 * (ux * yy[7] + uy * yy[8])
    along = ux * gx + uy * gy + uz * gz
    zero = jnp.zeros((5, EDGES), F32)
    disp = jnp.concatenate(
        [
            live * ((gx - ux * along) * inv + ux * d_r),
            live * ((gy - uy * along) * inv + uy * d_r),
            live * ((gz - uz * along) * inv + uz * d_r),
            zero,
        ],
        0,
    )
    hi, mid, lo = pieces(disp)
    disp24 = jnp.concatenate([hi, mid, lo], 0).astype(BF16)
    acc = None
    mine = None
    for k in range(8):
        term = disp[:, k * 128 : (k + 1) * 128]
        mine = term if mine is None else mine + term
    mine = slot_total(mine)
    for i in range(4):
        cols = pl.ds(i * 256, 256)
        hot = jnp.where(iota((NTAB, 256), 0) == slots[:, cols], 1.0, 0.0).astype(BF16)
        term = dot(disp24[:, i * 256 : (i + 1) * 256], hot, 1, 1)
        acc = term if acc is None else acc + term
    ghost[...] = acc[0:8] + acc[8:16] + acc[16:24]
    lane = iota((8, 128), 1)
    middle = ghost[:, 512:640] - jnp.where(
        (lane >= ATOMS) & (lane < 2 * ATOMS), pltpu.roll(mine, ATOMS, 1), 0.0
    )
    ghost[:, 512:640] = middle
    atoms = spread.shape[1]
    spread[...] = jnp.zeros_like(spread)
    total = jnp.zeros_like(spread)
    for bx in range(3):
        for by in range(3):
            block = 3 * bx + by
            spread[:, 0:128] = ghost[:, block * 128 : (block + 1) * 128]
            start = place[4] + ((bx - 1) * rows_y + by - 1) * rows_z * ATOMS - ATOMS
            total = total + pltpu.roll(spread[...], lax.rem(start + 2 * atoms, atoms), 1)
    for n in range(atoms // LATENT):
        small[144 + 8 * n : 152 + 8 * n, :] = total[:, n * LATENT : (n + 1) * LATENT]

    edge_energy = smooth * lat_out
    total = None
    for k in range(8):
        term = edge_energy[:, k * 128 : (k + 1) * 128]
        total = term if total is None else total + term
    total = slot_total(jnp.broadcast_to(total, (8, 128)))[0:1]
    hot = jnp.where(iota((NSPEC, 128), 0).astype(F32) == cent[3:4, 0:128], 1.0, 0.0)
    energy[...] = jnp.broadcast_to(
        jnp.sum(hot * columns[0:64, 8:9], 0, keepdims=True) * total
        + jnp.sum(hot * columns[0:64, 9:10], 0, keepdims=True),
        energy.shape,
    )
    cot = cent[4:5, 0:128] * jnp.where(iota((1, 128), 1) < ATOMS, 1.0, 0.0)
    stack = jnp.concatenate(
        [dpath[...], hot * (cot * total), hot * cot, jnp.zeros((64, 128), F32)], 0
    )
    row = jnp.sum(stack.T, 0, keepdims=True)
    small[136:144, :] = jnp.zeros((8, LATENT), F32)
    small[136:137, 0:768] = row
    small[137:138, :] = dout[0:1, :]
    mine = pl.ds(pl.multiple_of(place[3] * HALF, HALF), HALF)
    other = pl.ds(pl.multiple_of((1 - place[3]) * HALF, HALF), HALF)
    for out, cols in ((small_keep, mine), (small_send, other)):
        out[0:192, :] = more[:, cols]
        out[192:, :] = small[:, cols]


def weights_kernel(dvwh, dvwl, x0h, x0l, dw1h, dw1l, x1h, x1l, out):
    out[0:128, :] = dot3(dvwh[...], dvwl[...], x0h[0:LATENT, :], x0l[0:LATENT, :], 1, 1)
    out[128:192, :] = dot3(dw1h[...], dw1l[...], x1h[0:LATENT, :], x1l[0:LATENT, :], 1, 1)


def halves(shape, dim):
    rows, cols = shape
    return (rows // 2, cols) if dim == 0 else (rows, cols // 2) if dim == 1 else shape


def half_of(shape, dim, bit):
    rows, cols = shape
    if dim == 0:
        rows //= 2
        return pl.ds(pl.multiple_of(bit * rows, 8), rows), slice(None)
    cols //= 2
    return slice(None), pl.ds(pl.multiple_of(bit * cols, 128), cols)


def down_kernel(dim, flag, place, keep, got, *outs):
    if dim is None:
        outs[0][...] = keep[...] + got[...]
        return
    for out, bit in zip(outs, (1 - place[flag], place[flag])):
        index = half_of(keep.shape, dim, bit)
        out[...] = keep[index] + got[index]


def up_kernel(dim, flag, place, mine, got, out):
    out[half_of(out.shape, dim, place[flag])] = mine[...]
    out[half_of(out.shape, dim, 1 - place[flag])] = got[...]


def end_kernel(parts, place, *refs):
    srcs, out, sem = refs[: len(parts)], refs[-2], refs[-1]
    copies = []
    for n, ((layer, start, mine), src) in enumerate(zip(parts, srcs)):
        block = place[3] if mine else 1 - place[3]
        cols = pl.ds(pl.multiple_of(block * HALF, HALF), HALF)
        rows = pl.ds(start, src.shape[0])
        copies.append(pltpu.make_async_copy(src, out.at[layer, rows, cols], sem.at[n]))
    for copy in copies:
        copy.start()
    for copy in copies:
        copy.wait()


def small_end_kernel(
    core_at, place, mine, got, energy,
    center, neigh, radial, value, env, path, out, scale, shift, grad, energies,
):
    for src, b in ((mine, place[core_at]), (got, 1 - place[core_at])):
        cols = pl.ds(pl.multiple_of(b * HALF, HALF), HALF)
        value[:, cols] = src[0:64, :]
        env[0, :, cols] = src[64:128, :]
        env[1, :, cols] = src[128:192, :]
        center[:, cols] = src[192:256, :]
        neigh[:, cols] = src[256:320, :]
        radial[:, cols] = src[320:328, :]
    is_first = place[core_at] == 0

    def whole(rows):
        first = jnp.where(is_first, mine[rows, :], got[rows, :])
        second = jnp.where(is_first, got[rows, :], mine[rows, :])
        return jnp.concatenate([first, second], 1)

    base = 336 + 8 * (place[4] // LATENT)
    spread = whole(pl.ds(pl.multiple_of(base, 8), 8))
    shift_by = LATENT - lax.rem(place[4], LATENT)
    grad[...] = pltpu.roll(spread, lax.rem(shift_by, LATENT), 1)[0:3, 0:ATOMS]
    energies[...] = energy[0:1, 0:ATOMS]
    row = whole(slice(328, 336))
    for n in range(9):
        path[n : n + 1, :] = row[0:1, n * 64 : (n + 1) * 64]
    scale[...] = row[0:1, 576:640]
    shift[...] = row[0:1, 640:704]
    for n in range(8):
        out[n : n + 1, :] = row[1:2, n * 128 : (n + 1) * 128]


VSPEC = pl.BlockSpec(memory_space=pltpu.VMEM)
SSPEC = pl.BlockSpec(memory_space=pltpu.SMEM)
ASPEC = pl.BlockSpec(memory_space=pl.ANY)
HSPEC = pl.BlockSpec(memory_space=pltpu.HBM)


PROGRAM = (
    "late", "send_a", "keep_a", "mid", "a", "early", "send_c", "a", "keep_c", "c",
    "a", "couple", "a", "pre0", "c", "a", "weights", "a", "pre1", "c",
    "a", "last", "c", "free", "a", "a", "a", "a", "end_a", "c",
    "s", "c", "s", "c", "s", "s", "c", "c", "c", "end_c",
    "s", "s", "s", "end_s",
)


COST = {
    "late": 6.5, "send_a": 4.6, "keep_a": 0.57, "mid": 3, "early": 5.0, "send_c": 4.6,
    "keep_c": 4.6, "couple": 25.2, "weights": 4, "pre0": 3.5, "pre1": 3.5, "last": 5,
    "land_a": 8, "land_c": 2, "land_s": 3.0,
}


class Order:
    def __init__(self):
        self.token = None
        self.free = False
        self.extra = ()

    def __call__(
        self, body, outs, args, scratch=(), scalar=False, hbm=(), plain=False, alias=None, us=1,
        limit=6, name=None, mark=False,
    ):
        specs = [HSPEC if n in hbm else VSPEC for n in range(len(args))]
        if scalar:
            specs[0] = SSPEC
        count, given = len(args), len(outs)
        marked = mark or not self.free
        tokens = () if self.token is None or self.free else (self.token,)
        tokens, self.extra = tokens + self.extra, ()

        def kernel(*refs):
            after = refs[count + len(tokens) :]
            if not marked:
                return body(*refs[:count], *after)
            after[given][...] = jnp.zeros((8, 128), F32)
            body(*refs[:count], *after[:given], *after[given + 1 :])

        if plain:
            shapes = [jax.ShapeDtypeStruct(shape, dtype) for shape, dtype in outs]
        else:
            shapes = [pltpu.VMEM(shape, dtype) for shape, dtype in outs]
        out_spec = HSPEC if plain == "hbm" else VSPEC
        got = pl.pallas_call(
            kernel,
            name=name or getattr(body, "func", body).__name__,
            out_shape=shapes + ([pltpu.VMEM((8, 128), F32)] if marked else []),
            in_specs=specs + [ASPEC] * len(tokens),
            out_specs=[out_spec] * given + ([VSPEC] if marked else []),
            scratch_shapes=list(scratch),
            input_output_aliases=alias or {},
            compiler_params=pltpu.CompilerParams(vmem_limit_bytes=limit << 20),
            cost_estimate=pl.CostEstimate(
                flops=int(us * 3e9), bytes_accessed=1 << 20, transcendentals=0
            ),
        )(*args, *tokens)
        if not marked:
            return got
        self.token = got[-1]
        return got[:-1]


def is_up(axis, bit):
    return (lax.axis_index(axis) // bit) & 1


def even_pairs(axis):
    return [(i, i ^ 1) for i in range(lax.axis_size(axis))]


def odd_pairs(axis):
    count = lax.axis_size(axis)
    return [p for i in range(1, count - 1, 2) for p in ((i, i + 1), (i + 1, i))]


def neighbours_of(axis, even, odd):
    pairs = odd_pairs(axis)
    return (
        lax.ppermute(even, axis, even_pairs(axis)),
        lax.ppermute(odd, axis, pairs) if pairs else jnp.zeros_like(odd),
    )


class Route:
    def __init__(self, mesh_sizes, base, tall_first=False):
        sizes = dict(mesh_sizes)
        names = list(sizes)

        def bits(axis, least=1):
            return [(axis, 1 << n) for n in range(20) if least <= 1 << n < sizes[axis]]

        flat, tall = bits("gx"), bits("gy") + bits("gz", 2)
        first = [("gz", 1)]
        one, two = (flat, tall), (flat[::-1], tall)
        if tall_first:
            one, two = one[::-1], two[::-1]
        self.steps = list(zip(first + one[0] + one[1], first + two[0] + two[1]))
        self.count = len(self.steps)
        self.base = base
        self.names = tuple(names)
        coords = [()]
        for name in names:
            coords = [c + (i,) for c in coords for i in range(sizes[name])]
        index = {c: n for n, c in enumerate(coords)}
        self.pairs = []
        for step in self.steps:
            pairs = []
            for c in coords:
                axis, bit = step[c[names.index("gz")] & 1]
                at = names.index(axis)
                pairs.append((index[c], index[c[:at] + (c[at] ^ bit,) + c[at + 1 :]]))
            self.pairs.append(pairs)

    def flags(self):
        core = is_up("gz", 1)
        return [jnp.where(core == 1, is_up(*two), is_up(*one)) for one, two in self.steps]

    def swap(self, x, at):
        return lax.ppermute(x, self.names, self.pairs[at])


class Sum:
    def __init__(self, name, order, place, route, send, dims):
        self.name = name
        self.order, self.place, self.route = order, place, route
        self.dims = (1,) + dims + (None,) * (route.count - 1 - len(dims))
        self.keep, self.send = None, send
        self.at, self.rising = 0, False
        self.shapes = []
        self.launch()

    def launch(self):
        with jax.named_scope(f"sum_{self.name}_{'up' if self.rising else 'down'}_{self.at}"):
            self.got = self.route.swap(self.send, self.at)

    @property
    def over(self):
        return self.rising and self.at == 0

    def land(self):
        (self.climb if self.rising else self.descend)()
        self.launch()

    def call(self, body, dim, flag, shapes, args):
        return self.order(
            functools.partial(body, dim, flag),
            [(shape, F32) for shape in shapes],
            (self.place, *args),
            scalar=True,
            us=COST[f"land_{self.name}"],
            name=f"land_{self.name}_{'up' if self.rising else 'down'}_{self.at}",
        )

    def descend(self):
        self.shapes.append(self.keep.shape)
        self.at += 1
        last = self.at == self.route.count
        dim = None if last else self.dims[self.at]
        shapes = [halves(self.keep.shape, dim)] * (1 if dim is None else 2)
        outs = self.call(
            down_kernel, dim, self.route.base + self.at, shapes, (self.keep, self.got)
        )
        self.send, self.keep = outs[0], outs[-1]
        if last:
            self.rising = True
            self.rise()

    def rise(self):
        self.at -= 1
        while self.at > 0 and self.dims[self.at] is None:
            self.at -= 1

    def climb(self):
        (self.send,) = self.call(
            up_kernel,
            self.dims[self.at],
            self.route.base + self.at,
            [self.shapes[self.at - 1]],
            (self.send, self.got),
        )
        self.rise()


def per_device(
    positions,
    species,
    neighbours,
    embed_center,
    embed_neigh,
    embed_radial,
    value_proj,
    env_weight,
    latent_weight,
    path_weight,
    out_weight,
    scale_table,
    shift_table,
    cotangent,
):
    vm, sem = pltpu.VMEM, pltpu.SemaphoreType
    order = Order()
    sizes = [(axis, lax.axis_size(axis)) for axis in ("gx", "gy", "gz")]
    route = Route(sizes, 5)
    steep = Route(sizes, 5 + route.count, tall_first=True)
    first_atom = lax.axis_index(("gx", "gy", "gz")) * ATOMS
    place = [is_up("gz", 1), is_up("gy", 1), is_up("gx", 1), is_up("gz", 1), first_atom]
    place = jnp.stack(place + route.flags() + steep.flags()).astype(jnp.int32)
    spec_row = species.reshape(1, ATOMS)

    (table,) = order(pack_kernel, [((8, 128), F32)], (positions, spec_row), us=1)
    even, odd = neighbours_of("gz", table, table)
    (table,) = order(
        join_z_kernel, [((8, 128), F32)], (place, table, even, odd), scalar=True, us=1
    )
    even, odd = neighbours_of("gy", table, table)
    (table,) = order(
        join_y_kernel,
        [((8, 384), F32)],
        (place, table, even, odd),
        scalar=True,
        us=1,
    )
    even, odd = neighbours_of("gx", table, table)

    wide = ((WIDE, EDGES), BF16)
    half = ((HALF, EDGES), BF16)
    row64 = ((64, LATENT), BF16)
    row128 = ((128, LATENT), BF16)
    w0h, w0l, w1h, w1l, hots, veh, vel, evh, evl, path, columns, slots, cent, rad_w = order(
        prep_kernel,
        [
            wide, wide, wide, wide, ((288, LATENT), BF16), row128, row128, row64, row64,
            ((576, 128), F32), ((128, 128), F32), ((1, EDGES), jnp.int32), ((8, EDGES), F32),
            ((8, LATENT), F32),
        ],
        (latent_weight, embed_center, embed_neigh, embed_radial, value_proj.T,
         jnp.swapaxes(env_weight, 1, 2), neighbours, positions, spec_row,
         cotangent.reshape(1, ATOMS), path_weight, out_weight.reshape(8, 128),
         scale_table.reshape(1, NSPEC), shift_table.reshape(1, NSPEC)),
        [
            vm((NSPEC, LATENT), F32), vm((NSPEC, LATENT), F32), vm((CHANNELS, LATENT), F32),
            vm((2, CHANNELS, LATENT), F32), vm((NB, ATOMS), jnp.int32), vm((3, ATOMS), F32),
            vm((1, ATOMS), jnp.int32), vm((1, ATOMS), F32), vm((9, CHANNELS), F32),
            vm((8, 128), F32), vm((1, NSPEC), F32), vm((1, NSPEC), F32), vm((128, 128), F32),
            sem.DMA((13,)),
        ],
        hbm=range(1, 14),
        us=4,
    )

    x0h, x0l, x1h, x1l, z0, vw, w1, geo, g0, g1, f1 = order(
        fwd_kernel,
        [
            wide, wide, wide, wide,
            ((LATENT, EDGES), F32), ((128, EDGES), F32), ((64, EDGES), F32), ((G_ROWS, EDGES), F32), ((576, 128), F32), ((576, 128), F32),
            ((576, EDGES), F32),
        ],
        (place, table, even, odd, slots, cent, w0h, w0l, hots, veh, vel, evh, evl, path, columns),
        [vm((8, EDGES), F32), vm((LATENT, 256), F32), vm((LATENT, 256), F32)],
        scalar=True,
        us=22,
        limit=18,
    )

    chains = {}

    def grad(mine, cost, xh, xl, qh, ql):
        return order(
            functools.partial(grad_kernel, mine),
            [((WIDE, HALF), F32)],
            (place, xh, xl, qh, ql),
            scalar=True,
            us=cost,
        )[0]

    def send(name, *args):
        chains[name] = Sum(name, order, place, route, grad(False, COST[f"send_{name}"], *args), (0, 0, 0, 1))

    def keep(name, *args):
        chains[name].keep = grad(True, COST[f"keep_{name}"], *args)

    def late():
        return order(
            late_kernel,
            [
                ((LATENT, EDGES), BF16), ((LATENT, EDGES), BF16), ((8, EDGES), F32),
                ((8, LATENT), F32),
            ],
            (x1h, x1l, w1h, w1l, columns, geo),
            [vm((LATENT, 128), F32), vm((LATENT, 256), F32), vm((LATENT, 256), F32)],
            us=COST["late"],
            limit=17,
        )

    def mid():
        return order(
            mid_kernel,
            [((192, EDGES), F32), ((64, EDGES), BF16), ((64, EDGES), BF16), ((16, EDGES), F32)],
            (v.q1h, v.q1l, w1h, w1l, f1, g1, w1, geo),
            [vm((576, 128), F32)],
            us=COST["mid"],
        )

    def early():
        return order(
            early_kernel,
            [
                ((LATENT, EDGES), F32), ((LATENT, EDGES), BF16), ((LATENT, EDGES), BF16),
                ((8, EDGES), F32),
            ],
            (v.q1h, v.q1l, w1h, w1l, evh, evl, v.dw1h, v.dw1l, columns, geo, z0),
            [vm((LATENT, 256), F32), vm((LATENT, 256), F32)],
            us=COST["early"],
            limit=12,
        )

    def couple():
        return order(
            couple_kernel,
            [
                ((128, EDGES), BF16), ((128, EDGES), BF16), ((16, EDGES), F32),
                ((576, 128), F32),
            ],
            (v.q0h, v.q0l, w0h, w0l, vw, geo, g0, g1, v.ds1, path, v.dy1),
            [vm((192, EDGES), F32), vm((576, 128), F32), vm((16, EDGES), F32)],
            us=COST["couple"],
        )

    def before(h):
        return order(
            functools.partial(pre_kernel, h),
            [half, half, ((8, EDGES), F32), ((8, EDGES), F32)],
            (v.q0h, v.q0l, w0h, w0l, veh, vel, v.dvwh, v.dvwl, v.dlat, hots, cent, geo, rad_w),
            [vm((HALF, 256), F32), vm((HALF, 256), F32), vm((HALF, 256), F32)],
            us=COST[f"pre{h}"],
        )

    def run_late():
        v.q1h, v.q1l, v.sl, v.dout = late()

    def run_mid():
        v.ds1, v.dw1h, v.dw1l, v.dy1 = mid()

    def run_early():
        v.dlat, v.q0h, v.q0l, v.se = early()

    def run_couple():
        v.dvwh, v.dvwl, v.dy, v.dpath = couple()

    def run_weights():
        (v.more,) = order(
            weights_kernel,
            [((192, LATENT), F32)],
            (v.dvwh, v.dvwl, x0h, x0l, v.dw1h, v.dw1l, x1h, x1l),
            us=COST["weights"],
        )

    def run_last():
        atoms = ATOMS * math.prod(size for _, size in sizes)
        height = 144 + 8 * (atoms // LATENT)
        (ah, al, side_a, drad_a), (bh, bl, side_b, drad_b) = v.pres
        keep, send, v.energy = order(
            lambda place, *refs: last_kernel(
                sizes[1][1], sizes[2][1], place, refs[0:4], refs[4:6], refs[6:8], *refs[8:]
            ),
            [((192 + height, HALF), F32), ((192 + height, HALF), F32), ((8, 128), F32)],
            (place, ah, al, bh, bl, side_a, side_b, drad_a, drad_b, geo, slots, cent, v.sl, v.se,
             v.dy, v.dpath, columns, v.dout, v.more),
            [vm((8, NTAB), F32), vm((height, LATENT), F32), vm((8, atoms), F32)],
            scalar=True,
            us=COST["last"],
            name="last_kernel",
        )
        chains["s"] = Sum("s", order, place, route, send, (1, 1))
        chains["s"].keep = keep

    def finish(parts, arrays, mark=False):
        last = 1 + len(arrays)
        done = () if v.d_latent is None else (v.d_latent,)
        (v.d_latent,) = order(
            functools.partial(end_kernel, parts),
            [((2, WIDE, LATENT), F32)],
            (place, *arrays, *done),
            [sem.DMA((len(parts),))],
            scalar=True,
            hbm=(last,) if done else (),
            plain="hbm",
            alias={last: 0} if done else None,
            us=3,
            mark=mark,
        )

    def finish_small():
        s = chains["s"]
        v.small = order(
            functools.partial(small_end_kernel, 3),
            [
                ((NSPEC, LATENT), F32), ((NSPEC, LATENT), F32), ((NBESSEL, LATENT), F32),
                ((CHANNELS, LATENT), F32), ((2, CHANNELS, LATENT), F32), ((9, CHANNELS), F32),
                ((8, 128), F32), ((1, NSPEC), F32), ((1, NSPEC), F32), ((3, ATOMS), F32),
                ((1, ATOMS), F32),
            ],
            (place, s.send, s.got, v.energy),
            scalar=True,
            plain=True,
            us=2,
        )

    def land(name):
        chain = chains[name]
        if chain.over:
            return
        if name == "c" and chain.rising and chain.at == 1 and v.d_latent is not None:
            order.extra = (order.token,)
        if name == "s" and chain.rising and chain.at == 1 and v.own_done:
            order.extra = (order.token,)
        chain.land()

    def settle(name):
        while not chains[name].over:
            land(name)

    def finish_a():
        settle("a")
        finish(((1, 0, True), (1, 0, False)), (chains["a"].send, chains["a"].got), mark=True)

    def finish_s():
        settle("s")
        finish_small()

    def finish_c():
        settle("c")
        finish(((0, 0, True),), (chains["c"].send,), mark=True)
        v.own_done = True

    def set_free():
        order.free = True

    def set_bound():
        order.free = False

    v = types.SimpleNamespace(d_latent=None, pres=[], own_done=False)
    steps = {
        "late": run_late,
        "mid": run_mid,
        "early": run_early,
        "couple": run_couple,
        "weights": run_weights,
        "pre0": lambda: v.pres.append(before(0)),
        "pre1": lambda: v.pres.append(before(1)),
        "last": run_last,
        "send_a": lambda: send("a", x1h, x1l, v.q1h, v.q1l),
        "keep_a": lambda: keep("a", x1h, x1l, v.q1h, v.q1l),
        "send_c": lambda: send("c", x0h, x0l, v.q0h, v.q0l),
        "keep_c": lambda: keep("c", x0h, x0l, v.q0h, v.q0l),
        "a": lambda: land("a"),
        "c": lambda: land("c"),
        "s": lambda: land("s"),
        "free": set_free,
        "bind": set_bound,
        "end_a": finish_a,
        "end_s": finish_s,
        "end_c": finish_c,
    }
    for step in PROGRAM:
        steps[step]()
    finish(((0, 0, False),), (chains["c"].got,))
    (center, neigh, radial, value, env, path_grad, out, scale, shift, position_grad,
     energies) = v.small
    d_latent = v.d_latent
    return (
        energies.reshape(ATOMS),
        position_grad,
        center,
        neigh,
        radial,
        value.T,
        jnp.swapaxes(env, 1, 2),
        d_latent,
        path_grad,
        out.reshape(LATENT),
        scale.reshape(NSPEC),
        shift.reshape(NSPEC),
    )


def solution(mesh):
    everything = ("gx", "gy", "gz")
    return jax.shard_map(
        per_device,
        mesh=mesh,
        in_specs=(
            P(None, everything),
            P(everything),
            P(None, everything),
            P(),
            P(),
            P(),
            P(),
            P(),
            P(),
            P(),
            P(),
            P(),
            P(),
            P(everything),
        ),
        out_specs=(
            P(everything),
            P(None, everything),
            P(),
            P(),
            P(),
            P(),
            P(),
            P(),
            P(),
            P(),
            P(),
            P(),
        ),
        check_vma=False,
    )
```
